32 devices in a mesh: dp: 8 (over z, x), expert: 4 (over y, core).
Axes of the slice: x: 2, y: 2, z: 4, core: 2. Of those that a mesh axis runs over, the one named last changes fastest.
Arguments:
- tokens: bfloat16 [25216, 768], P(('dp', 'expert')), may hold values from -6 to 6
- cotangent: bfloat16 [25216, 768], P(('dp', 'expert')), may hold values from -6 to 6
- bank_ids: int32 [128], P(('dp', 'expert')), may hold values from 0 to 7
- routes: int32 [25216, 2], P(('dp', 'expert')), may hold values from 0 to 7, all different within a row; in each aligned block of 788 rows (0 to 787, 788 to 1575, ...) at most 320 rows name the same one
- attn_gain: float32 [768], replicated, may hold values from 0.25 to 1.75
- expert_gain: float32 [768], replicated, may hold values from 0.25 to 1.75
- query_w: bfloat16 [768, 768], replicated, may hold values from -0.21875 to 0.21875
- key_w: bfloat16 [768, 768], replicated, may hold values from -0.21875 to 0.21875
- value_w: bfloat16 [768, 768], replicated, may hold values from -0.21875 to 0.21875
- out_w: bfloat16 [768, 768], replicated, may hold values from -0.875 to 0.875
- query_a: bfloat16 [768, 128], replicated, may hold values from -0.21875 to 0.21875
- query_b: bfloat16 [128, 768], replicated, may hold values from -1.5 to 1.5
- key_a: bfloat16 [768, 128], replicated, may hold values from -0.21875 to 0.21875
- key_b: bfloat16 [128, 768], replicated, may hold values from -1.5 to 1.5
- value_a: bfloat16 [768, 128], replicated, may hold values from -0.21875 to 0.21875
- value_b: bfloat16 [128, 768], replicated, may hold values from -1.5 to 1.5
- out_a: bfloat16 [768, 128], replicated, may hold values from -0.875 to 0.875
- out_b: bfloat16 [128, 768], replicated, may hold values from -1.5 to 1.5
- router_w: bfloat16 [768, 8], replicated, may hold values from -0.099609375 to 0.099609375
- router_a: bfloat16 [768, 128], replicated, may hold values from -0.21875 to 0.21875
- router_b: bfloat16 [128, 8], replicated, may hold values from -0.75 to 0.75
- up_w: bfloat16 [8, 768, 3072], P('expert'), may hold values from -0.21875 to 0.21875
- up_a: bfloat16 [8, 768, 128], P('expert'), may hold values from -0.21875 to 0.21875
- up_b: bfloat16 [8, 128, 3072], P('expert'), may hold values from -1.5 to 1.5
- down_w: bfloat16 [8, 3072, 768], P('expert'), may hold values from -0.4375 to 0.4375
- down_a: bfloat16 [8, 3072, 128], P('expert'), may hold values from -0.4375 to 0.4375
- down_b: bfloat16 [8, 128, 768], P('expert'), may hold values from -1.5 to 1.5
Outputs:
- mixed: bfloat16 [25216, 768], P(('dp', 'expert'))
- input_grad: float32 [25216, 768], P(('dp', 'expert'))
- query_a_grad: float32 [768, 128], replicated
- query_b_grad: float32 [128, 768], replicated
- key_a_grad: float32 [768, 128], replicated
- key_b_grad: float32 [128, 768], replicated
- value_a_grad: float32 [768, 128], replicated
- value_b_grad: float32 [128, 768], replicated
- out_a_grad: float32 [768, 128], replicated
- out_b_grad: float32 [128, 768], replicated
- router_a_grad: float32 [768, 128], replicated
- router_b_grad: float32 [128, 8], replicated
- up_a_grad: float32 [8, 768, 128], P('expert')
- up_b_grad: float32 [8, 128, 3072], P('expert')
- down_a_grad: float32 [8, 3072, 128], P('expert')
- down_b_grad: float32 [8, 128, 768], P('expert')
The draws below stay inside these ranges and needn't reach their ends.
Inputs may be any that keep to these rules, and one draw needn't show every extreme that they name: `routes`: the two experts of a row differ and every expert is named by some row. In the 788 rows of one device no expert is named by more than 320 rows, and in some device's rows one expert is named by exactly 320.
All inputs are finite; a program needn't handle non-finite values.
Results may differ from the reference program's by a relative error of at most 0.018.
The reference program's roundings to bfloat16 on the way count: a program that leaves them out, or rounds other values in their place, can miss the bound.
Values may be sent and summed in bfloat16 or wider, within the bound.
No kernel may reach another device: no remote copies, remote signals or barrier semaphores. Data moves between devices by JAX's collectives and lax.ppermute only.
A program may use at most 256 MiB of HBM per device.

```python
import math
import jax
import jax.numpy as jnp
import numpy as np
from jax import lax

D = 768
HEADS = 12
HEAD_DIM = 64
FF = 3072
RANK = 16
BANKS = 8
SEQ = 197
TOK_DEV = 788
EXPERTS = 8
CAP = 320
IMAGES = 128
TOKENS = 25216
N_DP = 8
N_EXPERT = 4


def touch_ends(result, key, smallest, high):
    shape = result.shape
    spot = [jax.random.randint(jax.random.fold_in(key, axis), (), 0, shape[axis]) for axis in range(len(shape))]
    result = result.at[tuple(spot)].set(smallest)
    longest = shape.index(max(shape))
    spot[longest] = (spot[longest] + 1) % shape[longest]
    return result.at[tuple(spot)].set(high)


def block_levels(own_key, extent, cuts, smallest, largest):
    def one(dim, blocks):
        draws = jax.random.uniform(jax.random.fold_in(jax.random.fold_in(own_key, 6), dim), (blocks,), jnp.float32, smallest / len(cuts), largest / len(cuts))
        return jnp.repeat(jnp.exp(draws), extent[dim] // blocks).reshape((-1,) + (1,) * (len(extent) - dim - 1))

    loudness = one(*cuts[0])
    for cut in cuts[1:]:
        loudness = loudness * one(*cut)
    return loudness


def shared_out(stream_key, own, number, rows, count, top, reach, lean):
    ranking = jax.random.permutation(stream_key, count)
    heavy_load, usual = portions_of(count, rows * top, reach, lean, True), portions_of(count, rows * top, reach, lean, False)
    places = jnp.arange(count)

    def named(sizes, rotation):
        used = int((sizes > 0).sum())
        fixed = max(1, used // 4)
        moved = fixed + (places - fixed + rotation * (used - fixed)) % max(1, count - fixed)
        return jnp.zeros((count,), jnp.int32).at[ranking[jnp.where(places < fixed, places, moved)]].set(jnp.asarray(sizes, jnp.int32))

    sizes = jnp.where(number % 4 == 0, named(heavy_load, number // 4), named(usual, number - number // 4 - 1))
    mixed = jax.random.permutation(jax.random.fold_in(own, 3), count)
    source_of, receiver = mixed[0:count // 2 * 2:2], mixed[1:count // 2 * 2:2]
    margin = jnp.minimum(sizes[source_of] - 1, reach - sizes[receiver]) // 2
    margin = jnp.where((source_of == ranking[0]) | (receiver == ranking[0]) | (sizes[receiver] == 0), 0, jnp.maximum(margin, 0))
    moved = jax.random.randint(jax.random.fold_in(own, 4), (count // 2,), 0, 1 << 20) % (margin + 1)
    sizes = sizes.at[source_of].add(-moved).at[receiver].add(moved)
    items = jnp.searchsorted(jnp.cumsum(sizes), jnp.arange(rows * top), side="right").astype(jnp.int32)
    listing = items.reshape(top, rows).T
    listing = listing[jax.random.permutation(jax.random.fold_in(own, 1), rows)]
    rotation = jax.random.randint(jax.random.fold_in(own, 2), (rows, 1), 0, top)
    return jnp.take_along_axis(listing, (jnp.arange(top)[None, :] + rotation) % top, axis=1)


def portions_of(amount, total, reach, slope, full):
    loads = [(1 << 20) // math.isqrt(standing ** slope) + 1 for standing in range(1, amount + 1)]
    largest = reach if full else min(reach, max(-(-total // amount), total * loads[0] // sum(loads)))
    least = 1 if total - largest >= amount - 1 else 0
    given, surplus = [largest] + [least] * (amount - 1), total - largest - least * (amount - 1)
    while surplus > 0:
        movable = [i for i in range(1, amount) if given[i] < largest] or [i for i in range(1, amount) if given[i] < reach]
        pool, budget = sum([loads[i] for i in movable]), surplus
        for i in movable:
            more = min(reach - given[i], max(1, budget * loads[i] // pool), surplus)
            given[i] = given[i] + more
            surplus = surplus - more
    return np.array(given)


def scatter_about(key, extent, scale, most, cuts=(), kind=jnp.bfloat16):
    values = scale * jax.random.normal(key, extent, jnp.float32)
    if cuts:
        values = values * block_levels(key, extent, cuts, -0.22, 0.18)
    return jnp.clip(values, -most, most).astype(kind)


def setup_inputs(seed: int = 0) -> dict:
    key_of = jax.random.split(jax.random.key(seed), 28)
    tokens = scatter_about(key_of[0], (TOKENS, D), 1.0, 6.0, ((0, 32),))
    cotangent = scatter_about(key_of[1], (TOKENS, D), 1.0, 6.0, ((0, 32),))
    bank_ids = touch_ends(jax.random.randint(key_of[2], (IMAGES,), 0, BANKS), jax.random.fold_in(key_of[2], 1), 0, BANKS - 1).astype(jnp.int32)
    routes_keys = jax.random.split(jax.random.fold_in(key_of[3], 1), TOKENS // TOK_DEV)
    routes_turns = jax.random.permutation(jax.random.fold_in(key_of[3], 3), TOKENS // TOK_DEV)
    routes = jax.vmap(lambda own, number: shared_out(jax.random.fold_in(key_of[3], 2), own, number, TOK_DEV, EXPERTS, 2, CAP, 1))(routes_keys, routes_turns).reshape((TOKENS, 2))
    attn_gain = jnp.clip(1.0 + 0.15 * jax.random.normal(key_of[4], (D,), jnp.float32), 0.25, 1.75)
    expert_gain = jnp.clip(1.0 + 0.15 * jax.random.normal(key_of[5], (D,), jnp.float32), 0.25, 1.75)
    query_w = scatter_about(key_of[6], (D, D), D ** -0.5, 0.21875)
    key_w = scatter_about(key_of[7], (D, D), D ** -0.5, 0.21875)
    value_w = scatter_about(key_of[8], (D, D), D ** -0.5, 0.21875)
    out_w = scatter_about(key_of[9], (D, D), (D // 16) ** -0.5, 0.875)
    query_a = scatter_about(key_of[10], (D, BANKS * RANK), D ** -0.5, 0.21875)
    query_b = scatter_about(key_of[11], (BANKS * RANK, D), RANK ** -0.5, 1.5)
    key_a = scatter_about(key_of[12], (D, BANKS * RANK), D ** -0.5, 0.21875)
    key_b = scatter_about(key_of[13], (BANKS * RANK, D), RANK ** -0.5, 1.5)
    value_a = scatter_about(key_of[14], (D, BANKS * RANK), D ** -0.5, 0.21875)
    value_b = scatter_about(key_of[15], (BANKS * RANK, D), RANK ** -0.5, 1.5)
    out_a = scatter_about(key_of[16], (D, BANKS * RANK), (D // 16) ** -0.5, 0.875)
    out_b = scatter_about(key_of[17], (BANKS * RANK, D), RANK ** -0.5, 1.5)
    router_w = scatter_about(key_of[18], (D, EXPERTS), 0.018, 0.099609375)
    router_a = scatter_about(key_of[19], (D, BANKS * RANK), D ** -0.5, 0.21875)
    router_b = scatter_about(key_of[20], (BANKS * RANK, EXPERTS), 0.125, 0.75)
    up_w = scatter_about(key_of[21], (EXPERTS, D, FF), D ** -0.5, 0.21875, ((0, 4),))
    up_a = scatter_about(key_of[22], (EXPERTS, D, BANKS * RANK), D ** -0.5, 0.21875, ((0, 4),))
    up_b = scatter_about(key_of[23], (EXPERTS, BANKS * RANK, FF), RANK ** -0.5, 1.5, ((0, 4),))
    down_w = scatter_about(key_of[24], (EXPERTS, FF, D), (FF // 16) ** -0.5, 0.4375, ((0, 4),))
    down_a = scatter_about(key_of[25], (EXPERTS, FF, BANKS * RANK), (FF // 16) ** -0.5, 0.4375, ((0, 4),))
    down_b = scatter_about(key_of[26], (EXPERTS, BANKS * RANK, D), RANK ** -0.5, 1.5, ((0, 4),))
    return {"tokens": tokens, "cotangent": cotangent, "bank_ids": bank_ids, "routes": routes, "attn_gain": attn_gain, "expert_gain": expert_gain, "query_w": query_w, "key_w": key_w, "value_w": value_w, "out_w": out_w, "query_a": query_a, "query_b": query_b, "key_a": key_a, "key_b": key_b, "value_a": value_a, "value_b": value_b, "out_a": out_a, "out_b": out_b, "router_w": router_w, "router_a": router_a, "router_b": router_b, "up_w": up_w, "up_a": up_a, "up_b": up_b, "down_w": down_w, "down_a": down_a, "down_b": down_b}


@jax.custom_vjp
def low(v):
    return lax.optimization_barrier(v.astype(jnp.bfloat16)).astype(jnp.float32)

@jax.custom_vjp
def low_back(v):
    return v

def low_keep(v):
    return (low(v), None)

def low_pass(kept, grad):
    return (grad,)

def back_keep(v):
    return (v, None)

def back_low(kept, grad):
    return (low(grad),)
low.defvjp(low_keep, low_pass)
low_back.defvjp(back_keep, back_low)
EPSILON = 1e-06
HIGHEST = lax.Precision.HIGHEST

def product(first_op, second_op):
    return jnp.dot(first_op, second_op, precision=HIGHEST)

def layer_norm(values, norm_gain):
    average = lax.optimization_barrier(jnp.mean(values, axis=-1, keepdims=True))
    centred = values - average
    spread = lax.optimization_barrier(jnp.mean(centred * centred, axis=-1, keepdims=True))
    return norm_gain * centred * lax.rsqrt(spread + EPSILON)

def bank_columns(row_banks, columns):
    column_bank = jnp.arange(columns, dtype=jnp.int32) // RANK
    return (column_bank[None, :] == row_banks[:, None]).astype(jnp.float32)

def adapted(row_block, weight, down_proj, up_proj, bank_cols):
    low_rank = low(low_back(product(row_block, down_proj) * bank_cols))
    return product(row_block, weight) + product(low_rank, up_proj)

def attend_block(parts):
    queries, keys_rows, values_rows = parts
    query_h = queries.reshape(-1, SEQ, HEADS, HEAD_DIM)
    key_h = keys_rows.reshape(-1, SEQ, HEADS, HEAD_DIM)
    value_h = values_rows.reshape(-1, SEQ, HEADS, HEAD_DIM)
    scores = low_back(jnp.einsum('bqhd,bkhd->bhqk', query_h, key_h, precision=HIGHEST) * HEAD_DIM ** (-0.5))
    weights = low(jax.nn.softmax(scores, axis=-1))
    attended = jnp.einsum('bhqk,bkhd->bqhd', weights, value_h, precision=HIGHEST)
    return attended.reshape(queries.shape[0], HEADS * HEAD_DIM)

def expert_block(parts):
    routed_rows, bank_cols, up_weight, up_first, up_second, down_weight, down_first, down_second = parts
    pre_act = low_back(adapted(routed_rows, up_weight, up_first, up_second, bank_cols))
    hidden = low(jax.nn.gelu(pre_act, approximate=False))
    return low(low_back(adapted(hidden, down_weight, down_first, down_second, bank_cols)))

def slot_tables(route_ids, devices):
    count = 2 * TOK_DEV
    flat_routes = route_ids.reshape(devices, count)
    expert_ids = jnp.arange(EXPERTS, dtype=jnp.int32)
    onehot = (flat_routes[:, :, None] == expert_ids[None, None, :]).astype(jnp.int32)
    before = (jnp.cumsum(onehot, axis=1) - onehot).astype(jnp.int32)
    position = lax.optimization_barrier(jnp.sum(before * onehot, axis=2)).astype(jnp.int32)
    device_ids = jnp.arange(devices, dtype=jnp.int32)[:, None]
    slot_index = ((flat_routes * devices + device_ids) * CAP + position).astype(jnp.int32)
    token_index = (device_ids * TOK_DEV + jnp.arange(count, dtype=jnp.int32)[None, :] // 2).astype(jnp.int32)
    source_index = jnp.full((EXPERTS * devices * CAP,), TOKENS, jnp.int32)
    source_index = source_index.at[slot_index.reshape(-1)].set(token_index.reshape(-1))
    return (slot_index.reshape(TOKENS, 2), source_index)

def reference(tokens, cotangent, bank_ids, routes, attn_gain, expert_gain, query_w, key_w, value_w, out_w, query_a, query_b, key_a, key_b, value_a, value_b, out_a, out_b, router_w, router_a, router_b, up_w, up_a, up_b, down_w, down_a, down_b):
    devices = N_DP * N_EXPERT
    adapter_width = BANKS * RANK
    route_ids = routes.astype(jnp.int32)
    token_banks = jnp.repeat(bank_ids.astype(jnp.int32), SEQ)
    token_cols = bank_columns(token_banks, adapter_width)
    slot_index, source_index = slot_tables(route_ids, devices)
    padded_banks = jnp.concatenate([token_banks, jnp.zeros((1,), jnp.int32)])
    slot_cols = bank_columns(padded_banks[source_index], adapter_width).reshape(EXPERTS, -1, adapter_width)
    image_group = math.gcd(IMAGES, 16)
    blocks = IMAGES // image_group
    attn_gain_f = attn_gain.astype(jnp.float32)
    expert_gain_f = expert_gain.astype(jnp.float32)
    query_wf = query_w.astype(jnp.float32)
    key_wf = key_w.astype(jnp.float32)
    value_wf = value_w.astype(jnp.float32)
    out_wf = out_w.astype(jnp.float32)
    router_wf = router_w.astype(jnp.float32)
    up_wf = up_w.astype(jnp.float32)
    down_wf = down_w.astype(jnp.float32)

    def forward(tokens_wide, q_first, q_second, k_first, k_second, v_first, v_second, o_first, o_second, r_first, r_second, u_first, u_second, d_first, d_second):
        normed_one = low(layer_norm(tokens_wide, attn_gain_f))
        queries = low(low_back(adapted(normed_one, query_wf, q_first, q_second, token_cols)))
        keys_rows = low(low_back(adapted(normed_one, key_wf, k_first, k_second, token_cols)))
        values_rows = low(low_back(adapted(normed_one, value_wf, v_first, v_second, token_cols)))
        stacked = lax.map(jax.checkpoint(attend_block), (queries.reshape(blocks, -1, D), keys_rows.reshape(blocks, -1, D), values_rows.reshape(blocks, -1, D)))
        attended = low(low_back(stacked.reshape(TOKENS, D)))
        mid_sum = tokens_wide + low_back(adapted(attended, out_wf, o_first, o_second, token_cols))
        normed_two = low(layer_norm(mid_sum, expert_gain_f))
        logits = low_back(adapted(normed_two, router_wf, r_first, r_second, token_cols))
        router_probs = jax.nn.softmax(logits, axis=-1)
        gate_values = jnp.take_along_axis(router_probs, route_ids, axis=1)
        padded_rows = jnp.concatenate([normed_two, jnp.zeros((1, D), jnp.float32)], axis=0)
        routed_rows = low_back(padded_rows[source_index]).reshape(EXPERTS, -1, D)
        expert_out = lax.map(jax.checkpoint(expert_block), (routed_rows, slot_cols, up_wf, u_first, u_second, down_wf, d_first, d_second))
        returned = expert_out.reshape(-1, D)[slot_index.reshape(-1)].reshape(TOKENS, 2, D)
        return mid_sum + lax.optimization_barrier(jnp.sum(gate_values[:, :, None] * returned, axis=1))
    mixed_out, pullback = jax.vjp(forward, tokens.astype(jnp.float32), query_a.astype(jnp.float32), query_b.astype(jnp.float32), key_a.astype(jnp.float32), key_b.astype(jnp.float32), value_a.astype(jnp.float32), value_b.astype(jnp.float32), out_a.astype(jnp.float32), out_b.astype(jnp.float32), router_a.astype(jnp.float32), router_b.astype(jnp.float32), up_a.astype(jnp.float32), up_b.astype(jnp.float32), down_a.astype(jnp.float32), down_b.astype(jnp.float32))
    gradients = pullback(cotangent.astype(jnp.float32))
    return (mixed_out.astype(jnp.bfloat16), gradients[0], gradients[1], gradients[2], gradients[3], gradients[4], gradients[5], gradients[6], gradients[7], gradients[8], gradients[9], gradients[10], gradients[11], gradients[12], gradients[13], gradients[14])
```

```python
import functools
import math

import jax
import jax.numpy as jnp
from jax import lax
from jax.experimental import pallas as pl
from jax.experimental.pallas import tpu as pltpu
from jax.sharding import PartitionSpec as P

HEAD_DIM = 64
RANK = 16
SEQ = 197
EPS = 1e-06
BF = jnp.bfloat16
F32 = jnp.float32
I32 = jnp.int32
LOG2E = math.log2(math.e)
SCALE2 = HEAD_DIM ** (-0.5) * LOG2E
NEG = -1e30
TILE = 256
CHUNK = 768
VMEM = pl.BlockSpec(memory_space=pltpu.VMEM)
SMEM = pl.BlockSpec(memory_space=pltpu.SMEM)


def up16(n):
    return -(-n // 16) * 16


def nn(a, b):
    return jnp.dot(a, b, preferred_element_type=F32)


def nt(a, b):
    return lax.dot_general(a, b, (((1,), (1,)), ((), ())), preferred_element_type=F32)


def tn(a, b):
    return lax.dot_general(a, b, (((0,), (0,)), ((), ())), preferred_element_type=F32)


def params(mib):
    return pltpu.CompilerParams(vmem_limit_bytes=mib * 1024 * 1024)


def image_banks(banks, row, images):
    bank = jnp.full(row.shape, banks[0], I32)
    for i in range(1, images):
        bank = jnp.where(row >= SEQ * i, banks[i], bank)
    return bank


def bank_mask(banks, start, count, images, width):
    row = lax.broadcasted_iota(I32, (count, width), 0) + start
    col = lax.broadcasted_iota(I32, (count, width), 1)
    return (col // RANK == image_banks(banks, row, images)).astype(F32)


def norm_parts(x):
    mean = jnp.mean(x, axis=-1, keepdims=True)
    cen = x - mean
    rstd = lax.rsqrt(jnp.mean(cen * cen, axis=-1, keepdims=True) + EPS)
    return cen * rstd, rstd


def norm_back(xhat, rstd, gain, grad):
    gy = grad * gain
    return rstd * (
        gy
        - jnp.mean(gy, axis=-1, keepdims=True)
        - xhat * jnp.mean(gy * xhat, axis=-1, keepdims=True)
    )


def attn_fwd_kernel(
    banks, tok, g1, g2, wq, wk, wv, wo, aq, bq, ak, bk, av, bv, ao, bo, rwt, ra, rbt,
    n1_o, q_o, k_o, v_o, lq_o, lk_o, lv_o, att_o, lo_o, mid_o, n2_o, lr_o, pt_o, lse_o,
    tokp, lset,
):
    rows = tok.shape[0]
    rp = n1_o.shape[0]
    images = rows // SEQ
    d = tok.shape[1]
    width = aq.shape[1]
    win = lse_o.shape[2]
    step_rows = 16 * (SEQ // 16)
    tokp[pl.ds(rp - 16, 16), :] = jnp.zeros((16, d), BF)
    tokp[0:rows, :] = tok[...]

    def ln1(i, _):
        r = pl.multiple_of(i * 32, 32)
        xhat, _r = norm_parts(tokp[pl.ds(r, 32), :].astype(F32))
        n1_o[pl.ds(r, 32), :] = (g1[...] * xhat).astype(BF)
        return 0

    lax.fori_loop(0, rp // 32, ln1, 0)
    half = rp // 2

    def qkv(i, _):
        r = pl.multiple_of(i * half, 16)
        x = n1_o[pl.ds(r, half), :]
        mask = bank_mask(banks, r, half, images, width)
        for w, a, b, out, low in (
            (wq, aq, bq, q_o, lq_o),
            (wk, ak, bk, k_o, lk_o),
            (wv, av, bv, v_o, lv_o),
        ):
            u = (nn(x, a[...]) * mask).astype(BF)
            low[pl.ds(r, half), :] = u
            out[pl.ds(r, half), :] = (nn(x, w[...]) + nn(u, b[...])).astype(BF)
        return 0

    lax.fori_loop(0, 2, qkv, 0)

    lane = lax.broadcasted_iota(I32, (win, 128), 1)
    first = lane < HEAD_DIM
    row_i = lax.broadcasted_iota(I32, (win, 128), 0)
    keys_i = lax.broadcasted_iota(I32, (win, win), 1)

    def image(i, _):
        off = pl.multiple_of(i * step_rows, 64)
        lo = i * (SEQ - step_rows)
        bias = jnp.where((keys_i >= lo) & (keys_i < lo + SEQ), 0.0, NEG)
        keep = row_i < lo
        lset[...] = jnp.zeros_like(lset)
        lse_tile = jnp.zeros((win, 128), F32)
        for p in range(d // 128):
            cols = slice(p * 128, p * 128 + 128)
            qp = q_o[pl.ds(off, win), cols]
            kp = k_o[pl.ds(off, win), cols]
            vp = v_o[pl.ds(off, win), cols]
            outs = []
            for h in range(2):
                mine = first if h == 0 else jnp.logical_not(first)
                qm = jnp.where(mine, qp, jnp.zeros_like(qp))
                s = nt(qm, kp) * SCALE2 + bias
                top = jnp.max(s, axis=-1, keepdims=True)
                e = jnp.exp2(s - top)
                den = jnp.sum(e, axis=-1, keepdims=True)
                w = (e * pl.reciprocal(den)).astype(BF)
                outs.append(nn(w, vp))
                lse = top + jnp.log2(den)
                lse_tile = jnp.where(lane == 2 * p + h, lse, lse_tile)
            new = jnp.where(first, outs[0], outs[1]).astype(BF)
            att_o[pl.ds(off, win), cols] = jnp.where(keep, att_o[pl.ds(off, win), cols], new)
        lset[0:win, :] = lse_tile
        lse_o[i] = jnp.transpose(lset[...])[0 : lse_o.shape[1], 0:win]
        return 0

    lax.fori_loop(0, images, image, 0)

    def out_proj(i, _):
        r = pl.multiple_of(i * half, 16)
        x = att_o[pl.ds(r, half), :]
        mask = bank_mask(banks, r, half, images, width)
        u = (nn(x, ao[...]) * mask).astype(BF)
        lo_o[pl.ds(r, half), :] = u
        mid_o[pl.ds(r, half), :] = (
            tokp[pl.ds(r, half), :].astype(F32) + nn(x, wo[...]) + nn(u, bo[...])
        )
        return 0

    lax.fori_loop(0, 2, out_proj, 0)

    def ln2(i, _):
        r = pl.multiple_of(i * 32, 32)
        xhat, _r = norm_parts(mid_o[pl.ds(r, 32), :])
        n2_o[pl.ds(r, 32), :] = (g2[...] * xhat).astype(BF)
        return 0

    lax.fori_loop(0, rp // 32, ln2, 0)
    x = n2_o[...]
    u = (nn(x, ra[...]) * bank_mask(banks, 0, rp, images, width)).astype(BF)
    lr_o[...] = u
    logits = nt(rwt[...], x) + nt(rbt[...], u)
    e = jnp.exp(logits - jnp.max(logits, axis=0, keepdims=True))
    pt_o[...] = e / jnp.sum(e, axis=0, keepdims=True)


def attn_forward(banks, tok, g1, g2, ws):
    rows, d = tok.shape
    rp = 32 * (-(-rows // 32))
    images = rows // SEQ
    step_rows = 16 * (SEQ // 16)
    win = rp - step_rows * (images - 1)
    width = ws[4].shape[1]
    experts = ws[12].shape[0]
    heads_pad = 16 * (-(-d // (16 * HEAD_DIM)))
    bfd = jax.ShapeDtypeStruct((rp, d), BF)
    low = jax.ShapeDtypeStruct((rp, width), BF)
    out_shape = (
        bfd, bfd, bfd, bfd, low, low, low, bfd, low,
        jax.ShapeDtypeStruct((rp, d), F32), bfd, low,
        jax.ShapeDtypeStruct((experts, rp), F32),
        jax.ShapeDtypeStruct((images, heads_pad, win), F32),
    )
    return pl.pallas_call(
        attn_fwd_kernel,
        out_shape=out_shape,
        in_specs=[SMEM] + [VMEM] * 18,
        out_specs=tuple([VMEM] * len(out_shape)),
        scratch_shapes=[pltpu.VMEM((rp, d), BF), pltpu.VMEM((256, 128), F32)],
        compiler_params=params(56),
        name="attn_fwd",
    )(banks, tok, g1, g2, *ws)


def tables_kernel(eidx, routes, posr_o, posc_o):
    groups, _, rp = routes.shape
    local = posr_o.shape[0] // groups
    row = lax.broadcasted_iota(I32, (rp, rp), 0)
    col = lax.broadcasted_iota(I32, (rp, rp), 1)
    upper = (row < col).astype(BF)
    upper_inc = (row <= col).astype(BF)
    lower = (col < row).astype(BF)
    lower_inc = (col <= row).astype(BF)
    which = lax.broadcasted_iota(I32, (groups * local, rp), 0)
    hot = jnp.zeros((groups * local, rp), F32)
    for s in range(groups):
        r0 = routes[s, 0:1, :]
        r1 = routes[s, 1:2, :]
        for j in range(local):
            e = eidx[0] * local + j
            hit = ((r0 == e) | (r1 == e)).astype(F32)
            hot = jnp.where(which == s * local + j, hit, hot)
    hb = hot.astype(BF)
    before = nn(hb, upper)
    with_own = nn(hb, upper_inc)
    posr_o[...] = jnp.where(with_own > before, before, -1.0)
    before = nt(lower, hb)
    with_own = nt(lower_inc, hb)
    posc_o[...] = jnp.where(with_own > before, before, -1.0)


def routing_tables(eidx, routes, local):
    groups, _, rp = routes.shape
    n = groups * local
    return pl.pallas_call(
        tables_kernel,
        out_shape=(jax.ShapeDtypeStruct((n, rp), F32), jax.ShapeDtypeStruct((rp, n), F32)),
        in_specs=[SMEM, VMEM],
        out_specs=(VMEM, VMEM),
        compiler_params=params(32),
        name="routing_tables",
    )(eidx, routes)


def gelu_parts(x):
    e = jnp.exp2((-0.5 * LOG2E) * (x * x))
    t = pl.reciprocal(1.0 + (0.3275911 / math.sqrt(2.0)) * jnp.abs(x))
    poly = 1.061405429 * 0.5
    for c in (-1.453152027, 1.421413741, -0.284496736, 0.254829592):
        poly = poly * t + 0.5 * c
    q = poly * t * e
    phi = jnp.where(x >= 0.0, 1.0 - q, q)
    return x * phi, phi + x * (e * (1.0 / math.sqrt(2.0 * math.pi)))


def expert_kernel(cfg, *refs):
    j, sources, combine, has_acc, cap, local, images = cfg
    refs = list(refs)
    take = lambda n: [refs.pop(0) for _ in range(n)]
    eidx, banks = take(2)
    posr, posc = take(2)
    gates = take(len(sources))
    nrows = take(len(sources))
    crows = take(len(sources))
    upw, upa, upb, dnw, dna, dnb = take(6)
    if combine:
        ret_in, grow_in, gg_in = take(3)
    if has_acc:
        acc_in = take(4)
    acc_out = take(4)
    if combine:
        grow_out = take(len(sources))
        mix_out = take(len(sources))
        gg_out = take(len(sources))
        xbuf, cbuf, gate_b, mask_b, gg_b, hid, dgl, stage, ret_b, grow_b = take(10)
    else:
        ret_b, grow_b, gg_rows = take(3)
        xbuf, cbuf, gate_b, mask_b, gg_b, hid, dgl = take(7)
    rp, d = nrows[0].shape
    ff = upw.shape[2]
    width = upa.shape[2]
    uaacc, ubacc, daacc, dbacc = acc_out
    if has_acc:
        for a, b in zip(acc_out, acc_in):
            a[...] = b[...]
    else:
        for a in acc_out:
            a[...] = jnp.zeros_like(a)
    slot_r = lax.broadcasted_iota(I32, (cap, rp), 0).astype(F32)
    slot_c = lax.broadcasted_iota(I32, (rp, cap), 1).astype(F32)
    token = lax.broadcasted_iota(I32, (1, rp), 1)
    experts = gates[0].shape[0]
    expert_row = lax.broadcasted_iota(I32, (experts, rp), 0)
    mine = expert_row == eidx[0] * local + j
    col_bank = (lax.broadcasted_iota(I32, (cap, width), 1) // RANK).astype(F32)

    def count_of(s, e):
        line = posr[s * local + e : s * local + e + 1, :]
        n = jnp.sum((line >= 0.0).astype(F32)).astype(I32)
        return ((n + 15) // 16) * 16

    offs = []
    off = jnp.int32(0)
    for i, s in enumerate(sources):
        off = pl.multiple_of(off, 16)
        offs.append(off)
        line = posr[s * local + j : s * local + j + 1, :]
        hit = line == slot_r
        gate_line = jnp.sum(jnp.where(mine, gates[i][...], 0.0), axis=0, keepdims=True)
        bank = jnp.full((1, rp), banks[s, 0], I32)
        for k in range(1, images):
            bank = jnp.where(token >= SEQ * k, banks[s, k], bank)
        gate = jnp.sum(jnp.where(hit, gate_line, 0.0), axis=1, keepdims=True)
        slot_bank = jnp.sum(jnp.where(hit, bank.astype(F32), 0.0), axis=1, keepdims=True)
        pick = hit.astype(F32).astype(BF)
        xbuf[pl.ds(off, cap), :] = nn(pick, nrows[i][...]).astype(BF)
        cbuf[pl.ds(off, cap), :] = nn(pick, crows[i][...]).astype(BF)
        gate_b[pl.ds(off, cap), :] = jnp.broadcast_to(gate, (cap, 128))
        mask_b[pl.ds(off, cap), :] = (col_bank == slot_bank).astype(F32)
        off = off + count_of(s, j)
    total = off
    last = pl.multiple_of(offs[-1] + cap, 16)
    xbuf[pl.ds(last, TILE), :] = jnp.zeros((TILE, d), BF)
    cbuf[pl.ds(last, TILE), :] = jnp.zeros((TILE, d), BF)
    gate_b[pl.ds(last, TILE), :] = jnp.zeros((TILE, 128), F32)
    mask_b[pl.ds(last, TILE), :] = jnp.zeros((TILE, width), F32)
    tiles = (total + TILE - 1) // TILE
    nc = ff // CHUNK

    def tile(t, _):
        rs = pl.ds(pl.multiple_of(t * TILE, TILE), TILE)
        x = xbuf[rs, :]
        m = mask_b[rs, :]
        u = (nn(x, upa[0]) * m).astype(BF)
        out = jnp.zeros((TILE, d), F32)
        ud = jnp.zeros((TILE, width), F32)
        for c in range(nc):
            cs = slice(c * CHUNK, (c + 1) * CHUNK)
            h, dg = gelu_parts(nn(x, upw[0, :, cs]) + nn(u, upb[0, :, cs]))
            hb = h.astype(BF)
            hid[:, cs] = hb
            dgl[:, cs] = dg
            ud = ud + nn(hb, dna[0, cs, :])
            out = out + nn(hb, dnw[0, cs, :])
        udl = (ud * m).astype(BF)
        ret = (out + nn(udl, dnb[0])).astype(BF).astype(F32)
        cot = cbuf[rs, :].astype(F32)
        gate = gate_b[rs, 0:1]
        gg_b[rs, :] = jnp.broadcast_to(jnp.sum(cot * ret, axis=1, keepdims=True), (TILE, 128))
        ret_b[rs, :] = (gate * ret).astype(BF)
        g = (gate * cot).astype(BF)
        gud = (nt(g, dnb[0]) * m).astype(BF)
        dbacc[...] += tn(udl, g)
        gul = jnp.zeros((TILE, width), F32)
        gr = jnp.zeros((TILE, d), F32)
        for c in range(nc):
            cs = slice(c * CHUNK, (c + 1) * CHUNK)
            gh = nt(g, dnw[0, cs, :]) + nt(gud, dna[0, cs, :])
            gp = (gh * dgl[:, cs]).astype(BF)
            gul = gul + nt(gp, upb[0, :, cs])
            gr = gr + nt(gp, upw[0, :, cs])
            ubacc[:, cs] += tn(u, gp)
            daacc[:, cs] += tn(gud, hid[:, cs])
        guu = (gul * m).astype(BF)
        uaacc[...] += tn(guu, x)
        grow_b[rs, :] = (gr + nt(guu, upa[0])).astype(BF)
        return 0

    lax.fori_loop(0, tiles, tile, 0)
    done = pl.multiple_of(tiles * TILE, 16)
    ret_b[pl.ds(done, cap), :] = jnp.zeros((cap, d), BF)
    grow_b[pl.ds(done, cap), :] = jnp.zeros((cap, d), BF)
    gg_b[pl.ds(done, cap), :] = jnp.zeros((cap, 128), F32)
    gg_lines = []
    for i, s in enumerate(sources):
        line = posr[s * local + j : s * local + j + 1, :]
        col = gg_b[pl.ds(offs[i], cap), 0:1]
        gg_lines.append(
            jnp.sum(jnp.where(line == slot_r, col, 0.0), axis=0, keepdims=True)
        )
    if not combine:
        for i, s in enumerate(sources):
            gg_rows[s : s + 1, :] = gg_lines[i]
        return
    base = jnp.int32(0)
    firsts = {}
    for s in range(len(banks_range(posr, local))):
        firsts[s] = pl.multiple_of(base, 16)
        base = base + count_of(s, 0)
    for i, s in enumerate(sources):
        p0 = (posc[:, s * local : s * local + 1] == slot_c).astype(F32).astype(BF)
        p1 = (posc[:, s * local + 1 : s * local + 2] == slot_c).astype(F32).astype(BF)
        for mine_b, other, result in (
            (grow_b, grow_in, grow_out[i]),
            (ret_b, ret_in, mix_out[i]),
        ):
            result[...] = (
                nn(p0, other[pl.ds(firsts[s], cap), :]) + nn(p1, mine_b[pl.ds(offs[i], cap), :])
            ).astype(BF)
        e0 = eidx[0] * local
        gg_out[i][...] = jnp.where(
            expert_row == e0,
            gg_in[s : s + 1, :],
            jnp.where(expert_row == e0 + 1, gg_lines[i], 0.0),
        )


def banks_range(posr, local):
    return range(posr.shape[0] // local)


def expert_call(j, sources, combine, eidx, banks, tables, gates, nrows, crows, ws, cap, first, acc):
    posr, posc = tables
    rp, d = nrows[0].shape
    images = banks.shape[1]
    upw, upa, upb, dnw, dna, dnb = ws
    local, _, ff = upw.shape
    width = upa.shape[2]
    experts = gates[0].shape[0]
    n = len(sources)
    cfg = (j, tuple(sources), combine, acc is not None, cap, local, images)
    buf_rows = n * cap + TILE + cap
    args = [eidx, banks, posr, posc]
    args += [gates[s] for s in sources] + [nrows[s] for s in sources] + [crows[s] for s in sources]
    in_specs = [SMEM, SMEM] + [VMEM] * (2 + 3 * n)
    args += list(ws)
    for w in ws:
        in_specs.append(pl.BlockSpec((1,) + w.shape[1:], lambda i: (j, 0, 0)))
    whole = lambda shape: pl.BlockSpec(shape, lambda i: (0,) * len(shape))
    in_specs = [
        s if s.memory_space == pltpu.SMEM or s.block_shape is not None else s for s in in_specs
    ]
    if combine:
        args += list(first)
        in_specs += [VMEM] * 3
    if acc is not None:
        args += list(acc)
        in_specs += [VMEM] * 4
    acc_shapes = ((width, d), (width, ff), (width, ff), (width, d))
    out_shape = [jax.ShapeDtypeStruct(s, F32) for s in acc_shapes]
    if combine:
        out_shape += [jax.ShapeDtypeStruct((rp, d), BF)] * (2 * n)
        out_shape += [jax.ShapeDtypeStruct((experts, rp), F32)] * n
    else:
        out_shape += [jax.ShapeDtypeStruct((buf_rows, d), BF)] * 2
        out_shape += [jax.ShapeDtypeStruct((n, rp), F32)]
    scratch = [
        pltpu.VMEM((buf_rows, d), BF),
        pltpu.VMEM((buf_rows, d), BF),
        pltpu.VMEM((buf_rows, 128), F32),
        pltpu.VMEM((buf_rows, width), F32),
        pltpu.VMEM((buf_rows, 128), F32),
        pltpu.VMEM((TILE, ff), BF),
        pltpu.VMEM((TILE, ff), F32),
    ]
    if combine:
        scratch += [
            pltpu.VMEM((16, 128), BF),
            pltpu.VMEM((buf_rows, d), BF),
            pltpu.VMEM((buf_rows, d), BF),
        ]
    return pl.pallas_call(
        functools.partial(expert_kernel, cfg),
        grid=(1,),
        out_shape=tuple(out_shape),
        in_specs=in_specs,
        out_specs=tuple([VMEM] * len(out_shape)),
        scratch_shapes=scratch,
        compiler_params=params(60),
        name="experts",
    )(*args)


def attn_bwd_kernel(
    banks, tok, cot, g1, g2, wq, wk, wv, wo, aq, bq, ak, bk, av, bv, ao, bo, rwt, ra, rbt,
    n1, q, k, v, lq, lk, lv, att, lo, mid, n2, lr, pt, lse, gpt, p0, p1, p2,
    inp_o, gr_o, rb_o,
    gmid, gml, ga, gq, gk, gv,
):
    rows, d = tok.shape
    rp = n1.shape[0]
    images = rows // SEQ
    width = aq.shape[1]
    win = lse.shape[2]
    step_rows = 16 * (SEQ // 16)
    probs = pt[...]
    gp = gpt[...]
    glt = (probs * (gp - jnp.sum(gp * probs, axis=0, keepdims=True))).astype(BF)
    rb_o[...] = nn(glt, lr[...])
    mask = bank_mask(banks, 0, rp, images, width)
    gu = (tn(glt, rbt[...]) * mask).astype(BF)
    gr_o[8] = tn(gu, n2[...])
    gmid[...] = tn(glt, rwt[...]) + nt(gu, ra[...])

    def ln2(i, _):
        rs = pl.ds(pl.multiple_of(i * 32, 32), 32)
        grad = gmid[rs, :] + (p0[rs, :].astype(F32) + p1[rs, :].astype(F32) + p2[rs, :].astype(F32))
        xhat, rstd = norm_parts(mid[rs, :])
        g = cot[rs, :].astype(F32) + norm_back(xhat, rstd, g2[...], grad)
        gmid[rs, :] = g
        gml[rs, :] = g.astype(BF)
        return 0

    lax.fori_loop(0, rp // 32, ln2, 0)
    g = gml[...]
    gr_o[7] = tn(lo[...], g)
    gu = (nt(g, bo[...]) * mask).astype(BF)
    gr_o[6] = tn(gu, att[...])
    ga[...] = (nt(g, wo[...]) + nt(gu, ao[...])).astype(BF)

    lane = lax.broadcasted_iota(I32, (win, 128), 1)
    first = lane < HEAD_DIM
    row_i = lax.broadcasted_iota(I32, (win, 128), 0)
    key_i = lax.broadcasted_iota(I32, (win, win), 0)
    query_i = lax.broadcasted_iota(I32, (win, win), 1)

    def image(i, _):
        off = pl.multiple_of(i * step_rows, 64)
        start = i * (SEQ - step_rows)
        bias = jnp.where(
            (key_i >= start) & (key_i < start + SEQ) & (query_i >= start) & (query_i < start + SEQ),
            0.0,
            NEG,
        )
        keep = row_i < start
        ws = pl.ds(off, win)
        for p in range(d // 128):
            cols = slice(p * 128, p * 128 + 128)
            qp = q[ws, cols]
            kp = k[ws, cols]
            vp = v[ws, cols]
            gap = ga[ws, cols]
            rq, rk, rv = [], [], []
            for h in range(2):
                mine = first if h == 0 else jnp.logical_not(first)
                km = jnp.where(mine, kp, jnp.zeros_like(kp))
                vm = jnp.where(mine, vp, jnp.zeros_like(vp))
                prob = jnp.exp2(
                    nt(km, qp) * SCALE2 + bias - lse[i, 2 * p + h : 2 * p + h + 1, :]
                )
                gw = nt(vm, gap)
                delta = jnp.sum(gw * prob, axis=0, keepdims=True)
                gs = (prob * (gw - delta)).astype(BF)
                rv.append(nn(prob.astype(BF), gap))
                rk.append(nn(gs, qp))
                rq.append(tn(gs, kp))
            for parts, ref, scale in ((rq, gq, 0.125), (rk, gk, 0.125), (rv, gv, 1.0)):
                new = (jnp.where(first, parts[0], parts[1]) * scale).astype(BF)
                ref[ws, cols] = jnp.where(keep, ref[ws, cols], new)
        return 0

    lax.fori_loop(0, images, image, 0)
    x = n1[...]
    total = None
    for n, (grad, low, w, a, b) in enumerate(
        ((gq, lq, wq, aq, bq), (gk, lk, wk, ak, bk), (gv, lv, wv, av, bv))
    ):
        g = grad[...]
        gr_o[2 * n + 1] = tn(low[...], g)
        gu = (nt(g, b[...]) * mask).astype(BF)
        gr_o[2 * n] = tn(gu, x)
        part = nt(g, w[...]) + nt(gu, a[...])
        total = part if total is None else total + part

    whole = rows // 16 * 16
    for r, count in [(s, min(112, whole - s)) for s in range(0, whole, 112)] + (
        [(whole, rows - whole)] if rows > whole else []
    ):
        rs = slice(r, r + count)
        xhat, rstd = norm_parts(tok[rs, :].astype(F32))
        inp_o[rs, :] = gmid[rs, :] + norm_back(xhat, rstd, g1[...], total[rs, :])


def attn_backward(banks, tok, cot, g1, g2, ws, kept, gpt, parts):
    rows, d = tok.shape
    rp = cot.shape[0]
    width = ws[4].shape[1]
    experts = gpt.shape[0]
    bfd = pltpu.VMEM((rp, d), BF)
    out_shape = (
        jax.ShapeDtypeStruct((rows, d), F32),
        jax.ShapeDtypeStruct((9, width, d), F32),
        jax.ShapeDtypeStruct((experts, width), F32),
    )
    return pl.pallas_call(
        attn_bwd_kernel,
        out_shape=out_shape,
        in_specs=[SMEM] + [VMEM] * 37,
        out_specs=(VMEM,) * 3,
        scratch_shapes=[pltpu.VMEM((rp, d), F32), bfd, bfd, bfd, bfd, bfd],
        compiler_params=params(60),
        name="attn_bwd",
    )(banks, tok, cot, g1, g2, *ws, *kept, gpt, *parts)


def hop(x, axis, k):
    n = lax.axis_size(axis)
    return lax.ppermute(x, axis, [(i, i ^ k) for i in range(n)])


def bits(axis):
    n = lax.axis_size(axis)
    return [1 << i for i in range(n.bit_length() - 1)]


def all_reduce(buf, steps):
    trail = []
    for axis, k in steps:
        half = buf.shape[0] // 2
        bit = (lax.axis_index(axis) // k) % 2
        keep = lax.dynamic_slice_in_dim(buf, bit * half, half, 0)
        send = lax.dynamic_slice_in_dim(buf, (1 - bit) * half, half, 0).astype(BF)
        buf = keep + hop(send, axis, k).astype(F32)
        trail.append((axis, k, bit))
    buf = buf.astype(BF)
    for axis, k, bit in reversed(trail):
        other = hop(buf, axis, k)
        buf = jnp.where(
            bit == 0,
            jnp.concatenate([buf, other], axis=0),
            jnp.concatenate([other, buf], axis=0),
        )
    return buf.astype(F32)


def gather4(x):
    near = hop(x, "expert", 1)
    far = hop(x, "expert", 2)
    return [x, near, far, hop(far, "expert", 1)]


def body(
    tokens, cotangent, bank_ids, routes, attn_gain, expert_gain, query_w, key_w, value_w, out_w,
    query_a, query_b, key_a, key_b, value_a, value_b, out_a, out_b, router_w, router_a, router_b,
    up_w, up_a, up_b, down_w, down_a, down_b,
):
    rows, d = tokens.shape
    rp = 32 * (-(-rows // 32))
    width = query_a.shape[1]
    local = up_w.shape[0]
    groups = lax.axis_size("expert")
    experts = local * groups
    cap = 13 * rows // (4 * experts)
    me = lax.axis_index("expert").astype(I32).reshape(1)
    cot = jnp.pad(cotangent, ((0, rp - rows), (0, 0)))
    crows = gather4(cot)
    routes_t = jnp.pad(routes.T, ((0, 0), (0, rp - rows)), constant_values=-1)
    routes_all = jnp.stack(gather4(routes_t))
    banks_all = jnp.stack(gather4(bank_ids))
    tables = routing_tables(me, routes_all, local)
    g1 = attn_gain.reshape(1, d)
    g2 = expert_gain.reshape(1, d)
    ws = (
        query_w, key_w, value_w, out_w, query_a, query_b, key_a, key_b, value_a, value_b,
        out_a, out_b, router_w.T, router_a, router_b.T,
    )
    kept = attn_forward(bank_ids, tokens, g1, g2, ws)
    mid, n2, pt = kept[9], kept[10], kept[12]
    nrows = gather4(n2)
    gates = gather4(pt)
    ews = (up_w, up_a, up_b, down_w, down_a, down_b)
    common = (me, banks_all, tables, gates, nrows, crows, ews, cap)
    e0 = expert_call(0, (0, 1, 2, 3), False, *common, None, None)
    acc0, first = e0[:4], e0[4:]
    far = expert_call(1, (2, 3), True, *common, first, None)
    acc1 = far[:4]
    near = expert_call(1, (0, 1), True, *common, first, acc1)
    acc1 = near[:4]

    def fold(a, b):
        mine = a.astype(F32) + hop(b, "expert", 1).astype(F32)
        return hop(mine.astype(a.dtype), "expert", 2)

    grow_far = fold(far[4], far[5])
    gg_far = fold(far[8], far[9])
    mix_far = fold(far[6], far[7])
    grow_near = hop(near[5], "expert", 1)
    gg_near = hop(near[9], "expert", 1)
    mix_near = hop(near[7], "expert", 1)
    gpt = near[8] + gg_near + gg_far
    mixed = mid[:rows] + (
        near[6][:rows].astype(F32) + mix_near[:rows].astype(F32) + mix_far[:rows].astype(F32)
    )
    input_grad, grads, rb = attn_backward(
        bank_ids, tokens, cot, g1, g2, ws, kept, gpt, (near[4], grow_near, grow_far)
    )
    dp_steps = [("dp", k) for k in bits("dp")]
    ex_steps = [("expert", k) for k in bits("expert")]
    pad = jnp.zeros((experts, d - width), F32)
    flat = jnp.concatenate([grads.reshape(9 * width, d), jnp.concatenate([rb, pad], axis=1)])
    shares = lax.axis_size("dp") * groups
    extra = -flat.shape[0] % shares
    flat = jnp.pad(flat, ((0, extra), (0, 0)))
    flat = all_reduce(flat, ex_steps + dp_steps)
    parts = [flat[i * width : (i + 1) * width] for i in range(9)]
    rb = flat[9 * width : 9 * width + experts, :width].T
    outs = []
    for acc in (acc0, acc1):
        outs.append(all_reduce(jnp.concatenate(acc, axis=1), dp_steps))
    ff = up_w.shape[2]
    both = jnp.stack(outs)
    ua = jnp.swapaxes(both[:, :, :d], 1, 2)
    ub = both[:, :, d : d + ff]
    da = jnp.swapaxes(both[:, :, d + ff : d + 2 * ff], 1, 2)
    db = both[:, :, d + 2 * ff :]
    return (
        mixed.astype(BF), input_grad,
        parts[0].T, parts[1], parts[2].T, parts[3], parts[4].T, parts[5], parts[6].T, parts[7],
        parts[8].T, rb, ua, ub, da, db,
    )


def solution(mesh):
    split = P(("dp", "expert"), None)
    by_expert = P("expert", None, None)
    in_specs = (split, split, P(("dp", "expert")), split) + (P(),) * 17 + (by_expert,) * 6
    out_specs = (split, split) + (P(),) * 10 + (by_expert,) * 4
    return jax.shard_map(body, mesh=mesh, in_specs=in_specs, out_specs=out_specs, check_vma=False)
```

```python
import functools
import math

import jax
import jax.numpy as jnp
from jax import lax
from jax.experimental import pallas as pl
from jax.experimental.pallas import tpu as pltpu
from jax.sharding import PartitionSpec as P

HEAD_DIM = 64
RANK = 16
SEQ = 197
EPS = 1e-06
BF = jnp.bfloat16
F32 = jnp.float32
I32 = jnp.int32
LOG2E = math.log2(math.e)
SCALE2 = HEAD_DIM ** (-0.5) * LOG2E
NEG = -1e30
CHUNK = 1536
VMEM = pl.BlockSpec(memory_space=pltpu.VMEM)
SMEM = pl.BlockSpec(memory_space=pltpu.SMEM)
ANY = pl.BlockSpec(memory_space=pl.ANY)


def nn(a, b):
    return jnp.dot(a, b, preferred_element_type=F32)


def nt(a, b):
    return lax.dot_general(a, b, (((1,), (1,)), ((), ())), preferred_element_type=F32)


def tn(a, b):
    return lax.dot_general(a, b, (((0,), (0,)), ((), ())), preferred_element_type=F32)


def params(mib):
    return pltpu.CompilerParams(vmem_limit_bytes=mib * 1024 * 1024)


def cost(us):
    return pl.CostEstimate(
        flops=int(us * 1.1e9), bytes_accessed=int(us * 3e6), transcendentals=0
    )


def split_parts(x, n):
    parts = []
    for _ in range(n):
        low = x.astype(BF)
        parts.append(low)
        x = x - low.astype(F32)
    return parts


def store_lines(ref, start, lines, n):
    d = ref.shape[1]
    for i, part in enumerate(split_parts(lines, n)):
        part = part.astype(F32)
        rest = part.shape[1] - d
        tail = jnp.concatenate(
            [part[:, d:], jnp.zeros((part.shape[0], d - rest), F32)], axis=1
        )
        ref[start + 16 * i : start + 16 * i + 16, :] = jnp.concatenate(
            [part[:, :d], tail], axis=0
        ).astype(BF)


def load_lines(block, rest, n):
    total = sum(block[16 * i : 16 * i + 16, :] for i in range(n))
    return jnp.concatenate([total[:8], total[8:, :rest]], axis=1)


def image_banks(banks, row, images):
    bank = jnp.full(row.shape, banks[0], I32)
    for i in range(1, images):
        bank = jnp.where(row >= SEQ * i, banks[i], bank)
    return bank


def bank_mask(banks, start, count, images, width):
    row = lax.broadcasted_iota(I32, (count, width), 0) + start
    col = lax.broadcasted_iota(I32, (count, width), 1)
    return (col // RANK == image_banks(banks, row, images)).astype(F32)


def norm_parts(x):
    mean = jnp.mean(x, axis=-1, keepdims=True)
    cen = x - mean
    rstd = lax.rsqrt(jnp.mean(cen * cen, axis=-1, keepdims=True) + EPS)
    return cen * rstd, rstd


def norm_back(xhat, rstd, gain, grad):
    gy = grad * gain
    return rstd * (
        gy
        - jnp.mean(gy, axis=-1, keepdims=True)
        - xhat * jnp.mean(gy * xhat, axis=-1, keepdims=True)
    )


def attn_fwd_kernel(
    banks, tok, g1, wq, wk, wv, aq, bq, ak, bk, av, bv,
    n1_o, q_o, k_o, v_o, lq_o, lk_o, lv_o, att_o, lse_o,
    tokp, lset,
):
    rows = tok.shape[0]
    rp = n1_o.shape[0]
    images = rows // SEQ
    d = tok.shape[1]
    width = aq.shape[1]
    win = lse_o.shape[2]
    step_rows = 16 * (SEQ // 16)
    tokp[pl.ds(rp - 16, 16), :] = jnp.zeros((16, d), BF)
    tokp[0:rows, :] = tok[...]

    def ln1(i, _):
        r = pl.multiple_of(i * 32, 32)
        xhat, _r = norm_parts(tokp[pl.ds(r, 32), :].astype(F32))
        n1_o[pl.ds(r, 32), :] = (g1[...] * xhat).astype(BF)
        return 0

    lax.fori_loop(0, rp // 32, ln1, 0)
    half = rp // 2

    def qkv(i, _):
        r = pl.multiple_of(i * half, 16)
        x = n1_o[pl.ds(r, half), :]
        mask = bank_mask(banks, r, half, images, width)
        for w, a, b, out, low in (
            (wq, aq, bq, q_o, lq_o),
            (wk, ak, bk, k_o, lk_o),
            (wv, av, bv, v_o, lv_o),
        ):
            u = (nn(x, a[...]) * mask).astype(BF)
            low[pl.ds(r, half), :] = u
            out[pl.ds(r, half), :] = (nn(x, w[...]) + nn(u, b[...])).astype(BF)
        return 0

    lax.fori_loop(0, 2, qkv, 0)

    lane = lax.broadcasted_iota(I32, (win, 128), 1)
    first = lane < HEAD_DIM
    row_i = lax.broadcasted_iota(I32, (win, 128), 0)
    keys_i = lax.broadcasted_iota(I32, (win, win), 1)

    def image(i, _):
        off = pl.multiple_of(i * step_rows, 64)
        lo = i * (SEQ - step_rows)
        bias = jnp.where((keys_i >= lo) & (keys_i < lo + SEQ), 0.0, NEG)
        keep = row_i < lo
        lset[...] = jnp.zeros_like(lset)
        lse_tile = jnp.zeros((win, 128), F32)
        for p in range(d // 128):
            cols = slice(p * 128, p * 128 + 128)
            qp = q_o[pl.ds(off, win), cols]
            kp = k_o[pl.ds(off, win), cols]
            vp = v_o[pl.ds(off, win), cols]
            outs = []
            for h in range(2):
                mine = first if h == 0 else jnp.logical_not(first)
                qm = jnp.where(mine, qp, jnp.zeros_like(qp))
                s = nt(qm, kp) * SCALE2 + bias
                top = jnp.max(s, axis=-1, keepdims=True)
                e = jnp.exp2(s - top)
                den = jnp.sum(e, axis=-1, keepdims=True)
                w = (e * pl.reciprocal(den)).astype(BF)
                outs.append(nn(w, vp))
                lse = top + jnp.log2(den)
                lse_tile = jnp.where(lane == 2 * p + h, lse, lse_tile)
            new = jnp.where(first, outs[0], outs[1]).astype(BF)
            att_o[pl.ds(off, win), cols] = jnp.where(keep, att_o[pl.ds(off, win), cols], new)
        lset[0:win, :] = lse_tile
        lse_o[i] = jnp.transpose(lset[...])[0 : lse_o.shape[1], 0:win]
        return 0

    lax.fori_loop(0, images, image, 0)


def out_fwd_kernel(
    banks, tok, g2, att, wo, ao, bo, rwt, ra, rbt, *rest
):
    lo_o, mid_o, n2_o, lr_o, pt_o, tokp = rest[-6:]
    rows, d = tok.shape
    rp = att.shape[0]
    images = rows // SEQ
    width = ao.shape[1]
    half = rp // 2
    tokp[pl.ds(rp - 16, 16), :] = jnp.zeros((16, d), BF)
    tokp[0:rows, :] = tok[...]

    def out_proj(i, _):
        r = pl.multiple_of(i * half, 16)
        x = att[pl.ds(r, half), :]
        mask = bank_mask(banks, r, half, images, width)
        u = (nn(x, ao[...]) * mask).astype(BF)
        lo_o[pl.ds(r, half), :] = u
        mid_o[pl.ds(r, half), :] = (
            tokp[pl.ds(r, half), :].astype(F32) + nn(x, wo[...]) + nn(u, bo[...])
        )
        return 0

    lax.fori_loop(0, 2, out_proj, 0)

    def ln2(i, _):
        r = pl.multiple_of(i * 32, 32)
        xhat, _r = norm_parts(mid_o[pl.ds(r, 32), :])
        n2_o[pl.ds(r, 32), :] = (g2[...] * xhat).astype(BF)
        return 0

    lax.fori_loop(0, rp // 32, ln2, 0)
    x = n2_o[0:rp, :]
    u = (nn(x, ra[...]) * bank_mask(banks, 0, rp, images, width)).astype(BF)
    lr_o[...] = u
    logits = nt(rwt[...], x) + nt(rbt[...], u)
    e = jnp.exp(logits - jnp.max(logits, axis=0, keepdims=True))
    probs = e / jnp.sum(e, axis=0, keepdims=True)
    pt_o[...] = probs
    store_lines(n2_o, rp, probs, 3)


def attn_forward(banks, tok, g1, ws):
    rows, d = tok.shape
    rp = 32 * (-(-rows // 32))
    images = rows // SEQ
    step_rows = 16 * (SEQ // 16)
    win = rp - step_rows * (images - 1)
    width = ws[3].shape[1]
    heads_pad = 16 * (-(-d // (16 * HEAD_DIM)))
    bfd = jax.ShapeDtypeStruct((rp, d), BF)
    low = jax.ShapeDtypeStruct((rp, width), BF)
    out_shape = (bfd, bfd, bfd, bfd, low, low, low, bfd) + (
        jax.ShapeDtypeStruct((images, heads_pad, win), F32),
    )
    return pl.pallas_call(
        attn_fwd_kernel,
        out_shape=out_shape,
        in_specs=[SMEM] + [VMEM] * 11,
        out_specs=tuple([VMEM] * len(out_shape)),
        scratch_shapes=[pltpu.VMEM((rp, d), BF), pltpu.VMEM((256, 128), F32)],
        compiler_params=params(56),
        cost_estimate=cost(25),
        name="attn_fwd",
    )(banks, tok, g1, *ws)


def out_forward(banks, tok, g2, att, ws, after):
    rows, d = tok.shape
    rp = att.shape[0]
    low = jax.ShapeDtypeStruct((rp, ws[1].shape[1]), BF)
    out_shape = (
        low,
        jax.ShapeDtypeStruct((rp, d), F32),
        jax.ShapeDtypeStruct((rp + 48, d), BF),
        low,
        jax.ShapeDtypeStruct((ws[3].shape[0], rp), F32),
    )
    return pl.pallas_call(
        out_fwd_kernel,
        out_shape=out_shape,
        in_specs=[SMEM] + [VMEM] * 9 + [ANY] * len(after),
        out_specs=tuple([VMEM] * len(out_shape)),
        scratch_shapes=[pltpu.VMEM((rp, d), BF)],
        compiler_params=params(32),
        cost_estimate=cost(9),
        name="out_fwd",
    )(banks, tok, g2, att, *ws, *after)


def tables_kernel(eidx, routes, posr_o, posc_o):
    groups, _, rp = routes.shape
    local = posr_o.shape[0] // groups
    row = lax.broadcasted_iota(I32, (rp, rp), 0)
    col = lax.broadcasted_iota(I32, (rp, rp), 1)
    upper = (row < col).astype(BF)
    upper_inc = (row <= col).astype(BF)
    lower = (col < row).astype(BF)
    lower_inc = (col <= row).astype(BF)
    which = lax.broadcasted_iota(I32, (groups * local, rp), 0)
    hot = jnp.zeros((groups * local, rp), F32)
    for s in range(groups):
        r0 = routes[s, 0:1, :]
        r1 = routes[s, 1:2, :]
        for j in range(local):
            e = eidx[0] * local + j
            hit = ((r0 == e) | (r1 == e)).astype(F32)
            hot = jnp.where(which == s * local + j, hit, hot)
    hb = hot.astype(BF)
    before = nn(hb, upper)
    with_own = nn(hb, upper_inc)
    posr_o[...] = jnp.where(with_own > before, before, -1.0)
    before = nt(lower, hb)
    with_own = nt(lower_inc, hb)
    posc_o[...] = jnp.where(with_own > before, before, -1.0)


def routing_tables(eidx, routes, local):
    groups, _, rp = routes.shape
    n = groups * local
    return pl.pallas_call(
        tables_kernel,
        out_shape=(jax.ShapeDtypeStruct((n, rp), F32), jax.ShapeDtypeStruct((rp, n), F32)),
        in_specs=[SMEM, VMEM],
        out_specs=(VMEM, VMEM),
        compiler_params=params(32),
        cost_estimate=cost(2),
        name="routing_tables",
    )(eidx, routes)


def gelu_parts(x):
    e = jnp.exp2((-0.5 * LOG2E) * (x * x))
    t = pl.reciprocal(1.0 + (0.3275911 / math.sqrt(2.0)) * jnp.abs(x))
    poly = 1.061405429 * 0.5
    for c in (-1.453152027, 1.421413741, -0.284496736, 0.254829592):
        poly = poly * t + 0.5 * c
    q = poly * t * e
    phi = jnp.where(x >= 0.0, 1.0 - q, q)
    return x * phi, phi + x * (e * (1.0 / math.sqrt(2.0 * math.pi)))


def slot_count(posr, row):
    n = jnp.sum((posr[row : row + 1, :] >= 0.0).astype(F32)).astype(I32)
    return ((n + 15) // 16) * 16


def expert_kernel(cfg, *refs):
    j, sources, has_acc, merge, cap, local, experts = cfg
    n = len(sources)
    refs = list(refs)
    take = lambda k: [refs.pop(0) for _ in range(k)]
    (eidx,) = take(1)
    posr, meta = take(2)
    nrows = take(n)
    crows = take(n)
    upw, upa, upb, dnw, dna, dnb = take(6)
    if has_acc:
        (acc_in,) = take(1)
    if merge:
        posc, ret_in, grow_in, gg_in = take(4)
    (acc,) = take(1)
    if merge:
        grow_o = take(n)
        mix_o = take(n)
    else:
        ret_b, grow_b, gg_o = take(3)
    up, ua, dn, db, xbuf, cbuf, gate_b, mask_b, gg_b, hid, dgl, sems = take(12)
    if merge:
        ret_b, grow_b, ret0, grow0 = take(4)
    rp = posr.shape[1]
    d = upw.shape[1]
    ff = upw.shape[2]
    width = upa.shape[2]
    loads = [
        pltpu.make_async_copy(upa.at[j], ua, sems.at[0]),
        pltpu.make_async_copy(upw.at[j], up.at[0:d], sems.at[1]),
        pltpu.make_async_copy(upb.at[j], up.at[d : d + width], sems.at[2]),
        pltpu.make_async_copy(dnw.at[j], dn.at[:, 0:d], sems.at[3]),
        pltpu.make_async_copy(dna.at[j], dn.at[:, d : d + width], sems.at[4]),
        pltpu.make_async_copy(dnb.at[j], db, sems.at[5]),
    ]
    if has_acc:
        loads.append(pltpu.make_async_copy(acc_in, acc, sems.at[6]))
    if merge:
        loads.append(pltpu.make_async_copy(ret_in, ret0, sems.at[7]))
        loads.append(pltpu.make_async_copy(grow_in, grow0, sems.at[8]))
    for load in loads:
        load.start()
    if not has_acc:
        acc[...] = jnp.zeros_like(acc)
    slot_r = lax.broadcasted_iota(I32, (cap, rp), 0).astype(F32)
    mine = lax.broadcasted_iota(I32, (experts, rp), 0) == eidx[0] * local + j
    col_bank = (lax.broadcasted_iota(I32, (cap, width), 1) // RANK).astype(F32)
    offs = []
    off = jnp.int32(0)
    for i, s in enumerate(sources):
        off = pl.multiple_of(off, 16)
        offs.append(off)
        hit = posr[s * local + j : s * local + j + 1, :] == slot_r
        probs = load_lines(nrows[i][rp : rp + 48, :].astype(F32), rp - d, 3)
        gate_line = jnp.sum(jnp.where(mine, probs, 0.0), axis=0, keepdims=True)
        bank = meta[s, 2:3, :].astype(F32)
        gate = jnp.sum(jnp.where(hit, gate_line, 0.0), axis=1, keepdims=True)
        slot_bank = jnp.sum(jnp.where(hit, bank, 0.0), axis=1, keepdims=True)
        pick = hit.astype(F32).astype(BF)
        xbuf[pl.ds(off, cap), :] = nn(pick, nrows[i][0:rp, :]).astype(BF)
        cbuf[pl.ds(off, cap), :] = nn(pick, crows[i][...]).astype(BF)
        gate_b[pl.ds(off, cap), :] = jnp.broadcast_to(gate, (cap, 128))
        mask_b[pl.ds(off, cap), :] = (col_bank == slot_bank).astype(F32)
        off = off + slot_count(posr, s * local + j)
    total = off
    rest = pl.ds(pl.multiple_of(offs[-1] + cap, 16), cap)
    xbuf[rest, :] = jnp.zeros((cap, d), BF)
    cbuf[rest, :] = jnp.zeros((cap, d), BF)
    gate_b[rest, :] = jnp.zeros((cap, 128), F32)
    mask_b[rest, :] = jnp.zeros((cap, width), F32)
    tiles = (total + cap - 1) // cap
    chunks = [slice(c, min(c + CHUNK, ff)) for c in range(0, ff, CHUNK)]
    for load in loads:
        load.wait()

    def tile(t, _):
        rs = pl.ds(pl.multiple_of(t * cap, 16), cap)
        x = xbuf[rs, :]
        m = mask_b[rs, :]
        u = (nn(x, ua[...]) * m).astype(BF)
        xu = jnp.concatenate([x, u], axis=1)
        out = jnp.zeros((cap, d + width), F32)
        for cs in chunks:
            h, dg = gelu_parts(nn(xu, up[:, cs]))
            hb = h.astype(BF)
            hid[:, cs] = hb
            dgl[:, cs] = dg
            out = out + nn(hb, dn[cs, :])
        ud = (out[:, d:] * m).astype(BF)
        ret = (out[:, :d] + nn(ud, db[...])).astype(BF).astype(F32)
        cot = cbuf[rs, :].astype(F32)
        gate = gate_b[rs, 0:1]
        gg_b[rs, :] = jnp.broadcast_to(jnp.sum(cot * ret, axis=1, keepdims=True), (cap, 128))
        ret_b[rs, :] = (gate * ret).astype(BF)
        g = (gate * cot).astype(BF)
        gud = (nt(g, db[...]) * m).astype(BF)
        acc[:, d + 2 * ff :] += tn(ud, g)
        gg = jnp.concatenate([g, gud], axis=1)
        gr = jnp.zeros((cap, d + width), F32)
        for cs in chunks:
            gp = (nt(gg, dn[cs, :]) * dgl[:, cs]).astype(BF)
            gr = gr + nt(gp, up[:, cs])
            acc[:, d + cs.start : d + cs.stop] += tn(u, gp)
            acc[:, d + ff + cs.start : d + ff + cs.stop] += tn(gud, hid[:, cs])
        guu = (gr[:, d:] * m).astype(BF)
        acc[:, 0:d] += tn(guu, x)
        grow_b[rs, :] = (gr[:, :d] + nt(guu, ua[...])).astype(BF)
        return 0

    lax.fori_loop(0, tiles, tile, 0)
    done = pl.ds(pl.multiple_of(tiles * cap, 16), cap)
    ret_b[done, :] = jnp.zeros((cap, d), BF)
    grow_b[done, :] = jnp.zeros((cap, d), BF)
    gg_b[done, :] = jnp.zeros((cap, 128), F32)
    gg_lines = []
    for i, s in enumerate(sources):
        hit = posr[s * local + j : s * local + j + 1, :] == slot_r
        col = gg_b[pl.ds(offs[i], cap), 0:1]
        gg_lines.append(jnp.sum(jnp.where(hit, col, 0.0), axis=0, keepdims=True))
    if not merge:
        for i in range(n):
            gg_o[i : i + 1, :] = gg_lines[i]
    else:
        slot_c = lax.broadcasted_iota(I32, (rp, cap), 1).astype(F32)
        expert_row = lax.broadcasted_iota(I32, (experts, rp), 0)
        off0 = jnp.int32(0)
        for i, s in enumerate(sources):
            r0 = pl.ds(pl.multiple_of(off0, 16), cap)
            r1 = pl.ds(offs[i], cap)
            p0 = (posc[:, s * local : s * local + 1] == slot_c).astype(F32).astype(BF)
            p1 = (posc[:, s * local + 1 : s * local + 2] == slot_c).astype(F32).astype(BF)
            pick = jnp.concatenate([p0, p1], axis=1)
            for b0, b1, result in ((grow0, grow_b, grow_o[i]), (ret0, ret_b, mix_o[i])):
                both = jnp.concatenate([b0[r0, :], b1[r1, :]], axis=0)
                result[0:rp, :] = nn(pick, both).astype(BF)
            gg = jnp.where(
                expert_row == eidx[0] * local,
                gg_in[i : i + 1, :],
                jnp.where(expert_row == eidx[0] * local + 1, gg_lines[i], 0.0),
            )
            store_lines(grow_o[i], rp, gg, 2)
            off0 = off0 + slot_count(posr, s * local)


def expert_call(j, sources, eidx, tables, nrows, crows, ws, cap, acc, first=None):
    posr, posc, meta = tables
    rp, d = crows[0].shape
    local, _, ff = ws[0].shape
    width = ws[1].shape[2]
    n = len(sources)
    experts = local * lax.axis_size("expert")
    merge = first is not None
    cfg = (j, tuple(sources), acc is not None, merge, cap, local, experts)
    buf = (n + 1) * cap
    args = [eidx, posr, meta]
    args += [nrows[s] for s in sources] + [crows[s] for s in sources] + list(ws)
    in_specs = [SMEM] + [VMEM] * (2 + 2 * n) + [ANY] * 6
    if acc is not None:
        args.append(acc)
        in_specs.append(ANY)
    if merge:
        args += [posc, *first]
        in_specs += [VMEM, ANY, ANY, VMEM]
    wide = (width, 2 * d + 2 * ff)
    out_shape = (jax.ShapeDtypeStruct(wide, F32),)
    if merge:
        out_shape += (jax.ShapeDtypeStruct((rp + 32, d), BF),) * n
        out_shape += (jax.ShapeDtypeStruct((rp, d), BF),) * n
    else:
        out_shape += (jax.ShapeDtypeStruct((buf, d), BF),) * 2
        out_shape += (jax.ShapeDtypeStruct((n, rp), F32),)
    scratch = [
        pltpu.VMEM((d + width, ff), BF),
        pltpu.VMEM((d, width), BF),
        pltpu.VMEM((ff, d + width), BF),
        pltpu.VMEM((width, d), BF),
        pltpu.VMEM((buf, d), BF),
        pltpu.VMEM((buf, d), BF),
        pltpu.VMEM((buf, 128), F32),
        pltpu.VMEM((buf, width), F32),
        pltpu.VMEM((buf, 128), F32),
        pltpu.VMEM((cap, ff), BF),
        pltpu.VMEM((cap, ff), F32),
        pltpu.SemaphoreType.DMA((9,)),
    ]
    if merge:
        scratch += [pltpu.VMEM((buf, d), BF)] * 4
    return pl.pallas_call(
        functools.partial(expert_kernel, cfg),
        out_shape=out_shape,
        in_specs=in_specs,
        out_specs=(VMEM,) * len(out_shape),
        scratch_shapes=scratch,
        compiler_params=params(56 if merge else 44),
        cost_estimate=cost(30),
        name=f"expert{j}_{'far' if sources[0] else 'near'}",
    )(*args)


def out_bwd_kernel(
    banks, cot, g2, att, lo, mid, n2, lr, pt, wo, ao, bo, rwt, ra, rbt, p0, p1, p2,
    gmid, ga, gr_o,
    gml,
):
    rp, d = cot.shape
    experts = pt.shape[0]
    images = banks.shape[0]
    width = ao.shape[1]
    probs = pt[...]
    lines = sum(p[rp : rp + 32, :].astype(F32) for p in (p0, p1, p2))
    gp = load_lines(lines, rp - d, 2)
    glt = (probs * (gp - jnp.sum(gp * probs, axis=0, keepdims=True))).astype(BF)
    rb = jnp.concatenate([nn(glt, lr[...]), jnp.zeros((experts, d - width), F32)], axis=1)
    rb = jnp.concatenate([rb, jnp.zeros((32 - experts, d), F32)], axis=0)
    gr_o[3 * width : 3 * width + 32, :] = rb.astype(BF)
    mask = bank_mask(banks, 0, rp, images, width)
    gu = (tn(glt, rbt[...]) * mask).astype(BF)
    gr_o[2 * width : 3 * width, :] = tn(gu, n2[0:rp, :]).astype(BF)
    gmid[...] = tn(glt, rwt[...]) + nt(gu, ra[...])

    def ln2(i, _):
        rs = pl.ds(pl.multiple_of(i * 32, 32), 32)
        grad = gmid[rs, :] + (p0[rs, :].astype(F32) + p1[rs, :].astype(F32) + p2[rs, :].astype(F32))
        xhat, rstd = norm_parts(mid[rs, :])
        g = cot[rs, :].astype(F32) + norm_back(xhat, rstd, g2[...], grad)
        gmid[rs, :] = g
        gml[rs, :] = g.astype(BF)
        return 0

    lax.fori_loop(0, rp // 32, ln2, 0)
    g = gml[...]
    gr_o[width : 2 * width, :] = tn(lo[...], g).astype(BF)
    gu = (nt(g, bo[...]) * mask).astype(BF)
    gr_o[0:width, :] = tn(gu, att[...]).astype(BF)
    ga[...] = (nt(g, wo[...]) + nt(gu, ao[...])).astype(BF)


def out_backward(banks, cot, g2, kept, ws, parts):
    rp, d = cot.shape
    width = ws[1].shape[1]
    return pl.pallas_call(
        out_bwd_kernel,
        out_shape=(
            jax.ShapeDtypeStruct((rp, d), F32),
            jax.ShapeDtypeStruct((rp, d), BF),
            jax.ShapeDtypeStruct((3 * width + 32, d), BF),
        ),
        in_specs=[SMEM] + [VMEM] * 17,
        out_specs=(VMEM,) * 3,
        scratch_shapes=[pltpu.VMEM((rp, d), BF)],
        compiler_params=params(48),
        cost_estimate=cost(14),
        name="out_bwd",
    )(banks, cot, g2, *kept, *ws, *parts)


def attn_bwd_kernel(
    banks, n1, q, k, v, lq, lk, lv, lse, ga, bq, bk, bv,
    gq, gk, gv, uq, uk, uv, gr_o,
):
    rp, d = n1.shape
    images = banks.shape[0]
    width = bq.shape[0]
    win = lse.shape[2]
    step_rows = 16 * (SEQ // 16)
    lane = lax.broadcasted_iota(I32, (win, 128), 1)
    first = lane < HEAD_DIM
    row_i = lax.broadcasted_iota(I32, (win, 128), 0)
    key_i = lax.broadcasted_iota(I32, (win, win), 0)
    query_i = lax.broadcasted_iota(I32, (win, win), 1)

    def image(i, _):
        off = pl.multiple_of(i * step_rows, 64)
        start = i * (SEQ - step_rows)
        bias = jnp.where(
            (key_i >= start) & (key_i < start + SEQ) & (query_i >= start) & (query_i < start + SEQ),
            0.0,
            NEG,
        )
        keep = row_i < start
        ws = pl.ds(off, win)
        for p in range(d // 128):
            cols = slice(p * 128, p * 128 + 128)
            qp = q[ws, cols]
            kp = k[ws, cols]
            vp = v[ws, cols]
            gap = ga[ws, cols]
            rq, rk, rv = [], [], []
            for h in range(2):
                mine = first if h == 0 else jnp.logical_not(first)
                km = jnp.where(mine, kp, jnp.zeros_like(kp))
                vm = jnp.where(mine, vp, jnp.zeros_like(vp))
                prob = jnp.exp2(
                    nt(km, qp) * SCALE2 + bias - lse[i, 2 * p + h : 2 * p + h + 1, :]
                )
                gw = nt(vm, gap)
                delta = jnp.sum(gw * prob, axis=0, keepdims=True)
                gs = (prob * (gw - delta)).astype(BF)
                rv.append(nn(prob.astype(BF), gap))
                rk.append(nn(gs, qp))
                rq.append(tn(gs, kp))
            for parts, ref, scale in ((rq, gq, 0.125), (rk, gk, 0.125), (rv, gv, 1.0)):
                new = (jnp.where(first, parts[0], parts[1]) * scale).astype(BF)
                ref[ws, cols] = jnp.where(keep, ref[ws, cols], new)
        return 0

    lax.fori_loop(0, images, image, 0)
    x = n1[...]
    mask = bank_mask(banks, 0, rp, images, width)
    for i, (grad, low, b, u) in enumerate(((gq, lq, bq, uq), (gk, lk, bk, uk), (gv, lv, bv, uv))):
        g = grad[...]
        gr_o[(2 * i + 1) * width : (2 * i + 2) * width, :] = tn(low[...], g).astype(BF)
        gu = (nt(g, b[...]) * mask).astype(BF)
        u[...] = gu
        gr_o[2 * i * width : (2 * i + 1) * width, :] = tn(gu, x).astype(BF)


def attn_backward(banks, kept, ga, bs):
    rp, d = ga.shape
    width = bs[0].shape[0]
    bfd = jax.ShapeDtypeStruct((rp, d), BF)
    low = jax.ShapeDtypeStruct((rp, width), BF)
    return pl.pallas_call(
        attn_bwd_kernel,
        out_shape=(bfd, bfd, bfd, low, low, low, jax.ShapeDtypeStruct((6 * width, d), BF)),
        in_specs=[SMEM] + [VMEM] * 12,
        out_specs=(VMEM,) * 7,
        compiler_params=params(48),
        cost_estimate=cost(25),
        name="attn_bwd",
    )(banks, *kept, ga, *bs)


def input_bwd_kernel(
    tok, g1, gmid, gq, gk, gv, uq, uk, uv, wq, wk, wv, aq, ak, av, inp_o, total
):
    rows, d = tok.shape
    total[...] = (
        (nt(gq[...], wq[...]) + nt(uq[...], aq[...]))
        + (nt(gk[...], wk[...]) + nt(uk[...], ak[...]))
        + (nt(gv[...], wv[...]) + nt(uv[...], av[...]))
    )
    whole = rows // 16 * 16
    for r, count in [(s, min(112, whole - s)) for s in range(0, whole, 112)] + (
        [(whole, rows - whole)] if rows > whole else []
    ):
        rs = slice(r, r + count)
        xhat, rstd = norm_parts(tok[rs, :].astype(F32))
        inp_o[rs, :] = gmid[rs, :] + norm_back(xhat, rstd, g1[...], total[rs, :])


def input_backward(tok, g1, gmid, grads, ws):
    rows, d = tok.shape
    return pl.pallas_call(
        input_bwd_kernel,
        out_shape=jax.ShapeDtypeStruct((rows, d), F32),
        in_specs=[VMEM] * 15,
        out_specs=VMEM,
        scratch_shapes=[pltpu.VMEM(gmid.shape, F32)],
        compiler_params=params(48),
        cost_estimate=cost(10),
        name="input_bwd",
    )(tok, g1, gmid, *grads, *ws)


def finish_kernel(qkv, outr, *outs):
    width, d = outs[1].shape
    experts = outs[9].shape[1]
    for i in range(4):
        src, base = (qkv, 2 * i * width) if i < 3 else (outr, 0)
        outs[2 * i][...] = jnp.transpose(src[base : base + width, :].astype(F32))
        outs[2 * i + 1][...] = src[base + width : base + 2 * width, :].astype(F32)
    outs[8][...] = jnp.transpose(outr[2 * width : 3 * width, :].astype(F32))
    rb = jnp.transpose(outr[3 * width : 3 * width + 16, 0:width].astype(F32))
    outs[9][...] = rb[:, 0:experts]


def finish(qkv, outr, width, experts):
    d = qkv.shape[1]
    tall = jax.ShapeDtypeStruct((d, width), F32)
    wide = jax.ShapeDtypeStruct((width, d), F32)
    return pl.pallas_call(
        finish_kernel,
        out_shape=(tall, wide) * 4 + (tall, jax.ShapeDtypeStruct((width, experts), F32)),
        in_specs=[VMEM] * 2,
        out_specs=(VMEM,) * 10,
        compiler_params=params(32),
        cost_estimate=cost(3),
        name="finish",
    )(qkv, outr)


def finish_experts_kernel(*refs):
    ins, (ua, ub, da, db) = refs[:-4], refs[-4:]
    d, width = ua.shape[1:]
    ff = ub.shape[2]
    for j, src in enumerate(ins):
        ua[j] = jnp.transpose(src[:, 0:d].astype(F32))
        ub[j] = src[:, d : d + ff].astype(F32)
        da[j] = jnp.transpose(src[:, d + ff : d + 2 * ff].astype(F32))
        db[j] = src[:, d + 2 * ff :].astype(F32)


def finish_experts(bufs, d, ff):
    n = len(bufs)
    width = bufs[0].shape[0]
    shapes = ((n, d, width), (n, width, ff), (n, ff, width), (n, width, d))
    return pl.pallas_call(
        finish_experts_kernel,
        out_shape=tuple(jax.ShapeDtypeStruct(s, F32) for s in shapes),
        in_specs=[VMEM] * n,
        out_specs=(VMEM,) * 4,
        compiler_params=params(32),
        cost_estimate=cost(5),
        name="finish_experts",
    )(*bufs)


def hop(x, axis, k):
    n = lax.axis_size(axis)
    return lax.ppermute(x, axis, [(i, i ^ k) for i in range(n)])


def bits(axis):
    n = lax.axis_size(axis)
    return [1 << i for i in range(n.bit_length() - 1)]


def add(a, b):
    return (a.astype(F32) + b.astype(F32)).astype(BF)


def part_of(terms, bit, flip):
    half = terms[0].shape[0] // 2
    start = (bit if not flip else 1 - bit) * half
    return sum(lax.dynamic_slice_in_dim(t, start, half, 0).astype(F32) for t in terms).astype(BF)


def reduce_step(terms, axis, k):
    bit = (lax.axis_index(axis) // k) % 2
    send = part_of(terms, bit, True)
    return send, part_of(terms, bit, False), hop(send, axis, k)


def gather_step(buf, axis, k, wait=None):
    bit = (lax.axis_index(axis) // k) % 2
    other = hop(buf, axis, k)
    other = other if wait is None else after(other, wait)
    return jnp.where(
        bit == 0,
        jnp.concatenate([buf, other], axis=0),
        jnp.concatenate([other, buf], axis=0),
    )


def after(x, *deps):
    return lax.optimization_barrier((x,) + deps)[0]


def gather4(x):
    near = hop(x, "expert", 1)
    far = hop(x, "expert", 2)
    return [x, near, far, hop(far, "expert", 1)]


def body(
    tokens, cotangent, bank_ids, routes, attn_gain, expert_gain, query_w, key_w, value_w, out_w,
    query_a, query_b, key_a, key_b, value_a, value_b, out_a, out_b, router_w, router_a, router_b,
    up_w, up_a, up_b, down_w, down_a, down_b,
):
    rows, d = tokens.shape
    rp = 32 * (-(-rows // 32))
    width = query_a.shape[1]
    local = up_w.shape[0]
    groups = lax.axis_size("expert")
    experts = local * groups
    cap = 13 * rows // (4 * experts)
    me = lax.axis_index("expert").astype(I32).reshape(1)
    cot = jnp.pad(cotangent, ((0, rp - rows), (0, 0)))
    cot1 = hop(cot, "expert", 1)
    cot2 = hop(cot, "expert", 2)
    meta = jnp.concatenate([routes.T, jnp.repeat(bank_ids, SEQ)[None, :]], axis=0)
    meta = jnp.pad(meta, ((0, 0), (0, rp - rows)), constant_values=-1)
    meta = jnp.stack(gather4(meta))
    tables = routing_tables(me, meta, local) + (meta,)
    g1 = attn_gain.reshape(1, d)
    g2 = expert_gain.reshape(1, d)
    kept = attn_forward(
        bank_ids, tokens, g1,
        (query_w, key_w, value_w, query_a, query_b, key_a, key_b, value_a, value_b),
    )
    n1, q, k, v, lq, lk, lv, att, lse = kept
    out_ws = (out_w, out_a, out_b, router_w.T, router_a, router_b.T)
    lo, mid, n2, lr, pt = out_forward(
        bank_ids, tokens, g2, after(att, tables[0]), out_ws, (cot1, cot2)
    )
    near1 = hop(n2, "expert", 1)
    far2 = hop(n2, "expert", 2)
    cot3 = hop(after(cot2, n2), "expert", 1)
    crows = [cot, cot1, cot2, cot3]
    ews = (up_w, up_a, up_b, down_w, down_a, down_b)
    common = (crows, ews, cap)
    nrows = [n2, near1, None, None]
    e0n = expert_call(0, (0, 1), me, tables, nrows, *common, None)
    far2 = after(far2, e0n[1])
    nrows = [n2, near1, far2, hop(far2, "expert", 1)]
    e0f = expert_call(0, (2, 3), me, tables, nrows, *common, e0n[0])
    dp_steps = [("dp", k) for k in bits("dp")]
    ex_steps = [("expert", k) for k in bits("expert")]
    send0, keep0, got0 = reduce_step([e0f[0]], *dp_steps[0])
    e1f = expert_call(
        1, (2, 3), after(me, e0f[1], send0), tables, nrows, *common, None, e0f[1:]
    )
    grow = add(e1f[1], hop(e1f[2], "expert", 1))
    mix = add(e1f[3], hop(e1f[4], "expert", 1))
    send0, keep0, got0 = reduce_step([keep0, after(got0, e1f[1])], *dp_steps[1])
    e1n = expert_call(
        1, (0, 1), after(me, grow, send0), tables, nrows, *common, e1f[0], e0n[1:]
    )
    near = e1n[1:]
    grow_far = hop(grow, "expert", 2)
    grow_near = hop(after(near[1], grow_far), "expert", 1)
    mix_far = hop(after(mix, near[0]), "expert", 2)
    send0, keep0, got0 = reduce_step([keep0, after(got0, near[0])], *dp_steps[2])
    send1, keep1, got1 = reduce_step([after(e1n[0], near[0])], *dp_steps[0])
    gmid, ga, outr = out_backward(
        bank_ids, cot, g2, (att, lo, mid, n2, lr, pt), out_ws,
        (near[0], after(grow_near, send0, send1), grow_far),
    )
    got0 = after(got0, gmid)
    for step in dp_steps[3:]:
        _, keep0, got0 = reduce_step([keep0, got0], *step)
    buf0 = add(keep0, got0)
    send1, keep1, got1 = reduce_step([keep1, after(got1, gmid)], *dp_steps[1])
    *grads, qkv = attn_backward(
        bank_ids, (n1, q, k, v, lq, lk, lv, lse), after(ga, buf0, send1),
        (query_b, key_b, value_b),
    )
    up_steps = dp_steps[::-1]
    buf0 = gather_step(buf0, *up_steps[0], wait=qkv)
    mix_near = hop(after(near[3], qkv), "expert", 1)
    got1 = after(got1, qkv)
    shares = lax.axis_size("dp") * groups
    used = qkv.shape[0]
    flat = jnp.concatenate([qkv, outr], axis=0)
    flat = jnp.pad(flat, ((0, -flat.shape[0] % shares), (0, 0)))
    _, keep, got = reduce_step([flat], *ex_steps[0])
    send, keep, got = reduce_step([keep, got], *ex_steps[1])
    input_grad = input_backward(
        tokens, g1, after(gmid, send), grads,
        (query_w, key_w, value_w, query_a, key_a, value_a),
    )
    got = after(got, input_grad)
    for step in up_steps[1:]:
        buf0 = gather_step(buf0, *step)
    for step in dp_steps[2:]:
        _, keep1, got1 = reduce_step([keep1, got1], *step)
    buf1 = add(keep1, got1)
    for step in ex_steps[2:] + dp_steps:
        _, keep, got = reduce_step([keep, got], *step)
    flat = add(keep, got)
    for step in up_steps:
        buf1 = gather_step(buf1, *step)
    for step in reversed(ex_steps + dp_steps):
        flat = gather_step(flat, *step)
    qkv, outr = flat[:used], flat[used:]
    mixed = mid[:rows] + (
        near[2][:rows].astype(F32) + mix_near[:rows].astype(F32) + mix_far[:rows].astype(F32)
    )
    small = finish(qkv, outr, width, experts)
    large = finish_experts((buf0, buf1), d, up_w.shape[2])
    return (mixed.astype(BF), input_grad, *small, *large)


def solution(mesh):
    split = P(("dp", "expert"), None)
    by_expert = P("expert", None, None)
    in_specs = (split, split, P(("dp", "expert")), split) + (P(),) * 17 + (by_expert,) * 6
    out_specs = (split, split) + (P(),) * 10 + (by_expert,) * 4
    return jax.shard_map(body, mesh=mesh, in_specs=in_specs, out_specs=out_specs, check_vma=False)
```

```python
import functools
import math

import jax
import jax.numpy as jnp
from jax import lax
from jax.experimental import pallas as pl
from jax.experimental.pallas import tpu as pltpu
from jax.sharding import PartitionSpec as P

HEAD_DIM = 64
RANK = 16
SEQ = 197
EPS = 1e-06
BF = jnp.bfloat16
F32 = jnp.float32
I32 = jnp.int32
LOG2E = math.log2(math.e)
SCALE2 = HEAD_DIM ** (-0.5) * LOG2E
NEG = -1e30
CHUNK = 1536
VMEM = pl.BlockSpec(memory_space=pltpu.VMEM)
SMEM = pl.BlockSpec(memory_space=pltpu.SMEM)
HBM = pl.BlockSpec(memory_space=pltpu.HBM)


def nn(a, b):
    return jnp.dot(a, b, preferred_element_type=F32)


def nt(a, b):
    return lax.dot_general(a, b, (((1,), (1,)), ((), ())), preferred_element_type=F32)


def tn(a, b):
    return lax.dot_general(a, b, (((0,), (0,)), ((), ())), preferred_element_type=F32)


def params(mib):
    return pltpu.CompilerParams(vmem_limit_bytes=mib * 1024 * 1024)


def cost(us):
    return pl.CostEstimate(
        flops=int(us * 1.1e9), bytes_accessed=int(us * 3e6), transcendentals=0
    )


def staged(kernel, args, kinds, outs, scratch, mib, us, name, direct=False, aliases=None):
    specs = {"s": SMEM, "v": VMEM, "h": HBM, "m": HBM}
    moved = [i for i, k in enumerate(kinds) if k == "m"]
    large = [] if direct else [
        i
        for i, o in enumerate(outs)
        if math.prod(o.shape) >= 1 << 15 and (o.dtype == F32 or o.shape[-2] % 16 == 0)
    ]
    n_in, n_out = len(args), len(outs)
    copies = len(moved) + len(large)

    def run(*refs):
        ins, results = list(refs[:n_in]), list(refs[n_in : n_in + n_out])
        own = refs[n_in + n_out : n_in + n_out + len(scratch)]
        buffers = refs[n_in + n_out + len(scratch) : -1]
        sems = refs[-1]
        arriving, leaving = [], []
        for n, i in enumerate(moved):
            copy = pltpu.make_async_copy(ins[i], buffers[n], sems.at[n])
            copy.start(priority=1)
            arriving.append([buffers[n], copy, False])
            ins[i] = buffers[n]
        for n, i in enumerate(large, len(moved)):
            copy = pltpu.make_async_copy(buffers[n], results[i], sems.at[n])
            leaving.append([buffers[n], copy, False])
            results[i] = buffers[n]

        def need(*wanted):
            for entry in arriving:
                if not entry[2] and any(entry[0] is ref for ref in wanted):
                    entry[1].wait()
                    entry[2] = True

        def flush(*ready):
            for entry in leaving:
                if not entry[2] and any(entry[0] is ref for ref in ready):
                    entry[1].start()
                    entry[2] = True

        kernel(need, flush, *ins, *results, *own)
        need(*[entry[0] for entry in arriving])
        flush(*[entry[0] for entry in leaving])
        for entry in leaving:
            entry[1].wait()

    return pl.pallas_call(
        run,
        out_shape=tuple(outs),
        in_specs=[specs[k] for k in kinds],
        out_specs=tuple(HBM if direct or i in large else VMEM for i in range(n_out)),
        input_output_aliases=aliases or {},
        scratch_shapes=list(scratch)
        + [pltpu.VMEM(args[i].shape, args[i].dtype) for i in moved]
        + [pltpu.VMEM(outs[i].shape, outs[i].dtype) for i in large]
        + [pltpu.SemaphoreType.DMA((max(copies, 1),))],
        compiler_params=params(60 if mib == 60 else 63),
        cost_estimate=cost(us),
        name=name,
    )(*args)


def split_parts(x, n):
    parts = []
    for _ in range(n):
        low = x.astype(BF)
        parts.append(low)
        x = x - low.astype(F32)
    return parts


def store_lines(ref, start, lines, n):
    d = ref.shape[1]
    for i, part in enumerate(split_parts(lines, n)):
        part = part.astype(F32)
        rest = part.shape[1] - d
        tail = jnp.concatenate(
            [part[:, d:], jnp.zeros((part.shape[0], d - rest), F32)], axis=1
        )
        ref[start + 16 * i : start + 16 * i + 16, :] = jnp.concatenate(
            [part[:, :d], tail], axis=0
        ).astype(BF)


def load_lines(block, rest, n):
    total = sum(block[16 * i : 16 * i + 16, :] for i in range(n))
    return jnp.concatenate([total[:8], total[8:, :rest]], axis=1)


def image_banks(banks, row, images):
    bank = jnp.full(row.shape, banks[0], I32)
    for i in range(1, images):
        bank = jnp.where(row >= SEQ * i, banks[i], bank)
    return bank


def bank_mask(banks, start, count, images, width):
    row = lax.broadcasted_iota(I32, (count, width), 0) + start
    col = lax.broadcasted_iota(I32, (count, width), 1)
    return (col // RANK == image_banks(banks, row, images)).astype(F32)


def norm_parts(x):
    mean = jnp.mean(x, axis=-1, keepdims=True)
    cen = x - mean
    rstd = lax.rsqrt(jnp.mean(cen * cen, axis=-1, keepdims=True) + EPS)
    return cen * rstd, rstd


def norm_back(xhat, rstd, gain, grad):
    gy = grad * gain
    return rstd * (
        gy
        - jnp.mean(gy, axis=-1, keepdims=True)
        - xhat * jnp.mean(gy * xhat, axis=-1, keepdims=True)
    )


def attn_fwd_kernel(
    need, flush, banks, tok, g1, wq, aq, bq, wk, ak, bk, wv, av, bv,
    n1_o, q_o, k_o, v_o, lq_o, lk_o, lv_o, att_o, lse_o,
    tokp, lset,
):
    rows = tok.shape[0]
    rp = n1_o.shape[0]
    images = rows // SEQ
    d = tok.shape[1]
    width = aq.shape[1]
    win = lse_o.shape[2]
    step_rows = 16 * (SEQ // 16)
    tokp[pl.ds(rp - 16, 16), :] = jnp.zeros((16, d), BF)
    tokp[0:rows, :] = tok[...]

    def ln1(i, _):
        r = pl.multiple_of(i * 160, 160)
        xhat, _r = norm_parts(tokp[pl.ds(r, 160), :].astype(F32))
        n1_o[pl.ds(r, 160), :] = (g1[...] * xhat).astype(BF)
        return 0

    lax.fori_loop(0, rp // 160, ln1, 0)
    flush(n1_o)
    half = rp // 2
    for w, a, b, out, low in (
        (wq, aq, bq, q_o, lq_o),
        (wk, ak, bk, k_o, lk_o),
        (wv, av, bv, v_o, lv_o),
    ):
        need(w, a, b)
        for r in (0, half):
            x = n1_o[r : r + half, :]
            mask = bank_mask(banks, r, half, images, width)
            u = (nn(x, a[...]) * mask).astype(BF)
            low[r : r + half, :] = u
            out[r : r + half, :] = (nn(x, w[...]) + nn(u, b[...])).astype(BF)
        flush(out, low)

    lane = lax.broadcasted_iota(I32, (win, 128), 1)
    first = lane < HEAD_DIM
    row_i = lax.broadcasted_iota(I32, (win, 128), 0)
    keys_i = lax.broadcasted_iota(I32, (win, win), 1)

    def image(i, _):
        off = pl.multiple_of(i * step_rows, 64)
        lo = i * (SEQ - step_rows)
        bias = jnp.where((keys_i >= lo) & (keys_i < lo + SEQ), 0.0, NEG)
        keep = row_i < lo
        lset[...] = jnp.zeros_like(lset)
        lse_tile = jnp.zeros((win, 128), F32)
        for p in range(d // 128):
            cols = slice(p * 128, p * 128 + 128)
            qp = q_o[pl.ds(off, win), cols]
            kp = k_o[pl.ds(off, win), cols]
            vp = v_o[pl.ds(off, win), cols]
            outs = []
            for h in range(2):
                mine = first if h == 0 else jnp.logical_not(first)
                qm = jnp.where(mine, qp, jnp.zeros_like(qp))
                s = nt(qm, kp) * SCALE2 + bias
                top = jnp.max(s, axis=-1, keepdims=True)
                e = jnp.exp2(s - top)
                den = jnp.sum(e, axis=-1, keepdims=True)
                w = (e * pl.reciprocal(den)).astype(BF)
                outs.append(nn(w, vp))
                lse = top + jnp.log2(den)
                lse_tile = jnp.where(lane == 2 * p + h, lse, lse_tile)
            new = jnp.where(first, outs[0], outs[1]).astype(BF)
            att_o[pl.ds(off, win), cols] = jnp.where(keep, att_o[pl.ds(off, win), cols], new)
        lset[0:win, :] = lse_tile
        lse_o[i] = jnp.transpose(lset[...])[0 : lse_o.shape[1], 0:win]
        return 0

    lax.fori_loop(0, images, image, 0)


def out_fwd_kernel(
    need, flush, banks, tok, g2, att, wo, ao, bo, rwt, ra, rbt, *rest
):
    lo_o, mid_o, n2_o, lr_o, pt_o, tokp = rest[-6:]
    rows, d = tok.shape
    rp = att.shape[0]
    images = rows // SEQ
    width = ao.shape[1]
    half = rp // 2
    tokp[pl.ds(rp - 16, 16), :] = jnp.zeros((16, d), BF)
    tokp[0:rows, :] = tok[...]

    need(att, wo, ao, bo)

    def out_proj(i, _):
        r = pl.multiple_of(i * half, 16)
        x = att[pl.ds(r, half), :]
        mask = bank_mask(banks, r, half, images, width)
        u = (nn(x, ao[...]) * mask).astype(BF)
        lo_o[pl.ds(r, half), :] = u
        mid_o[pl.ds(r, half), :] = (
            tokp[pl.ds(r, half), :].astype(F32) + nn(x, wo[...]) + nn(u, bo[...])
        )
        return 0

    lax.fori_loop(0, 2, out_proj, 0)
    flush(lo_o, mid_o)

    def ln2(i, _):
        r = pl.multiple_of(i * 160, 160)
        xhat, _r = norm_parts(mid_o[pl.ds(r, 160), :])
        n2_o[pl.ds(r, 160), :] = (g2[...] * xhat).astype(BF)
        return 0

    lax.fori_loop(0, rp // 160, ln2, 0)
    need(ra)
    x = n2_o[0:rp, :]
    u = (nn(x, ra[...]) * bank_mask(banks, 0, rp, images, width)).astype(BF)
    lr_o[...] = u
    logits = nt(rwt[...], x) + nt(rbt[...], u)
    e = jnp.exp(logits - jnp.max(logits, axis=0, keepdims=True))
    probs = e / jnp.sum(e, axis=0, keepdims=True)
    pt_o[...] = probs
    store_lines(n2_o, rp, probs, 3)


def attn_forward(banks, tok, g1, ws):
    rows, d = tok.shape
    rp = 32 * (-(-rows // 32))
    images = rows // SEQ
    step_rows = 16 * (SEQ // 16)
    win = rp - step_rows * (images - 1)
    width = ws[1].shape[1]
    heads_pad = 16 * (-(-d // (16 * HEAD_DIM)))
    bfd = jax.ShapeDtypeStruct((rp, d), BF)
    low = jax.ShapeDtypeStruct((rp, width), BF)
    out_shape = (bfd, bfd, bfd, bfd, low, low, low, bfd) + (
        jax.ShapeDtypeStruct((images, heads_pad, win), F32),
    )
    return staged(
        attn_fwd_kernel,
        (banks, tok, g1, *ws),
        "svv" + "m" * 9,
        out_shape,
        [pltpu.VMEM((rp, d), BF), pltpu.VMEM((256, 128), F32)],
        36, 20, "attn_fwd",
    )


def out_forward(banks, tok, g2, att, ws, after):
    rows, d = tok.shape
    rp = att.shape[0]
    low = jax.ShapeDtypeStruct((rp, ws[1].shape[1]), BF)
    out_shape = (
        low,
        jax.ShapeDtypeStruct((rp, d), F32),
        jax.ShapeDtypeStruct((rp + 48, d), BF),
        low,
        jax.ShapeDtypeStruct((ws[3].shape[0], rp), F32),
    )
    return staged(
        out_fwd_kernel,
        (banks, tok, g2, att, *ws, *after),
        "svvmmmmvmv" + "h" * len(after),
        out_shape,
        [pltpu.VMEM((rp, d), BF)],
        24, 7, "out_fwd",
    )


def tables_kernel(eidx, routes, posr_o, posc_o):
    groups, _, rp = routes.shape
    local = posr_o.shape[0] // groups
    row = lax.broadcasted_iota(I32, (rp, rp), 0)
    col = lax.broadcasted_iota(I32, (rp, rp), 1)
    upper = (row < col).astype(BF)
    upper_inc = (row <= col).astype(BF)
    lower = (col < row).astype(BF)
    lower_inc = (col <= row).astype(BF)
    which = lax.broadcasted_iota(I32, (groups * local, rp), 0)
    hot = jnp.zeros((groups * local, rp), F32)
    for s in range(groups):
        r0 = routes[s, 0:1, :]
        r1 = routes[s, 1:2, :]
        for j in range(local):
            e = eidx[0] * local + j
            hit = ((r0 == e) | (r1 == e)).astype(F32)
            hot = jnp.where(which == s * local + j, hit, hot)
    hb = hot.astype(BF)
    before = nn(hb, upper)
    with_own = nn(hb, upper_inc)
    posr_o[...] = jnp.where(with_own > before, before, -1.0)
    before = nt(lower, hb)
    with_own = nt(lower_inc, hb)
    posc_o[...] = jnp.where(with_own > before, before, -1.0)


def routing_tables(eidx, routes, local):
    groups, _, rp = routes.shape
    n = groups * local
    return pl.pallas_call(
        tables_kernel,
        out_shape=(jax.ShapeDtypeStruct((n, rp), F32), jax.ShapeDtypeStruct((rp, n), F32)),
        in_specs=[SMEM, VMEM],
        out_specs=(VMEM, VMEM),
        compiler_params=params(63),
        cost_estimate=cost(2),
        name="routing_tables",
    )(eidx, routes)


def gelu_parts(x):
    e = jnp.exp2((-0.5 * LOG2E) * (x * x))
    t = pl.reciprocal(1.0 + (0.3275911 / math.sqrt(2.0)) * jnp.abs(x))
    poly = 1.061405429 * 0.5
    for c in (-1.453152027, 1.421413741, -0.284496736, 0.254829592):
        poly = poly * t + 0.5 * c
    q = poly * t * e
    phi = jnp.where(x >= 0.0, 1.0 - q, q)
    return x * phi, phi + x * (e * (1.0 / math.sqrt(2.0 * math.pi)))


def slot_count(posr, row):
    n = jnp.sum((posr[row : row + 1, :] >= 0.0).astype(F32)).astype(I32)
    return ((n + 15) // 16) * 16


def expert_kernel(cfg, need, flush, *refs):
    j, sources, has_acc, merge, cap, local, experts = cfg
    last = has_acc
    n = len(sources)
    refs = list(refs)
    take = lambda k: [refs.pop(0) for _ in range(k)]
    (eidx,) = take(1)
    posr, meta = take(2)
    nrows = take(n)
    crows = take(n)
    upw, upa, upb, dnw, dna, dnb = take(6)
    if has_acc:
        (acc_in,) = take(1)
    if merge:
        posc, ret_in, grow_in, gg_in = take(4)
    if last:
        send_o, keep_o = take(2)
    else:
        (acc_b,) = take(1)
    if merge:
        grow_o = take(n)
        mix_o = take(n)
    else:
        ret_b, grow_b, gg_o = take(3)
    up, ua, dn, db, xbuf, cbuf, gate_b, mask_b, gg_b, hid, dgl, sems = take(12)
    (acc,) = take(1)
    if last:
        (acc_b,) = take(1)
    if merge:
        ret_b, grow_b, ret0, grow0 = take(4)
    rp = posr.shape[1]
    d = upw.shape[1]
    ff = upw.shape[2]
    width = upa.shape[2]
    loads = [
        pltpu.make_async_copy(upa.at[j], ua, sems.at[0]),
        pltpu.make_async_copy(upw.at[j], up.at[0:d], sems.at[1]),
        pltpu.make_async_copy(upb.at[j], up.at[d : d + width], sems.at[2]),
        pltpu.make_async_copy(dnw.at[j], dn.at[:, 0:d], sems.at[3]),
        pltpu.make_async_copy(dna.at[j], dn.at[:, d : d + width], sems.at[4]),
        pltpu.make_async_copy(dnb.at[j], db, sems.at[5]),
    ]
    if has_acc:
        loads.append(pltpu.make_async_copy(acc_in, acc_b, sems.at[6]))
    if merge:
        loads.append(pltpu.make_async_copy(ret_in, ret0, sems.at[7]))
        loads.append(pltpu.make_async_copy(grow_in, grow0, sems.at[8]))
    need(nrows[0], crows[0])
    for load in loads:
        load.start(priority=1)
    acc[...] = jnp.zeros_like(acc)
    slot_r = lax.broadcasted_iota(I32, (cap, rp), 0).astype(F32)
    mine = lax.broadcasted_iota(I32, (experts, rp), 0) == eidx[0] * local + j
    col_bank = (lax.broadcasted_iota(I32, (cap, width), 1) // RANK).astype(F32)
    offs = []
    off = jnp.int32(0)
    for i, s in enumerate(sources):
        off = pl.multiple_of(off, 16)
        offs.append(off)
        need(nrows[i], crows[i])
        hit = posr[s * local + j : s * local + j + 1, :] == slot_r
        probs = load_lines(nrows[i][rp : rp + 48, :].astype(F32), rp - d, 3)
        gate_line = jnp.sum(jnp.where(mine, probs, 0.0), axis=0, keepdims=True)
        bank = meta[s, 2:3, :].astype(F32)
        gate = jnp.sum(jnp.where(hit, gate_line, 0.0), axis=1, keepdims=True)
        slot_bank = jnp.sum(jnp.where(hit, bank, 0.0), axis=1, keepdims=True)
        pick = hit.astype(F32).astype(BF)
        xbuf[pl.ds(off, cap), :] = nn(pick, nrows[i][0:rp, :]).astype(BF)
        cbuf[pl.ds(off, cap), :] = nn(pick, crows[i][...]).astype(BF)
        gate_b[pl.ds(off, cap), :] = jnp.broadcast_to(gate, (cap, 128))
        mask_b[pl.ds(off, cap), :] = (col_bank == slot_bank).astype(F32)
        off = off + slot_count(posr, s * local + j)
    total = off
    rest = pl.ds(pl.multiple_of(offs[-1] + cap, 16), cap)
    xbuf[rest, :] = jnp.zeros((cap, d), BF)
    cbuf[rest, :] = jnp.zeros((cap, d), BF)
    gate_b[rest, :] = jnp.zeros((cap, 128), F32)
    mask_b[rest, :] = jnp.zeros((cap, width), F32)
    short = cap // 2
    rem = total % cap
    tiles = total // cap + (rem > short).astype(I32)
    tail = (rem > 0) & (rem <= short)
    chunks = [slice(c, min(c + CHUNK, ff)) for c in range(0, ff, CHUNK)]
    for load in loads:
        load.wait()

    def tile(start, size):
        rs = pl.ds(pl.multiple_of(start, 16), size)
        x = xbuf[rs, :]
        m = mask_b[rs, :]
        u = (nn(x, ua[...]) * m).astype(BF)
        xu = jnp.concatenate([x, u], axis=1)
        out = jnp.zeros((size, d + width), F32)
        for cs in chunks:
            h, dg = gelu_parts(nn(xu, up[:, cs]))
            hb = h.astype(BF)
            hid[0:size, cs] = hb
            dgl[0:size, cs] = dg
            out = out + nn(hb, dn[cs, :])
        ud = (out[:, d:] * m).astype(BF)
        ret = (out[:, :d] + nn(ud, db[...])).astype(BF).astype(F32)
        cot = cbuf[rs, :].astype(F32)
        gate = gate_b[rs, 0:1]
        gg_b[rs, :] = jnp.broadcast_to(jnp.sum(cot * ret, axis=1, keepdims=True), (size, 128))
        ret_b[rs, :] = (gate * ret).astype(BF)
        g = (gate * cot).astype(BF)
        gud = (nt(g, db[...]) * m).astype(BF)
        acc[:, d + 2 * ff :] += tn(ud, g)
        gg = jnp.concatenate([g, gud], axis=1)
        gr = jnp.zeros((size, d + width), F32)
        for cs in chunks:
            gp = (nt(gg, dn[cs, :]) * dgl[0:size, cs]).astype(BF)
            gr = gr + nt(gp, up[:, cs])
            acc[:, d + cs.start : d + cs.stop] += tn(u, gp)
            acc[:, d + ff + cs.start : d + ff + cs.stop] += tn(gud, hid[0:size, cs])
        guu = (gr[:, d:] * m).astype(BF)
        acc[:, 0:d] += tn(guu, x)
        grow_b[rs, :] = (gr[:, :d] + nt(guu, ua[...])).astype(BF)

    def whole(t, _):
        tile(t * cap, cap)
        return 0

    lax.fori_loop(0, tiles, whole, 0)

    @pl.when(tail)
    def _():
        tile(tiles * cap, short)

    done = pl.ds(pl.multiple_of(tiles * cap + tail.astype(I32) * short, 16), cap)
    ret_b[done, :] = jnp.zeros((cap, d), BF)
    grow_b[done, :] = jnp.zeros((cap, d), BF)
    gg_b[done, :] = jnp.zeros((cap, 128), F32)
    if last:
        half = width // 2
        mine_rows = pl.multiple_of(eidx[1] * half, 16)
        peer_rows = pl.multiple_of((1 - eidx[1]) * half, 16)
        for rows, out in ((mine_rows, keep_o), (peer_rows, send_o)):
            both = acc[pl.ds(rows, half), :] + acc_b[pl.ds(rows, half), :].astype(F32)
            out[...] = both.astype(BF)
        flush(send_o, keep_o)
    else:
        acc_b[...] = acc[...].astype(BF)
        flush(acc_b)
    if not merge:
        flush(ret_b, grow_b)
    gg_lines = []
    for i, s in enumerate(sources):
        hit = posr[s * local + j : s * local + j + 1, :] == slot_r
        col = gg_b[pl.ds(offs[i], cap), 0:1]
        gg_lines.append(jnp.sum(jnp.where(hit, col, 0.0), axis=0, keepdims=True))
    if not merge:
        for i in range(n):
            gg_o[i : i + 1, :] = gg_lines[i]
    else:
        slot_c = lax.broadcasted_iota(I32, (rp, cap), 1).astype(F32)
        expert_row = lax.broadcasted_iota(I32, (experts, rp), 0)
        off0 = jnp.int32(0)
        for i, s in enumerate(sources):
            r0 = pl.ds(pl.multiple_of(off0, 16), cap)
            r1 = pl.ds(offs[i], cap)
            p0 = (posc[:, s * local : s * local + 1] == slot_c).astype(F32).astype(BF)
            p1 = (posc[:, s * local + 1 : s * local + 2] == slot_c).astype(F32).astype(BF)
            pick = jnp.concatenate([p0, p1], axis=1)
            for b0, b1, result in ((grow0, grow_b, grow_o[i]), (ret0, ret_b, mix_o[i])):
                both = jnp.concatenate([b0[r0, :], b1[r1, :]], axis=0)
                result[0:rp, :] = nn(pick, both).astype(BF)
            gg = jnp.where(
                expert_row == eidx[0] * local,
                gg_in[i : i + 1, :],
                jnp.where(expert_row == eidx[0] * local + 1, gg_lines[i], 0.0),
            )
            store_lines(grow_o[i], rp, gg, 2)
            flush(grow_o[i], mix_o[i])
            off0 = off0 + slot_count(posr, s * local)


def expert_call(j, sources, eidx, tables, nrows, crows, ws, cap, acc, first=None):
    posr, posc, meta = tables
    rp, d = crows[0].shape
    local, _, ff = ws[0].shape
    width = ws[1].shape[2]
    n = len(sources)
    experts = local * lax.axis_size("expert")
    merge = first is not None
    cfg = (j, tuple(sources), acc is not None, merge, cap, local, experts)
    buf = (n + 1) * cap
    kinds = "svv" + "m" * (2 * n) + "h" * 6
    args = [eidx, posr, meta]
    args += [nrows[s] for s in sources] + [crows[s] for s in sources] + list(ws)
    if acc is not None:
        args.append(acc)
        kinds += "h"
    if merge:
        args += [posc, *first]
        kinds += "vhhv"
    wide = (width, 2 * d + 2 * ff)
    if acc is not None:
        out_shape = (jax.ShapeDtypeStruct((width // 2, wide[1]), BF),) * 2
    else:
        out_shape = (jax.ShapeDtypeStruct(wide, BF),)
    if merge:
        out_shape += (jax.ShapeDtypeStruct((rp + 32, d), BF),) * n
        out_shape += (jax.ShapeDtypeStruct((rp, d), BF),) * n
    else:
        out_shape += (jax.ShapeDtypeStruct((buf, d), BF),) * 2
        out_shape += (jax.ShapeDtypeStruct((n, rp), F32),)
    scratch = [
        pltpu.VMEM((d + width, ff), BF),
        pltpu.VMEM((d, width), BF),
        pltpu.VMEM((ff, d + width), BF),
        pltpu.VMEM((width, d), BF),
        pltpu.VMEM((buf, d), BF),
        pltpu.VMEM((buf, d), BF),
        pltpu.VMEM((buf, 128), F32),
        pltpu.VMEM((buf, width), F32),
        pltpu.VMEM((buf, 128), F32),
        pltpu.VMEM((cap, ff), BF),
        pltpu.VMEM((cap, ff), F32),
        pltpu.SemaphoreType.DMA((9,)),
    ]
    scratch.append(pltpu.VMEM(wide, F32))
    if acc is not None:
        scratch.append(pltpu.VMEM(wide, BF))
    if merge:
        scratch += [pltpu.VMEM((buf, d), BF)] * 4
    return staged(
        functools.partial(expert_kernel, cfg),
        args,
        kinds,
        out_shape,
        scratch,
        60, 30, f"expert{j}_{'far' if sources[0] else 'near'}",
    )


def out_bwd_kernel(
    need, flush, banks, p0, p1, p2, lr, n2, ra, mid, cot, lo, bo, att, wo, ao, g2, pt, rwt, rbt,
    gmid, ga, gr_o,
    gml,
):
    rp, d = cot.shape
    experts = pt.shape[0]
    images = banks.shape[0]
    width = ao.shape[1]
    need(p0, p1, p2)
    probs = pt[...]
    lines = sum(p[rp : rp + 32, :].astype(F32) for p in (p0, p1, p2))
    gp = load_lines(lines, rp - d, 2)
    glt = (probs * (gp - jnp.sum(gp * probs, axis=0, keepdims=True))).astype(BF)
    need(lr)
    rb = jnp.concatenate([nn(glt, lr[...]), jnp.zeros((experts, d - width), F32)], axis=1)
    rb = jnp.concatenate([rb, jnp.zeros((32 - experts, d), F32)], axis=0)
    gr_o[3 * width : 3 * width + 32, :] = rb.astype(BF)
    mask = bank_mask(banks, 0, rp, images, width)
    gu = (tn(glt, rbt[...]) * mask).astype(BF)
    need(n2, ra)
    gr_o[2 * width : 3 * width, :] = tn(gu, n2[0:rp, :]).astype(BF)
    gmid[...] = tn(glt, rwt[...]) + nt(gu, ra[...])

    need(mid, cot)

    def ln2(i, _):
        rs = pl.ds(pl.multiple_of(i * 160, 160), 160)
        grad = gmid[rs, :] + (p0[rs, :].astype(F32) + p1[rs, :].astype(F32) + p2[rs, :].astype(F32))
        xhat, rstd = norm_parts(mid[rs, :])
        g = cot[rs, :].astype(F32) + norm_back(xhat, rstd, g2[...], grad)
        gmid[rs, :] = g
        gml[rs, :] = g.astype(BF)
        return 0

    lax.fori_loop(0, rp // 160, ln2, 0)
    flush(gmid)
    need(lo, bo, att, wo, ao)
    g = gml[...]
    gr_o[width : 2 * width, :] = tn(lo[...], g).astype(BF)
    gu = (nt(g, bo[...]) * mask).astype(BF)
    gr_o[0:width, :] = tn(gu, att[...]).astype(BF)
    ga[...] = (nt(g, wo[...]) + nt(gu, ao[...])).astype(BF)


def out_backward(banks, cot, g2, kept, ws, parts):
    rp, d = cot.shape
    width = ws[1].shape[1]
    wo, ao, bo, rwt, ra, rbt = ws
    att, lo, mid, n2, lr, pt = kept
    return staged(
        out_bwd_kernel,
        (banks, *parts, lr, n2, ra, mid, cot, lo, bo, att, wo, ao, g2, pt, rwt, rbt),
        "s" + "m" * 13 + "vvvv",
        (
            jax.ShapeDtypeStruct((rp, d), F32),
            jax.ShapeDtypeStruct((rp, d), BF),
            jax.ShapeDtypeStruct((3 * width + 32, d), BF),
        ),
        [pltpu.VMEM((rp, d), BF)],
        36, 12, "out_bwd",
    )


def attn_bwd_kernel(
    need, flush, banks, core, q, k, v, ga, lq, bq, n1, lk, bk, lv, bv, outr, lse,
    gq, gk, gv, uq, uk, uv, send_o, keep_o,
    gr_o,
):
    rp, d = n1.shape
    images = banks.shape[0]
    width = bq.shape[0]
    win = lse.shape[2]
    step_rows = 16 * (SEQ // 16)
    lane = lax.broadcasted_iota(I32, (win, 128), 1)
    first = lane < HEAD_DIM
    row_i = lax.broadcasted_iota(I32, (win, 128), 0)
    key_i = lax.broadcasted_iota(I32, (win, win), 0)
    query_i = lax.broadcasted_iota(I32, (win, win), 1)

    need(q, k, v, ga)

    def image(i, _):
        off = pl.multiple_of(i * step_rows, 64)
        start = i * (SEQ - step_rows)
        bias = jnp.where(
            (key_i >= start) & (key_i < start + SEQ) & (query_i >= start) & (query_i < start + SEQ),
            0.0,
            NEG,
        )
        keep = row_i < start
        ws = pl.ds(off, win)
        for p in range(d // 128):
            cols = slice(p * 128, p * 128 + 128)
            qp = q[ws, cols]
            kp = k[ws, cols]
            vp = v[ws, cols]
            gap = ga[ws, cols]
            rq, rk, rv = [], [], []
            for h in range(2):
                mine = first if h == 0 else jnp.logical_not(first)
                km = jnp.where(mine, kp, jnp.zeros_like(kp))
                vm = jnp.where(mine, vp, jnp.zeros_like(vp))
                prob = jnp.exp2(
                    nt(km, qp) * SCALE2 + bias - lse[i, 2 * p + h : 2 * p + h + 1, :]
                )
                gw = nt(vm, gap)
                delta = jnp.sum(gw * prob, axis=0, keepdims=True)
                gs = (prob * (gw - delta)).astype(BF)
                rv.append(nn(prob.astype(BF), gap))
                rk.append(nn(gs, qp))
                rq.append(tn(gs, kp))
            for parts, ref, scale in ((rq, gq, 0.125), (rk, gk, 0.125), (rv, gv, 1.0)):
                new = (jnp.where(first, parts[0], parts[1]) * scale).astype(BF)
                ref[ws, cols] = jnp.where(keep, ref[ws, cols], new)
        return 0

    lax.fori_loop(0, images, image, 0)
    flush(gq, gk, gv)
    need(n1, lq, lk, lv, bq, bk, bv)
    x = n1[...]
    mask = bank_mask(banks, 0, rp, images, width)
    for i, (grad, low, b, u) in enumerate(((gq, lq, bq, uq), (gk, lk, bk, uk), (gv, lv, bv, uv))):
        g = grad[...]
        gr_o[(2 * i + 1) * width : (2 * i + 2) * width, :] = tn(low[...], g).astype(BF)
        gu = (nt(g, b[...]) * mask).astype(BF)
        u[...] = gu
        gr_o[2 * i * width : (2 * i + 1) * width, :] = tn(gu, x).astype(BF)
    used = 6 * width + outr.shape[0]
    need(outr)
    gr_o[6 * width : used, :] = outr[...]
    if gr_o.shape[0] > used:
        gr_o[used:, :] = jnp.zeros((gr_o.shape[0] - used, d), BF)
    half = send_o.shape[0]
    keep_o[...] = gr_o[pl.ds(pl.multiple_of(core[0] * half, 16), half), :]
    send_o[...] = gr_o[pl.ds(pl.multiple_of((1 - core[0]) * half, 16), half), :]
    flush(send_o, keep_o)


def attn_backward(banks, core, kept, ga, bs, outr, shares):
    rp, d = ga.shape
    width = bs[0].shape[0]
    bfd = jax.ShapeDtypeStruct((rp, d), BF)
    low = jax.ShapeDtypeStruct((rp, width), BF)
    n1, q, k, v, lq, lk, lv, lse = kept
    bq, bk, bv = bs
    total = -(-(6 * width + outr.shape[0]) // (32 * shares)) * 32 * shares
    half = jax.ShapeDtypeStruct((total // 2, d), BF)
    return staged(
        attn_bwd_kernel,
        (banks, core, q, k, v, ga, lq, bq, n1, lk, bk, lv, bv, outr, lse),
        "ss" + "m" * 12 + "v",
        (bfd, bfd, bfd, low, low, low, half, half),
        [pltpu.VMEM((total, d), BF)],
        34, 20, "attn_bwd",
    )


def input_bwd_kernel(
    need, flush, tok, g1, gq, wq, uq, aq, gk, wk, uk, ak, gv, wv, uv, av, gmid, inp_o, total
):
    rows, d = tok.shape
    need(gq, wq, uq, aq)
    first = nt(gq[...], wq[...]) + nt(uq[...], aq[...])
    need(gk, wk, uk, ak)
    first = first + (nt(gk[...], wk[...]) + nt(uk[...], ak[...]))
    need(gv, wv, uv, av)
    total[...] = first + (nt(gv[...], wv[...]) + nt(uv[...], av[...]))
    need(gmid)
    whole = rows // 16 * 16
    for r, count in [(s, min(112, whole - s)) for s in range(0, whole, 112)] + (
        [(whole, rows - whole)] if rows > whole else []
    ):
        rs = slice(r, r + count)
        xhat, rstd = norm_parts(tok[rs, :].astype(F32))
        inp_o[rs, :] = gmid[rs, :] + norm_back(xhat, rstd, g1[...], total[rs, :])


def input_backward(tok, g1, gmid, grads, ws):
    rows, d = tok.shape
    gq, gk, gv, uq, uk, uv = grads
    wq, wk, wv, aq, ak, av = ws
    return staged(
        input_bwd_kernel,
        (tok, g1, gq, wq, uq, aq, gk, wk, uk, ak, gv, wv, uv, av, gmid),
        "vv" + "m" * 13,
        (jax.ShapeDtypeStruct((rows, d), F32),),
        [pltpu.VMEM(gmid.shape, F32)],
        34, 7, "input_bwd",
    )[0]


def join(bit, own, other, out, low, high):
    half = own.shape[0]
    out[0:half, low:high] = jnp.where(bit == 0, own[:, low:high], other[:, low:high])
    out[half : 2 * half, low:high] = jnp.where(bit == 0, other[:, low:high], own[:, low:high])


def finish_kernel(need, flush, bit, own, other, *rest):
    outs, flat = rest[:-1], rest[-1]
    width, d = outs[1].shape
    experts = outs[9].shape[0]
    need(own, other)
    join(bit[0], own, other, flat, 0, d)
    for i in range(5):
        base = 2 * i * width
        outs[2 * i][...] = jnp.transpose(flat[base : base + width, :].astype(F32))
        flush(outs[2 * i])
        if i < 4:
            outs[2 * i + 1][...] = flat[base + width : base + 2 * width, :].astype(F32)
            flush(outs[2 * i + 1])
    outs[9][...] = flat[9 * width : 9 * width + 16, 0:width].astype(F32)[0:experts]


def finish(bit, own, other, width, experts):
    d = own.shape[1]
    tall = jax.ShapeDtypeStruct((d, width), F32)
    wide = jax.ShapeDtypeStruct((width, d), F32)
    return staged(
        finish_kernel,
        (bit, own, other),
        "smm" if own.shape[0] % 16 == 0 else "svv",
        (tall, wide) * 4 + (tall, jax.ShapeDtypeStruct((experts, width), F32)),
        [pltpu.VMEM((2 * own.shape[0], d), BF)],
        16, 2, "finish",
    )


def finish_expert_kernel(cfg, need, flush, bit, own, other, *rest):
    j, aliased = cfg
    ua_o, ub_o, da_o, db_o, ua, ub, da, db, both, sems = rest[4:] if aliased else rest
    d, width = ua.shape
    ff = ub.shape[1]
    need(own, other)
    copies = []

    def put(n, src, out):
        copies.append(pltpu.make_async_copy(src, out.at[j], sems.at[n]))
        copies[-1].start()

    join(bit[0], own, other, both, d + ff, d + 2 * ff)
    da[...] = jnp.transpose(both[:, d + ff : d + 2 * ff].astype(F32))
    put(0, da, da_o)
    join(bit[0], own, other, both, d, d + ff)
    ub[...] = both[:, d : d + ff].astype(F32)
    put(1, ub, ub_o)
    join(bit[0], own, other, both, 0, d)
    ua[...] = jnp.transpose(both[:, 0:d].astype(F32))
    put(2, ua, ua_o)
    join(bit[0], own, other, both, d + 2 * ff, 2 * d + 2 * ff)
    db[...] = both[:, d + 2 * ff :].astype(F32)
    put(3, db, db_o)
    for copy in copies:
        copy.wait()


def finish_expert(j, n, bit, own, other, d, earlier=()):
    half, wide = own.shape
    width = 2 * half
    ff = wide // 2 - d
    shapes = ((d, width), (width, ff), (ff, width), (width, d))
    args = (bit, own, other, *earlier)
    return staged(
        functools.partial(finish_expert_kernel, (j, bool(earlier))),
        args,
        "smm" + "h" * len(earlier),
        tuple(jax.ShapeDtypeStruct((n,) + x, F32) for x in shapes),
        [pltpu.VMEM(x, F32) for x in shapes]
        + [pltpu.VMEM((width, wide), BF), pltpu.SemaphoreType.DMA((4,))],
        24, 3, f"finish_expert{j}",
        direct=True,
        aliases={3 + i: i for i in range(len(earlier))},
    )


def hop(x, axis, k):
    n = lax.axis_size(axis)
    return lax.ppermute(x, axis, [(i, i ^ k) for i in range(n)])


def bits(axis):
    n = lax.axis_size(axis)
    return [1 << i for i in range(n.bit_length() - 1)]


def add(a, b):
    return (a.astype(F32) + b.astype(F32)).astype(BF)


def part_of(terms, bit, flip):
    half = terms[0].shape[0] // 2
    start = (bit if not flip else 1 - bit) * half
    return sum(lax.dynamic_slice_in_dim(t, start, half, 0).astype(F32) for t in terms).astype(BF)


def reduce_step(terms, axis, k):
    bit = (lax.axis_index(axis) // k) % 2
    send = part_of(terms, bit, True)
    return send, part_of(terms, bit, False), hop(send, axis, k)


def gather_step(buf, axis, k, wait=None):
    bit = (lax.axis_index(axis) // k) % 2
    other = hop(buf, axis, k)
    if wait is not None:
        other = after(other, *(wait if isinstance(wait, tuple) else (wait,)))
    return jnp.where(
        bit == 0,
        jnp.concatenate([buf, other], axis=0),
        jnp.concatenate([other, buf], axis=0),
    )


def after(x, *deps):
    return lax.optimization_barrier((x,) + deps)[0]


def gather4(x):
    near = hop(x, "expert", 1)
    far = hop(x, "expert", 2)
    return [x, near, far, hop(far, "expert", 1)]


def body(
    tokens, cotangent, bank_ids, routes, attn_gain, expert_gain, query_w, key_w, value_w, out_w,
    query_a, query_b, key_a, key_b, value_a, value_b, out_a, out_b, router_w, router_a, router_b,
    up_w, up_a, up_b, down_w, down_a, down_b,
):
    rows, d = tokens.shape
    rp = 32 * (-(-rows // 32))
    width = query_a.shape[1]
    local = up_w.shape[0]
    groups = lax.axis_size("expert")
    experts = local * groups
    cap = 13 * rows // (4 * experts)
    me = jnp.stack([lax.axis_index("expert"), lax.axis_index("dp") % 2]).astype(I32)
    cot = jnp.pad(cotangent, ((0, rp - rows), (0, 0)))
    cot1 = hop(cot, "expert", 1)
    cot2 = hop(cot, "expert", 2)
    meta = jnp.concatenate([routes.T, jnp.repeat(bank_ids, SEQ)[None, :]], axis=0)
    meta = jnp.pad(meta, ((0, 0), (0, rp - rows)), constant_values=-1)
    meta = jnp.stack(gather4(meta))
    g1 = attn_gain.reshape(1, d)
    g2 = expert_gain.reshape(1, d)
    kept = attn_forward(
        bank_ids, tokens, g1,
        (query_w, query_a, query_b, key_w, key_a, key_b, value_w, value_a, value_b),
    )
    n1, q, k, v, lq, lk, lv, att, lse = kept
    out_ws = (out_w, out_a, out_b, router_w.T, router_a, router_b.T)
    lo, mid, n2, lr, pt = out_forward(
        bank_ids, tokens, g2, after(att, meta), out_ws, (cot1,)
    )
    near1 = hop(n2, "expert", 1)
    far2 = hop(after(n2, cot2), "expert", 2)
    cot3 = hop(after(cot2, n2), "expert", 1)
    tables = routing_tables(me, after(meta, n2), local) + (meta,)
    crows = [cot, cot1, cot2, cot3]
    ews = (up_w, up_a, up_b, down_w, down_a, down_b)
    common = (crows, ews, cap)
    nrows = [n2, near1, None, None]
    e0n = expert_call(0, (0, 1), after(me, cot3), tables, nrows, *common, None)
    far2 = after(far2, e0n[1])
    nrows = [n2, near1, far2, hop(far2, "expert", 1)]
    e0f = expert_call(0, (2, 3), me, tables, nrows, *common, e0n[0])
    dp_steps = [("dp", k) for k in bits("dp")]
    ex_steps = [("expert", k) for k in bits("expert")]
    got0 = hop(e0f[0], *dp_steps[0])
    keep0 = e0f[1]
    e1f = expert_call(
        1, (2, 3), after(me, keep0), tables, nrows, *common, None, e0f[2:]
    )
    grow = add(e1f[1], hop(e1f[2], "expert", 1))
    mix = add(e1f[3], hop(e1f[4], "expert", 1))
    send0, keep0, got0 = reduce_step([keep0, after(got0, e1f[1])], *dp_steps[1])
    e1n = expert_call(
        1, (0, 1), after(me, grow, send0, mix), tables, nrows, *common, e1f[0], e0n[1:]
    )
    send1, keep1, *near = e1n
    grow_far = hop(grow, "expert", 2)
    grow_near = hop(after(near[1], grow_far), "expert", 1)
    mix_far = hop(after(mix, near[0]), "expert", 2)
    send0, keep0, got0 = reduce_step([keep0, after(got0, near[0])], *dp_steps[2])
    got1 = hop(after(send1, near[0]), *dp_steps[0])
    gmid, ga, outr = out_backward(
        bank_ids, cot, g2, (att, lo, mid, n2, lr, pt), out_ws,
        (near[0], after(grow_near, send0), grow_far),
    )
    got0 = after(got0, gmid)
    for step in dp_steps[3:]:
        _, keep0, got0 = reduce_step([keep0, got0], *step)
    buf0 = add(keep0, got0)
    send1, keep1, got1 = reduce_step([keep1, after(got1, gmid)], *dp_steps[1])
    core = lax.axis_index("expert").astype(I32).reshape(1) % 2
    shares = lax.axis_size("dp") * groups // 32
    *grads, qkv, keep = attn_backward(
        bank_ids, core, (n1, q, k, v, lq, lk, lv, lse), after(ga, buf0, send1),
        (query_b, key_b, value_b), outr, shares,
    )
    up_steps = dp_steps[::-1]
    bit = me[1:]
    buf0 = gather_step(buf0, *up_steps[0], wait=qkv)
    qkv = after(qkv, mix_far)
    mix_near = hop(after(near[3], qkv), "expert", 1)
    send1, keep1, got1 = reduce_step([keep1, after(got1, qkv)], *dp_steps[2])
    got = hop(after(qkv, buf0, send1), *ex_steps[0])
    send, keep, got = reduce_step([keep, got], *ex_steps[1])
    input_grad = input_backward(
        tokens, g1, after(gmid, send), grads,
        (query_w, key_w, value_w, query_a, key_a, value_a),
    )
    got = after(got, input_grad)
    for step in dp_steps[3:]:
        _, keep1, got1 = reduce_step([keep1, got1], *step)
    buf1 = add(keep1, after(got1, input_grad))
    for step in up_steps[1:-1]:
        buf0 = gather_step(buf0, *step, wait=input_grad)
    for step in ex_steps[2:]:
        _, keep, got = reduce_step([keep, got], *step)
    send, keep, got = reduce_step([keep, after(got, buf0, buf1)], *dp_steps[0])
    peer0 = hop(after(buf0, send), *up_steps[-1])
    buf1 = gather_step(buf1, *up_steps[0])
    for step in dp_steps[1:-1]:
        _, keep, got = reduce_step([keep, got], *step)
    _, keep, got = reduce_step([keep, after(got, buf1)], *dp_steps[-1])
    for step in up_steps[1:-1]:
        buf1 = gather_step(buf1, *step)
    flat = after(add(keep, got), peer0)
    flat = gather_step(flat, *up_steps[0])
    for step in up_steps[1:-1]:
        flat = gather_step(after(flat, buf1), *step)
    peer1 = hop(buf1, *up_steps[-1])
    flat = gather_step(flat, *up_steps[-1])
    for step in reversed(ex_steps[2:]):
        flat = gather_step(flat, *step)
    mixed = mid[:rows] + (
        near[2][:rows].astype(F32) + mix_near[:rows].astype(F32) + mix_far[:rows].astype(F32)
    )
    mixed = mixed.astype(BF)
    large = finish_expert(0, local, bit, buf0, peer0, d)
    flat = gather_step(flat, *ex_steps[1], wait=(mixed, large[0]))
    peer = hop(after(flat, peer1), *ex_steps[0])
    large = finish_expert(1, local, bit, buf1, peer1, d, large)
    small = finish(
        core, flat, after(peer, large[0]), width, experts,
    )
    return (mixed, input_grad, *small[:9], small[9].T, *large)


def solution(mesh):
    split = P(("dp", "expert"), None)
    by_expert = P("expert", None, None)
    in_specs = (split, split, P(("dp", "expert")), split) + (P(),) * 17 + (by_expert,) * 6
    out_specs = (split, split) + (P(),) * 10 + (by_expert,) * 4
    return jax.shard_map(body, mesh=mesh, in_specs=in_specs, out_specs=out_specs, check_vma=False)
```

```python
import functools
import math

import jax
import jax.numpy as jnp
from jax import lax
from jax.experimental import pallas as pl
from jax.experimental.pallas import tpu as pltpu
from jax.sharding import PartitionSpec as P

HEAD_DIM = 64
RANK = 16
SEQ = 197
EPS = 1e-06
BF = jnp.bfloat16
F32 = jnp.float32
I32 = jnp.int32
LOG2E = math.log2(math.e)
SCALE2 = HEAD_DIM ** (-0.5) * LOG2E
NEG = -1e30
CHUNK = 1536
VMEM = pl.BlockSpec(memory_space=pltpu.VMEM)
SMEM = pl.BlockSpec(memory_space=pltpu.SMEM)
HBM = pl.BlockSpec(memory_space=pltpu.HBM)


def nn(a, b):
    return jnp.dot(a, b, preferred_element_type=F32)


def nt(a, b):
    return lax.dot_general(a, b, (((1,), (1,)), ((), ())), preferred_element_type=F32)


def tn(a, b):
    return lax.dot_general(a, b, (((0,), (0,)), ((), ())), preferred_element_type=F32)


def params(mib):
    return pltpu.CompilerParams(vmem_limit_bytes=mib * 1024 * 1024)


def cost(us):
    return pl.CostEstimate(
        flops=int(us * 1.1e9), bytes_accessed=int(us * 3e6), transcendentals=0
    )


def staged(kernel, args, kinds, outs, scratch, mib, us, name, direct=False, aliases=None):
    specs = {"s": SMEM, "v": VMEM, "h": HBM, "m": HBM}
    moved = [i for i, k in enumerate(kinds) if k == "m"]
    large = [] if direct else [
        i
        for i, o in enumerate(outs)
        if math.prod(o.shape) >= 1 << 15 and (o.dtype == F32 or o.shape[-2] % 16 == 0)
    ]
    n_in, n_out = len(args), len(outs)
    copies = len(moved) + len(large)

    def run(*refs):
        ins, results = list(refs[:n_in]), list(refs[n_in : n_in + n_out])
        own = refs[n_in + n_out : n_in + n_out + len(scratch)]
        buffers = refs[n_in + n_out + len(scratch) : -1]
        sems = refs[-1]
        arriving, leaving = [], []
        for n, i in enumerate(moved):
            copy = pltpu.make_async_copy(ins[i], buffers[n], sems.at[n])
            copy.start(priority=1)
            arriving.append([buffers[n], copy, False])
            ins[i] = buffers[n]
        for n, i in enumerate(large, len(moved)):
            copy = pltpu.make_async_copy(buffers[n], results[i], sems.at[n])
            leaving.append([buffers[n], copy, False])
            results[i] = buffers[n]

        def need(*wanted):
            for entry in arriving:
                if not entry[2] and any(entry[0] is ref for ref in wanted):
                    entry[1].wait()
                    entry[2] = True

        def flush(*ready):
            for entry in leaving:
                if not entry[2] and any(entry[0] is ref for ref in ready):
                    entry[1].start()
                    entry[2] = True

        kernel(need, flush, *ins, *results, *own)
        need(*[entry[0] for entry in arriving])
        flush(*[entry[0] for entry in leaving])
        for entry in leaving:
            entry[1].wait()

    return pl.pallas_call(
        run,
        out_shape=tuple(outs),
        in_specs=[specs[k] for k in kinds],
        out_specs=tuple(HBM if direct or i in large else VMEM for i in range(n_out)),
        input_output_aliases=aliases or {},
        scratch_shapes=list(scratch)
        + [pltpu.VMEM(args[i].shape, args[i].dtype) for i in moved]
        + [pltpu.VMEM(outs[i].shape, outs[i].dtype) for i in large]
        + [pltpu.SemaphoreType.DMA((max(copies, 1),))],
        compiler_params=params(60 if mib == 60 else 63),
        cost_estimate=cost(us),
        name=name,
    )(*args)


def split_parts(x, n):
    parts = []
    for _ in range(n):
        low = x.astype(BF)
        parts.append(low)
        x = x - low.astype(F32)
    return parts


def store_lines(ref, start, lines, n):
    d = ref.shape[1]
    for i, part in enumerate(split_parts(lines, n)):
        part = part.astype(F32)
        rest = part.shape[1] - d
        tail = jnp.concatenate(
            [part[:, d:], jnp.zeros((part.shape[0], d - rest), F32)], axis=1
        )
        ref[start + 16 * i : start + 16 * i + 16, :] = jnp.concatenate(
            [part[:, :d], tail], axis=0
        ).astype(BF)


def load_lines(block, rest, n):
    total = sum(block[16 * i : 16 * i + 16, :] for i in range(n))
    return jnp.concatenate([total[:8], total[8:, :rest]], axis=1)


def image_banks(banks, row, images):
    bank = jnp.full(row.shape, banks[0], I32)
    for i in range(1, images):
        bank = jnp.where(row >= SEQ * i, banks[i], bank)
    return bank


def bank_mask(banks, start, count, images, width):
    row = lax.broadcasted_iota(I32, (count, width), 0) + start
    col = lax.broadcasted_iota(I32, (count, width), 1)
    return (col // RANK == image_banks(banks, row, images)).astype(F32)


def norm_parts(x):
    mean = jnp.mean(x, axis=-1, keepdims=True)
    cen = x - mean
    rstd = lax.rsqrt(jnp.mean(cen * cen, axis=-1, keepdims=True) + EPS)
    return cen * rstd, rstd


def norm_back(xhat, rstd, gain, grad):
    gy = grad * gain
    return rstd * (
        gy
        - jnp.mean(gy, axis=-1, keepdims=True)
        - xhat * jnp.mean(gy * xhat, axis=-1, keepdims=True)
    )


def attn_fwd_kernel(
    need, flush, banks, tok, g1, wq, aq, bq, wk, ak, bk, wv, av, bv,
    n1_o, q_o, k_o, v_o, lq_o, lk_o, lv_o, att_o, lse_o, tokp,
    lset,
):
    rows = tok.shape[0]
    rp = n1_o.shape[0]
    images = rows // SEQ
    d = tok.shape[1]
    width = aq.shape[1]
    win = lse_o.shape[2]
    step_rows = 16 * (SEQ // 16)
    tokp[pl.ds(rp - 16, 16), :] = jnp.zeros((16, d), BF)
    tokp[0:rows, :] = tok[...]
    flush(tokp)
    need(g1)

    def ln1(i, _):
        r = pl.multiple_of(i * 160, 160)
        xhat, _r = norm_parts(tokp[pl.ds(r, 160), :].astype(F32))
        n1_o[pl.ds(r, 160), :] = (g1[...] * xhat).astype(BF)
        return 0

    lax.fori_loop(0, rp // 160, ln1, 0)
    flush(n1_o)
    half = rp // 2
    for w, a, b, out, low in (
        (wq, aq, bq, q_o, lq_o),
        (wk, ak, bk, k_o, lk_o),
        (wv, av, bv, v_o, lv_o),
    ):
        need(w, a, b)
        for r in (0, half):
            x = n1_o[r : r + half, :]
            mask = bank_mask(banks, r, half, images, width)
            u = (nn(x, a[...]) * mask).astype(BF)
            low[r : r + half, :] = u
            out[r : r + half, :] = (nn(x, w[...]) + nn(u, b[...])).astype(BF)
        flush(out, low)

    lane = lax.broadcasted_iota(I32, (win, 128), 1)
    first = lane < HEAD_DIM
    row_i = lax.broadcasted_iota(I32, (win, 128), 0)
    keys_i = lax.broadcasted_iota(I32, (win, win), 1)

    def image(i, _):
        off = pl.multiple_of(i * step_rows, 64)
        lo = i * (SEQ - step_rows)
        bias = jnp.where((keys_i >= lo) & (keys_i < lo + SEQ), 0.0, NEG)
        keep = row_i < lo
        lset[...] = jnp.zeros_like(lset)
        lse_tile = jnp.zeros((win, 128), F32)
        for p in range(d // 128):
            cols = slice(p * 128, p * 128 + 128)
            qp = q_o[pl.ds(off, win), cols]
            kp = k_o[pl.ds(off, win), cols]
            vp = v_o[pl.ds(off, win), cols]
            outs = []
            for h in range(2):
                mine = first if h == 0 else jnp.logical_not(first)
                qm = jnp.where(mine, qp, jnp.zeros_like(qp))
                s = nt(qm, kp) * SCALE2 + bias
                top = jnp.max(s, axis=-1, keepdims=True)
                e = jnp.exp2(s - top)
                den = jnp.sum(e, axis=-1, keepdims=True)
                w = (e * pl.reciprocal(den)).astype(BF)
                outs.append(nn(w, vp))
                lse = top + jnp.log2(den)
                lse_tile = jnp.where(lane == 2 * p + h, lse, lse_tile)
            new = jnp.where(first, outs[0], outs[1]).astype(BF)
            att_o[pl.ds(off, win), cols] = jnp.where(keep, att_o[pl.ds(off, win), cols], new)
        lset[0:win, :] = lse_tile
        lse_o[i] = jnp.transpose(lset[...])[0 : lse_o.shape[1], 0:win]
        return 0

    lax.fori_loop(0, images, image, 0)


def out_fwd_kernel(
    need, flush, banks, att, ao, bo, wo, tokp, g2, ra, rwt, rbt, *rest
):
    lo_o, mid_o, n2_o, lr_o, pt_o = rest[-5:]
    rp, d = tokp.shape
    images = banks.shape[0]
    width = ao.shape[1]
    half = rp // 2
    need(att, wo, ao, bo, tokp, g2)

    def out_proj(i, _):
        r = pl.multiple_of(i * half, 16)
        x = att[pl.ds(r, half), :]
        mask = bank_mask(banks, r, half, images, width)
        u = (nn(x, ao[...]) * mask).astype(BF)
        lo_o[pl.ds(r, half), :] = u
        mid_o[pl.ds(r, half), :] = (
            tokp[pl.ds(r, half), :].astype(F32) + nn(x, wo[...]) + nn(u, bo[...])
        )
        return 0

    lax.fori_loop(0, 2, out_proj, 0)
    flush(lo_o, mid_o)

    def ln2(i, _):
        r = pl.multiple_of(i * 160, 160)
        xhat, _r = norm_parts(mid_o[pl.ds(r, 160), :])
        n2_o[pl.ds(r, 160), :] = (g2[...] * xhat).astype(BF)
        return 0

    lax.fori_loop(0, rp // 160, ln2, 0)
    need(ra, rwt, rbt)
    x = n2_o[0:rp, :]
    u = (nn(x, ra[...]) * bank_mask(banks, 0, rp, images, width)).astype(BF)
    lr_o[...] = u
    logits = nt(rwt[...].astype(BF), x) + nt(rbt[...].astype(BF), u)
    e = jnp.exp(logits - jnp.max(logits, axis=0, keepdims=True))
    probs = e / jnp.sum(e, axis=0, keepdims=True)
    pt_o[...] = probs
    store_lines(n2_o, rp, probs, 3)


def attn_forward(banks, tok, g1, ws):
    rows, d = tok.shape
    rp = 32 * (-(-rows // 32))
    images = rows // SEQ
    step_rows = 16 * (SEQ // 16)
    win = rp - step_rows * (images - 1)
    width = ws[1].shape[1]
    heads_pad = 16 * (-(-d // (16 * HEAD_DIM)))
    bfd = jax.ShapeDtypeStruct((rp, d), BF)
    low = jax.ShapeDtypeStruct((rp, width), BF)
    out_shape = (bfd, bfd, bfd, bfd, low, low, low, bfd) + (
        jax.ShapeDtypeStruct((images, heads_pad, win), F32),
        bfd,
    )
    return staged(
        attn_fwd_kernel,
        (banks, tok, g1, *ws),
        "svm" + "m" * 9,
        out_shape,
        [pltpu.VMEM((256, 128), F32)],
        36, 20, "attn_fwd",
    )


def out_forward(banks, tokp, g2, att, ws, after):
    rp, d = tokp.shape
    low = jax.ShapeDtypeStruct((rp, ws[1].shape[1]), BF)
    out_shape = (
        low,
        jax.ShapeDtypeStruct((rp, d), F32),
        jax.ShapeDtypeStruct((rp + 48, d), BF),
        low,
        jax.ShapeDtypeStruct((ws[3].shape[0], rp), F32),
    )
    return staged(
        out_fwd_kernel,
        (banks, att, ws[1], ws[2], ws[0], tokp, g2, ws[4], ws[3], ws[5], *after),
        "s" + "m" * 9 + "h" * len(after),
        out_shape,
        [],
        24, 7, "out_fwd",
    )


def tables_kernel(need, flush, eidx, routes, posr_o, posc_o):
    groups, _, rp = routes.shape
    local = posr_o.shape[0] // groups
    need(routes)
    row = lax.broadcasted_iota(I32, (rp, rp), 0)
    col = lax.broadcasted_iota(I32, (rp, rp), 1)
    upper = (row < col).astype(BF)
    upper_inc = (row <= col).astype(BF)
    lower = (col < row).astype(BF)
    lower_inc = (col <= row).astype(BF)
    which = lax.broadcasted_iota(I32, (groups * local, rp), 0)
    hot = jnp.zeros((groups * local, rp), F32)
    for s in range(groups):
        r0 = routes[s, 0:1, :]
        r1 = routes[s, 1:2, :]
        for j in range(local):
            e = eidx[0] * local + j
            hit = ((r0 == e) | (r1 == e)).astype(F32)
            hot = jnp.where(which == s * local + j, hit, hot)
    hb = hot.astype(BF)
    before = nn(hb, upper)
    with_own = nn(hb, upper_inc)
    posr_o[...] = jnp.where(with_own > before, before, -1.0)
    before = nt(lower, hb)
    with_own = nt(lower_inc, hb)
    posc_o[...] = jnp.where(with_own > before, before, -1.0)


def routing_tables(eidx, routes, local):
    groups, _, rp = routes.shape
    n = groups * local
    return staged(
        tables_kernel,
        (eidx, routes),
        "sm",
        (jax.ShapeDtypeStruct((n, rp), F32), jax.ShapeDtypeStruct((rp, n), F32)),
        [],
        16, 2, "routing_tables",
    )


def gelu_parts(x):
    e = jnp.exp2((-0.5 * LOG2E) * (x * x))
    t = pl.reciprocal(1.0 + (0.3275911 / math.sqrt(2.0)) * jnp.abs(x))
    poly = 1.061405429 * 0.5
    for c in (-1.453152027, 1.421413741, -0.284496736, 0.254829592):
        poly = poly * t + 0.5 * c
    q = poly * t * e
    phi = jnp.where(x >= 0.0, 1.0 - q, q)
    return x * phi, phi + x * (e * (1.0 / math.sqrt(2.0 * math.pi)))


def slot_count(posr, row):
    n = jnp.sum((posr[row : row + 1, :] >= 0.0).astype(F32)).astype(I32)
    return ((n + 15) // 16) * 16


def expert_kernel(cfg, need, flush, *refs):
    j, sources, has_acc, merge, cap, local, experts = cfg
    last = has_acc
    streams = 2 if last and merge else 1
    n = len(sources)
    refs = list(refs)
    take = lambda k: [refs.pop(0) for _ in range(k)]
    (eidx,) = take(1)
    posr, meta = take(2)
    nrows = take(n)
    crows = take(n)
    upw, upa, upb, dnw, dna, dnb = take(6)
    if has_acc:
        (acc_in,) = take(1)
    if merge:
        posc, ret_in, grow_in, gg_in = take(4)
    if last:
        halves = take(2 * streams)
    else:
        (acc_b,) = take(1)
    if merge:
        grow_o = take(n)
        mix_o = take(n)
    else:
        ret_b, grow_b, gg_o = take(3)
    up, ua, dn, db, xbuf, cbuf, gate_b, mask_b, gg_b, hid, dgl, sems = take(12)
    (acc,) = take(1)
    if last:
        (acc_b,) = take(1)
    if merge:
        ret_b, grow_b, ret0, grow0 = take(4)
    rp = posr.shape[1]
    d = upw.shape[1]
    ff = upw.shape[2]
    width = upa.shape[2]
    loads = [
        pltpu.make_async_copy(upa.at[j], ua, sems.at[0]),
        pltpu.make_async_copy(upw.at[j], up.at[0:d], sems.at[1]),
        pltpu.make_async_copy(upb.at[j], up.at[d : d + width], sems.at[2]),
        pltpu.make_async_copy(dnw.at[j], dn.at[:, 0:d], sems.at[3]),
        pltpu.make_async_copy(dna.at[j], dn.at[:, d : d + width], sems.at[4]),
        pltpu.make_async_copy(dnb.at[j], db, sems.at[5]),
    ]
    late = []
    if has_acc:
        late.append(pltpu.make_async_copy(acc_in, acc_b, sems.at[6]))
    if merge:
        late.append(pltpu.make_async_copy(ret_in, ret0, sems.at[7]))
        late.append(pltpu.make_async_copy(grow_in, grow0, sems.at[8]))
    need(posr, meta, nrows[0], crows[0])
    for load in loads + late:
        load.start(priority=1)
    acc[...] = jnp.zeros_like(acc)
    slot_r = lax.broadcasted_iota(I32, (cap, rp), 0).astype(F32)
    mine = lax.broadcasted_iota(I32, (experts, rp), 0) == eidx[0] * local + j
    col_bank = (lax.broadcasted_iota(I32, (cap, width), 1) // RANK).astype(F32)
    offs = []
    off = jnp.int32(0)
    for i, s in enumerate(sources):
        off = pl.multiple_of(off, 16)
        offs.append(off)
        need(nrows[i], crows[i])
        hit = posr[s * local + j : s * local + j + 1, :] == slot_r
        probs = load_lines(nrows[i][rp : rp + 48, :].astype(F32), rp - d, 3)
        gate_line = jnp.sum(jnp.where(mine, probs, 0.0), axis=0, keepdims=True)
        bank = meta[s, 2:3, :].astype(F32)
        gate = jnp.sum(jnp.where(hit, gate_line, 0.0), axis=1, keepdims=True)
        slot_bank = jnp.sum(jnp.where(hit, bank, 0.0), axis=1, keepdims=True)
        pick = hit.astype(F32).astype(BF)
        xbuf[pl.ds(off, cap), :] = nn(pick, nrows[i][0:rp, :]).astype(BF)
        cbuf[pl.ds(off, cap), :] = nn(pick, crows[i][...]).astype(BF)
        gate_b[pl.ds(off, cap), :] = jnp.broadcast_to(gate, (cap, 128))
        mask_b[pl.ds(off, cap), :] = (col_bank == slot_bank).astype(F32)
        off = off + slot_count(posr, s * local + j)
    total = off
    rest = pl.ds(pl.multiple_of(offs[-1] + cap, 16), cap)
    xbuf[rest, :] = jnp.zeros((cap, d), BF)
    cbuf[rest, :] = jnp.zeros((cap, d), BF)
    gate_b[rest, :] = jnp.zeros((cap, 128), F32)
    mask_b[rest, :] = jnp.zeros((cap, width), F32)
    short = cap // 2
    rem = total % cap
    tiles = total // cap + (rem > short).astype(I32)
    tail = (rem > 0) & (rem <= short)
    chunks = [slice(c, min(c + CHUNK, ff)) for c in range(0, ff, CHUNK)]
    for load in loads:
        load.wait()

    def tile(start, size):
        rs = pl.ds(pl.multiple_of(start, 16), size)
        x = xbuf[rs, :]
        m = mask_b[rs, :]
        u = (nn(x, ua[...]) * m).astype(BF)
        xu = jnp.concatenate([x, u], axis=1)
        out = jnp.zeros((size, d + width), F32)
        for cs in chunks:
            h, dg = gelu_parts(nn(xu, up[:, cs]))
            hb = h.astype(BF)
            hid[0:size, cs] = hb
            dgl[0:size, cs] = dg
            out = out + nn(hb, dn[cs, :])
        ud = (out[:, d:] * m).astype(BF)
        ret = (out[:, :d] + nn(ud, db[...])).astype(BF).astype(F32)
        cot = cbuf[rs, :].astype(F32)
        gate = gate_b[rs, 0:1]
        gg_b[rs, :] = jnp.broadcast_to(jnp.sum(cot * ret, axis=1, keepdims=True), (size, 128))
        ret_b[rs, :] = (gate * ret).astype(BF)
        g = (gate * cot).astype(BF)
        gud = (nt(g, db[...]) * m).astype(BF)
        acc[:, d + 2 * ff :] += tn(ud, g)
        gg = jnp.concatenate([g, gud], axis=1)
        gr = jnp.zeros((size, d + width), F32)
        for cs in chunks:
            gp = (nt(gg, dn[cs, :]) * dgl[0:size, cs]).astype(BF)
            gr = gr + nt(gp, up[:, cs])
            acc[:, d + cs.start : d + cs.stop] += tn(u, gp)
            acc[:, d + ff + cs.start : d + ff + cs.stop] += tn(gud, hid[0:size, cs])
        guu = (gr[:, d:] * m).astype(BF)
        acc[:, 0:d] += tn(guu, x)
        grow_b[rs, :] = (gr[:, :d] + nt(guu, ua[...])).astype(BF)

    def whole(t, _):
        tile(t * cap, cap)
        return 0

    lax.fori_loop(0, tiles, whole, 0)

    @pl.when(tail)
    def _():
        tile(tiles * cap, short)

    done = pl.ds(pl.multiple_of(tiles * cap + tail.astype(I32) * short, 16), cap)
    ret_b[done, :] = jnp.zeros((cap, d), BF)
    grow_b[done, :] = jnp.zeros((cap, d), BF)
    gg_b[done, :] = jnp.zeros((cap, 128), F32)
    if last:
        late.pop(0).wait()
        half = width // 2
        part = half // 2
        wide = (2 * d + 2 * ff) // streams
        for n_s in range(streams):
            cols = slice(n_s * wide, (n_s + 1) * wide)
            for flip in range(2):
                out = halves[2 * n_s + flip]
                own = eidx[1 + n_s] if flip else 1 - eidx[1 + n_s]
                for b in range(2):
                    start = own * half + b * part if n_s == 0 else b * half + own * part
                    rs = pl.ds(pl.multiple_of(start, 16), part)
                    out[b * part : (b + 1) * part, :] = (
                        acc[rs, cols] + acc_b[rs, cols].astype(F32)
                    ).astype(BF)
        flush(*halves)
    else:
        acc_b[...] = acc[...].astype(BF)
        flush(acc_b)
    if not merge:
        flush(ret_b, grow_b)
    gg_lines = []
    for i, s in enumerate(sources):
        hit = posr[s * local + j : s * local + j + 1, :] == slot_r
        col = gg_b[pl.ds(offs[i], cap), 0:1]
        gg_lines.append(jnp.sum(jnp.where(hit, col, 0.0), axis=0, keepdims=True))
    if not merge:
        for i in range(n):
            gg_o[i : i + 1, :] = gg_lines[i]
    else:
        need(posc, gg_in)
        for load in late:
            load.wait()
        slot_c = lax.broadcasted_iota(I32, (rp, cap), 1).astype(F32)
        expert_row = lax.broadcasted_iota(I32, (experts, rp), 0)
        off0 = jnp.int32(0)
        for i, s in enumerate(sources):
            r0 = pl.ds(pl.multiple_of(off0, 16), cap)
            r1 = pl.ds(offs[i], cap)
            p0 = (posc[:, s * local : s * local + 1] == slot_c).astype(F32).astype(BF)
            p1 = (posc[:, s * local + 1 : s * local + 2] == slot_c).astype(F32).astype(BF)
            pick = jnp.concatenate([p0, p1], axis=1)
            for b0, b1, result in ((grow0, grow_b, grow_o[i]), (ret0, ret_b, mix_o[i])):
                both = jnp.concatenate([b0[r0, :], b1[r1, :]], axis=0)
                result[0:rp, :] = nn(pick, both).astype(BF)
            gg = jnp.where(
                expert_row == eidx[0] * local,
                gg_in[i : i + 1, :],
                jnp.where(expert_row == eidx[0] * local + 1, gg_lines[i], 0.0),
            )
            store_lines(grow_o[i], rp, gg, 2)
            flush(grow_o[i], mix_o[i])
            off0 = off0 + slot_count(posr, s * local)


def expert_call(j, sources, eidx, tables, nrows, crows, ws, cap, acc, first=None):
    posr, posc, meta = tables
    rp, d = crows[0].shape
    local, _, ff = ws[0].shape
    width = ws[1].shape[2]
    n = len(sources)
    experts = local * lax.axis_size("expert")
    merge = first is not None
    cfg = (j, tuple(sources), acc is not None, merge, cap, local, experts)
    buf = (n + 1) * cap
    kinds = "smm" + "m" * (2 * n) + "h" * 6
    args = [eidx, posr, meta]
    args += [nrows[s] for s in sources] + [crows[s] for s in sources] + list(ws)
    if acc is not None:
        args.append(acc)
        kinds += "h"
    if merge:
        args += [posc, *first]
        kinds += "mhhm"
    wide = (width, 2 * d + 2 * ff)
    if acc is not None:
        streams = 2 if merge else 1
        out_shape = (jax.ShapeDtypeStruct((width // 2, wide[1] // streams), BF),) * (2 * streams)
    else:
        out_shape = (jax.ShapeDtypeStruct(wide, BF),)
    if merge:
        out_shape += (jax.ShapeDtypeStruct((rp + 32, d), BF),) * n
        out_shape += (jax.ShapeDtypeStruct((rp, d), BF),) * n
    else:
        out_shape += (jax.ShapeDtypeStruct((buf, d), BF),) * 2
        out_shape += (jax.ShapeDtypeStruct((n, rp), F32),)
    scratch = [
        pltpu.VMEM((d + width, ff), BF),
        pltpu.VMEM((d, width), BF),
        pltpu.VMEM((ff, d + width), BF),
        pltpu.VMEM((width, d), BF),
        pltpu.VMEM((buf, d), BF),
        pltpu.VMEM((buf, d), BF),
        pltpu.VMEM((buf, 128), F32),
        pltpu.VMEM((buf, width), F32),
        pltpu.VMEM((buf, 128), F32),
        pltpu.VMEM((cap, ff), BF),
        pltpu.VMEM((cap, ff), F32),
        pltpu.SemaphoreType.DMA((9,)),
    ]
    scratch.append(pltpu.VMEM(wide, F32))
    if acc is not None:
        scratch.append(pltpu.VMEM(wide, BF))
    if merge:
        scratch += [pltpu.VMEM((buf, d), BF)] * 4
    return staged(
        functools.partial(expert_kernel, cfg),
        args,
        kinds,
        out_shape,
        scratch,
        60, 30, f"expert{j}_{'far' if sources[0] else 'near'}",
    )


def out_bwd_kernel(
    need, flush, banks, pt, p0, p1, p2, lr, rwt, rbt, n2, ra, mid, cot, g2, lo, bo, att, wo, ao,
    gmid, ga, gr_o,
    gml,
):
    rp, d = cot.shape
    experts = pt.shape[0]
    images = banks.shape[0]
    width = ao.shape[1]
    need(pt, p0, p1, p2)
    probs = pt[...]
    lines = sum(p[rp : rp + 32, :].astype(F32) for p in (p0, p1, p2))
    gp = load_lines(lines, rp - d, 2)
    glt = (probs * (gp - jnp.sum(gp * probs, axis=0, keepdims=True))).astype(BF)
    need(lr, rwt, rbt)
    rb = jnp.concatenate([nn(glt, lr[...]), jnp.zeros((experts, d - width), F32)], axis=1)
    rb = jnp.concatenate([rb, jnp.zeros((32 - experts, d), F32)], axis=0)
    gr_o[3 * width : 3 * width + 32, :] = rb.astype(BF)
    mask = bank_mask(banks, 0, rp, images, width)
    gu = (tn(glt, rbt[...].astype(BF)) * mask).astype(BF)
    need(n2, ra)
    gr_o[2 * width : 3 * width, :] = tn(gu, n2[0:rp, :]).astype(BF)
    gmid[...] = tn(glt, rwt[...].astype(BF)) + nt(gu, ra[...])

    need(mid, cot, g2)

    def ln2(i, _):
        rs = pl.ds(pl.multiple_of(i * 160, 160), 160)
        grad = gmid[rs, :] + (p0[rs, :].astype(F32) + p1[rs, :].astype(F32) + p2[rs, :].astype(F32))
        xhat, rstd = norm_parts(mid[rs, :])
        g = cot[rs, :].astype(F32) + norm_back(xhat, rstd, g2[...], grad)
        gmid[rs, :] = g
        gml[rs, :] = g.astype(BF)
        return 0

    lax.fori_loop(0, rp // 160, ln2, 0)
    flush(gmid)
    need(lo, bo, att, wo, ao)
    g = gml[...]
    gr_o[width : 2 * width, :] = tn(lo[...], g).astype(BF)
    gu = (nt(g, bo[...]) * mask).astype(BF)
    gr_o[0:width, :] = tn(gu, att[...]).astype(BF)
    ga[...] = (nt(g, wo[...]) + nt(gu, ao[...])).astype(BF)


def out_backward(banks, cot, g2, kept, ws, parts):
    rp, d = cot.shape
    width = ws[1].shape[1]
    wo, ao, bo, rwt, ra, rbt = ws
    att, lo, mid, n2, lr, pt = kept
    return staged(
        out_bwd_kernel,
        (banks, pt, *parts, lr, rwt, rbt, n2, ra, mid, cot, g2, lo, bo, att, wo, ao),
        "s" + "m" * 17,
        (
            jax.ShapeDtypeStruct((rp, d), F32),
            jax.ShapeDtypeStruct((rp, d), BF),
            jax.ShapeDtypeStruct((3 * width + 32, d), BF),
        ),
        [pltpu.VMEM((rp, d), BF)],
        36, 12, "out_bwd",
    )


def attn_bwd_kernel(
    need, flush, banks, core, q, k, lse, v, ga, lq, bq, n1, lk, bk, lv, bv, outr,
    gq, gk, gv, uq, uk, uv, send_o, keep_o,
    gr_o,
):
    rp, d = n1.shape
    images = banks.shape[0]
    width = bq.shape[0]
    win = lse.shape[2]
    step_rows = 16 * (SEQ // 16)
    lane = lax.broadcasted_iota(I32, (win, 128), 1)
    first = lane < HEAD_DIM
    row_i = lax.broadcasted_iota(I32, (win, 128), 0)
    key_i = lax.broadcasted_iota(I32, (win, win), 0)
    query_i = lax.broadcasted_iota(I32, (win, win), 1)

    need(q, k, v, ga, lse)

    def image(i, _):
        off = pl.multiple_of(i * step_rows, 64)
        start = i * (SEQ - step_rows)
        bias = jnp.where(
            (key_i >= start) & (key_i < start + SEQ) & (query_i >= start) & (query_i < start + SEQ),
            0.0,
            NEG,
        )
        keep = row_i < start
        ws = pl.ds(off, win)
        for p in range(d // 128):
            cols = slice(p * 128, p * 128 + 128)
            qp = q[ws, cols]
            kp = k[ws, cols]
            vp = v[ws, cols]
            gap = ga[ws, cols]
            rq, rk, rv = [], [], []
            for h in range(2):
                mine = first if h == 0 else jnp.logical_not(first)
                km = jnp.where(mine, kp, jnp.zeros_like(kp))
                vm = jnp.where(mine, vp, jnp.zeros_like(vp))
                prob = jnp.exp2(
                    nt(km, qp) * SCALE2 + bias - lse[i, 2 * p + h : 2 * p + h + 1, :]
                )
                gw = nt(vm, gap)
                delta = jnp.sum(gw * prob, axis=0, keepdims=True)
                gs = (prob * (gw - delta)).astype(BF)
                rv.append(nn(prob.astype(BF), gap))
                rk.append(nn(gs, qp))
                rq.append(tn(gs, kp))
            for parts, ref, scale in ((rq, gq, 0.125), (rk, gk, 0.125), (rv, gv, 1.0)):
                new = (jnp.where(first, parts[0], parts[1]) * scale).astype(BF)
                ref[ws, cols] = jnp.where(keep, ref[ws, cols], new)
        return 0

    lax.fori_loop(0, images, image, 0)
    flush(gq, gk, gv)
    need(n1, lq, lk, lv, bq, bk, bv)
    x = n1[...]
    mask = bank_mask(banks, 0, rp, images, width)
    for i, (grad, low, b, u) in enumerate(((gq, lq, bq, uq), (gk, lk, bk, uk), (gv, lv, bv, uv))):
        g = grad[...]
        gr_o[(2 * i + 1) * width : (2 * i + 2) * width, :] = tn(low[...], g).astype(BF)
        gu = (nt(g, b[...]) * mask).astype(BF)
        u[...] = gu
        gr_o[2 * i * width : (2 * i + 1) * width, :] = tn(gu, x).astype(BF)
    used = 6 * width + outr.shape[0]
    need(outr)
    gr_o[6 * width : used, :] = outr[...]
    if gr_o.shape[0] > used:
        gr_o[used:, :] = jnp.zeros((gr_o.shape[0] - used, d), BF)
    half = send_o.shape[0]
    keep_o[...] = gr_o[pl.ds(pl.multiple_of(core[0] * half, 16), half), :]
    send_o[...] = gr_o[pl.ds(pl.multiple_of((1 - core[0]) * half, 16), half), :]
    flush(send_o, keep_o)


def attn_backward(banks, core, kept, ga, bs, outr, shares):
    rp, d = ga.shape
    width = bs[0].shape[0]
    bfd = jax.ShapeDtypeStruct((rp, d), BF)
    low = jax.ShapeDtypeStruct((rp, width), BF)
    n1, q, k, v, lq, lk, lv, lse = kept
    bq, bk, bv = bs
    total = -(-(6 * width + outr.shape[0]) // (32 * shares)) * 32 * shares
    half = jax.ShapeDtypeStruct((total // 2, d), BF)
    return staged(
        attn_bwd_kernel,
        (banks, core, q, k, lse, v, ga, lq, bq, n1, lk, bk, lv, bv, outr),
        "ss" + "m" * 13,
        (bfd, bfd, bfd, low, low, low, half, half),
        [pltpu.VMEM((total, d), BF)],
        34, 20, "attn_bwd",
    )


def input_bwd_kernel(
    need, flush, gq, wq, uq, aq, gk, wk, uk, ak, gv, wv, uv, av, gmid, tok, g1, inp_o, total
):
    rows, d = inp_o.shape
    need(gq, wq, uq, aq)
    first = nt(gq[...], wq[...]) + nt(uq[...], aq[...])
    need(gk, wk, uk, ak)
    first = first + (nt(gk[...], wk[...]) + nt(uk[...], ak[...]))
    need(gv, wv, uv, av)
    total[...] = first + (nt(gv[...], wv[...]) + nt(uv[...], av[...]))
    need(gmid, tok, g1)
    whole = rows // 16 * 16
    for r, count in [(s, min(112, whole - s)) for s in range(0, whole, 112)] + (
        [(whole, rows - whole)] if rows > whole else []
    ):
        rs = slice(r, r + count)
        xhat, rstd = norm_parts(tok[rs, :].astype(F32))
        inp_o[rs, :] = gmid[rs, :] + norm_back(xhat, rstd, g1[...], total[rs, :])


def input_backward(tok, rows, g1, gmid, grads, ws):
    d = tok.shape[1]
    gq, gk, gv, uq, uk, uv = grads
    wq, wk, wv, aq, ak, av = ws
    return staged(
        input_bwd_kernel,
        (gq, wq, uq, aq, gk, wk, uk, ak, gv, wv, uv, av, gmid, tok, g1),
        "m" * 15,
        (jax.ShapeDtypeStruct((rows, d), F32),),
        [pltpu.VMEM(gmid.shape, F32)],
        34, 7, "input_bwd",
    )[0]


def join(bit, own, other, out, low, high):
    half = own.shape[0]
    out[0:half, low:high] = jnp.where(bit == 0, own[:, low:high], other[:, low:high])
    out[half : 2 * half, low:high] = jnp.where(bit == 0, other[:, low:high], own[:, low:high])


def finish_kernel(need, flush, bit, own, other, *rest):
    outs, flat = rest[:-1], rest[-1]
    width, d = outs[1].shape
    experts = outs[9].shape[0]
    need(own, other)
    join(bit[0], own, other, flat, 0, d)
    for i in range(5):
        base = 2 * i * width
        outs[2 * i][...] = jnp.transpose(flat[base : base + width, :].astype(F32))
        flush(outs[2 * i])
        if i < 4:
            outs[2 * i + 1][...] = flat[base + width : base + 2 * width, :].astype(F32)
            flush(outs[2 * i + 1])
    outs[9][...] = flat[9 * width : 9 * width + 16, 0:width].astype(F32)[0:experts]


def finish(bit, own, other, width, experts):
    d = own.shape[1]
    tall = jax.ShapeDtypeStruct((d, width), F32)
    wide = jax.ShapeDtypeStruct((width, d), F32)
    return staged(
        finish_kernel,
        (bit, own, other),
        "smm" if own.shape[0] % 16 == 0 else "svv",
        (tall, wide) * 4 + (tall, jax.ShapeDtypeStruct((experts, width), F32)),
        [pltpu.VMEM((2 * own.shape[0], d), BF)],
        16, 2, "finish",
    )


def finish_expert_kernel(cfg, need, flush, bit, own, other, *rest):
    j, aliased = cfg
    ua_o, ub_o, da_o, db_o, ua, ub, da, db, both, sems = rest[4:] if aliased else rest
    d, width = ua.shape
    ff = ub.shape[1]
    need(own, other)
    copies = []

    def put(n, src, out):
        copies.append(pltpu.make_async_copy(src, out.at[j], sems.at[n]))
        copies[-1].start()

    join(bit[0], own, other, both, d + ff, d + 2 * ff)
    da[...] = jnp.transpose(both[:, d + ff : d + 2 * ff].astype(F32))
    put(0, da, da_o)
    join(bit[0], own, other, both, d, d + ff)
    ub[...] = both[:, d : d + ff].astype(F32)
    put(1, ub, ub_o)
    join(bit[0], own, other, both, 0, d)
    ua[...] = jnp.transpose(both[:, 0:d].astype(F32))
    put(2, ua, ua_o)
    join(bit[0], own, other, both, d + 2 * ff, 2 * d + 2 * ff)
    db[...] = both[:, d + 2 * ff :].astype(F32)
    put(3, db, db_o)
    for copy in copies:
        copy.wait()


def finish_expert(j, n, bit, own, other, d, earlier=()):
    half, wide = own.shape
    width = 2 * half
    ff = wide // 2 - d
    shapes = ((d, width), (width, ff), (ff, width), (width, d))
    args = (bit, own, other, *earlier)
    return staged(
        functools.partial(finish_expert_kernel, (j, bool(earlier))),
        args,
        "smm" + "h" * len(earlier),
        tuple(jax.ShapeDtypeStruct((n,) + x, F32) for x in shapes),
        [pltpu.VMEM(x, F32) for x in shapes]
        + [pltpu.VMEM((width, wide), BF), pltpu.SemaphoreType.DMA((4,))],
        24, 3, f"finish_expert{j}",
        direct=True,
        aliases={3 + i: i for i in range(len(earlier))},
    )


def hop(x, axis, k):
    n = lax.axis_size(axis)
    return lax.ppermute(x, axis, [(i, i ^ k) for i in range(n)])


def bits(axis):
    n = lax.axis_size(axis)
    return [1 << i for i in range(n.bit_length() - 1)]


def add(a, b):
    return (a.astype(F32) + b.astype(F32)).astype(BF)


def part_of(terms, bit, flip):
    half = terms[0].shape[0] // 2
    start = (bit if not flip else 1 - bit) * half
    return sum(lax.dynamic_slice_in_dim(t, start, half, 0).astype(F32) for t in terms).astype(BF)


def reduce_step(terms, axis, k):
    bit = (lax.axis_index(axis) // k) % 2
    send = part_of(terms, bit, True)
    return send, part_of(terms, bit, False), hop(send, axis, k)


def gather_step(buf, axis, k, wait=None):
    bit = (lax.axis_index(axis) // k) % 2
    other = hop(buf, axis, k)
    if wait is not None:
        other = after(other, *(wait if isinstance(wait, tuple) else (wait,)))
    return jnp.where(
        bit == 0,
        jnp.concatenate([buf, other], axis=0),
        jnp.concatenate([other, buf], axis=0),
    )


def after(x, *deps):
    return lax.optimization_barrier((x,) + deps)[0]


def gather4(x):
    near = hop(x, "expert", 1)
    far = hop(x, "expert", 2)
    return [x, near, far, hop(far, "expert", 1)]


def body(
    tokens, cotangent, bank_ids, routes, attn_gain, expert_gain, query_w, key_w, value_w, out_w,
    query_a, query_b, key_a, key_b, value_a, value_b, out_a, out_b, router_w, router_a, router_b,
    up_w, up_a, up_b, down_w, down_a, down_b,
):
    rows, d = tokens.shape
    rp = 32 * (-(-rows // 32))
    width = query_a.shape[1]
    local = up_w.shape[0]
    groups = lax.axis_size("expert")
    experts = local * groups
    cap = 13 * rows // (4 * experts)
    place = lax.axis_index("dp")
    me = jnp.stack([lax.axis_index("expert"), place % 2, place // 2 % 2]).astype(I32)
    cot = jnp.pad(cotangent, ((0, rp - rows), (0, 0)))
    cot1 = hop(cot, "expert", 1)
    cot2 = hop(cot, "expert", 2)
    meta = jnp.concatenate([routes.T, jnp.repeat(bank_ids, SEQ)[None, :]], axis=0)
    meta = jnp.pad(meta, ((0, 0), (0, rp - rows)), constant_values=-1)
    meta = jnp.stack(gather4(meta))
    g1 = attn_gain.reshape(1, d)
    g2 = expert_gain.reshape(1, d)
    kept = attn_forward(
        bank_ids, tokens, g1,
        (query_w, query_a, query_b, key_w, key_a, key_b, value_w, value_a, value_b),
    )
    n1, q, k, v, lq, lk, lv, att, lse, tokp = kept
    out_ws = (out_w, out_a, out_b, router_w.T.astype(F32), router_a, router_b.T.astype(F32))
    lo, mid, n2, lr, pt = out_forward(
        bank_ids, tokp, g2, after(att, meta), out_ws, (cot1,)
    )
    near1 = hop(n2, "expert", 1)
    far2 = hop(after(n2, cot2), "expert", 2)
    cot3 = hop(after(cot2, n2), "expert", 1)
    tables = routing_tables(me, after(meta, n2), local) + (meta,)
    crows = [cot, cot1, cot2, cot3]
    ews = (up_w, up_a, up_b, down_w, down_a, down_b)
    common = (crows, ews, cap)
    nrows = [n2, near1, None, None]
    e0n = expert_call(0, (0, 1), after(me, cot3), tables, nrows, *common, None)
    far2 = after(far2, e0n[1])
    nrows = [n2, near1, far2, hop(far2, "expert", 1)]
    e0f = expert_call(0, (2, 3), me, tables, nrows, *common, e0n[0])
    dp_steps = [("dp", k) for k in bits("dp")]
    ex_steps = [("expert", k) for k in bits("expert")]
    got0 = hop(e0f[0], *dp_steps[0])
    keep0 = e0f[1]
    e1f = expert_call(
        1, (2, 3), after(me, keep0), tables, nrows, *common, None, e0f[2:]
    )
    grow = add(e1f[1], hop(e1f[2], "expert", 1))
    send0, keep0, got0 = reduce_step([keep0, after(got0, e1f[1])], *dp_steps[1])
    e1n = expert_call(
        1, (0, 1), after(me, grow, send0), tables, nrows, *common, e1f[0], e0n[1:]
    )
    send1, keep1, send2, keep2, *near = e1n
    grow_far = hop(grow, "expert", 2)
    grow_near = hop(after(near[1], grow_far), "expert", 1)
    mix_far = hop(after(e1f[3], near[0]), "expert", 2)
    mix_cross = hop(after(e1f[4], near[0]), "expert", 3)
    send0, keep0, got0 = reduce_step([keep0, after(got0, near[0])], *dp_steps[2])
    got1 = hop(after(send1, near[0]), *dp_steps[0])
    got2 = hop(after(send2, near[0]), *dp_steps[1])
    gmid, ga, outr = out_backward(
        bank_ids, cot, g2, (att, lo, mid, n2, lr, pt), out_ws,
        (near[0], after(grow_near, send0), grow_far),
    )
    got0 = after(got0, gmid)
    for step in dp_steps[3:]:
        _, keep0, got0 = reduce_step([keep0, got0], *step)
    buf0 = add(keep0, got0)
    send1, keep1, got1 = reduce_step([keep1, after(got1, gmid)], *dp_steps[1])
    send2, keep2, got2 = reduce_step([keep2, after(got2, gmid)], *dp_steps[0])
    core = lax.axis_index("expert").astype(I32).reshape(1) % 2
    shares = lax.axis_size("dp") * groups // 32
    *grads, qkv, keep = attn_backward(
        bank_ids, core, (n1, q, k, v, lq, lk, lv, lse), after(ga, buf0, send1, send2),
        (query_b, key_b, value_b), outr, shares,
    )
    up_steps = dp_steps[::-1]
    bit = me[1:2]
    buf0 = gather_step(buf0, *up_steps[0], wait=qkv)
    qkv = after(qkv, mix_far, mix_cross)
    mix_near = hop(after(near[3], qkv), "expert", 1)
    keep1 = jnp.concatenate([keep1, keep2], axis=1)
    got1 = jnp.concatenate([after(got1, qkv), after(got2, qkv)], axis=1)
    send1, keep1, got1 = reduce_step([keep1, got1], *dp_steps[2])
    got = hop(after(qkv, buf0, send1), *ex_steps[0])
    send, keep, got = reduce_step([keep, got], *ex_steps[1])
    input_grad = input_backward(
        tokp, rows, g1, after(gmid, send), grads,
        (query_w, key_w, value_w, query_a, key_a, value_a),
    )
    got = after(got, input_grad)
    for step in dp_steps[3:]:
        _, keep1, got1 = reduce_step([keep1, got1], *step)
    buf1 = add(keep1, after(got1, input_grad))
    for step in up_steps[1:-1]:
        buf0 = gather_step(buf0, *step, wait=input_grad)
    for step in ex_steps[2:]:
        _, keep, got = reduce_step([keep, got], *step)
    send, keep, got = reduce_step([keep, after(got, buf0, buf1)], *dp_steps[0])
    peer0 = hop(after(buf0, send), *up_steps[-1])
    buf1 = gather_step(buf1, *up_steps[0])
    for step in dp_steps[1:-1]:
        _, keep, got = reduce_step([keep, got], *step)
    _, keep, got = reduce_step([keep, after(got, buf1)], *dp_steps[-1])
    for step in up_steps[1:-1]:
        buf1 = gather_step(buf1, *step)
    flat = after(add(keep, got), peer0)
    flat = gather_step(flat, *up_steps[0])
    for step in up_steps[1:-1]:
        flat = gather_step(after(flat, buf1), *step)
    peer1 = hop(buf1, *up_steps[-1])
    flat = gather_step(flat, *up_steps[-1])
    for step in reversed(ex_steps[2:]):
        flat = gather_step(flat, *step)
    mixed = mid[:rows] + (
        (near[2][:rows].astype(F32) + mix_near[:rows].astype(F32))
        + (mix_far[:rows].astype(F32) + mix_cross[:rows].astype(F32))
    )
    mixed = mixed.astype(BF)
    large = finish_expert(0, local, bit, buf0, peer0, d)
    flat = gather_step(flat, *ex_steps[1], wait=(mixed, large[0]))
    peer = hop(after(flat, peer1), *ex_steps[0])
    large = finish_expert(1, local, bit, buf1, peer1, d, large)
    small = finish(
        core, flat, after(peer, large[0]), width, experts,
    )
    return (mixed, input_grad, *small[:9], small[9].T, *large)


def solution(mesh):
    split = P(("dp", "expert"), None)
    by_expert = P("expert", None, None)
    in_specs = (split, split, P(("dp", "expert")), split) + (P(),) * 17 + (by_expert,) * 6
    out_specs = (split, split) + (P(),) * 10 + (by_expert,) * 4
    return jax.shard_map(body, mesh=mesh, in_specs=in_specs, out_specs=out_specs, check_vma=False)
```

```python
import functools
import math

import jax
import jax.numpy as jnp
from jax import lax
from jax.experimental import pallas as pl
from jax.experimental.pallas import tpu as pltpu
from jax.sharding import PartitionSpec as P

HEAD_DIM = 64
RANK = 16
SEQ = 197
EPS = 1e-06
BF = jnp.bfloat16
F32 = jnp.float32
I32 = jnp.int32
LOG2E = math.log2(math.e)
SCALE2 = HEAD_DIM ** (-0.5) * LOG2E
NEG = -1e30
CHUNK = 1536
VMEM = pl.BlockSpec(memory_space=pltpu.VMEM)
SMEM = pl.BlockSpec(memory_space=pltpu.SMEM)
HBM = pl.BlockSpec(memory_space=pltpu.HBM)


def nn(a, b):
    return jnp.dot(a, b, preferred_element_type=F32)


def nt(a, b):
    return lax.dot_general(a, b, (((1,), (1,)), ((), ())), preferred_element_type=F32)


def tn(a, b):
    return lax.dot_general(a, b, (((0,), (0,)), ((), ())), preferred_element_type=F32)


def params(mib):
    return pltpu.CompilerParams(vmem_limit_bytes=mib * 1024 * 1024)


def cost(us):
    return pl.CostEstimate(
        flops=int(us * 1.1e9), bytes_accessed=int(us * 3e6), transcendentals=0
    )


def staged(kernel, args, kinds, outs, scratch, mib, us, name, direct=False, aliases=None):
    specs = {"s": SMEM, "v": VMEM, "h": HBM, "m": HBM}
    moved = [i for i, k in enumerate(kinds) if k == "m"]
    large = [] if direct else [
        i
        for i, o in enumerate(outs)
        if math.prod(o.shape) >= 1 << 15 and (o.dtype == F32 or o.shape[-2] % 16 == 0)
    ]
    n_in, n_out = len(args), len(outs)
    copies = len(moved) + len(large)

    def run(*refs):
        ins, results = list(refs[:n_in]), list(refs[n_in : n_in + n_out])
        own = refs[n_in + n_out : n_in + n_out + len(scratch)]
        buffers = refs[n_in + n_out + len(scratch) : -1]
        sems = refs[-1]
        arriving, leaving = [], []
        for n, i in enumerate(moved):
            copy = pltpu.make_async_copy(ins[i], buffers[n], sems.at[n])
            copy.start(priority=1)
            arriving.append([buffers[n], copy, False])
            ins[i] = buffers[n]
        for n, i in enumerate(large, len(moved)):
            copy = pltpu.make_async_copy(buffers[n], results[i], sems.at[n])
            leaving.append([buffers[n], copy, False])
            results[i] = buffers[n]

        def need(*wanted):
            for entry in arriving:
                if not entry[2] and any(entry[0] is ref for ref in wanted):
                    entry[1].wait()
                    entry[2] = True

        def flush(*ready):
            for entry in leaving:
                if not entry[2] and any(entry[0] is ref for ref in ready):
                    entry[1].start()
                    entry[2] = True

        kernel(need, flush, *ins, *results, *own)
        need(*[entry[0] for entry in arriving])
        flush(*[entry[0] for entry in leaving])
        for entry in leaving:
            entry[1].wait()

    return pl.pallas_call(
        run,
        out_shape=tuple(outs),
        in_specs=[specs[k] for k in kinds],
        out_specs=tuple(HBM if direct or i in large else VMEM for i in range(n_out)),
        input_output_aliases=aliases or {},
        scratch_shapes=list(scratch)
        + [pltpu.VMEM(args[i].shape, args[i].dtype) for i in moved]
        + [pltpu.VMEM(outs[i].shape, outs[i].dtype) for i in large]
        + [pltpu.SemaphoreType.DMA((max(copies, 1),))],
        compiler_params=params(60 if mib == 60 else 63),
        cost_estimate=cost(us),
        name=name,
    )(*args)


def split_parts(x, n):
    parts = []
    for _ in range(n):
        low = x.astype(BF)
        parts.append(low)
        x = x - low.astype(F32)
    return parts


def store_lines(ref, start, lines, n):
    d = ref.shape[1]
    for i, part in enumerate(split_parts(lines, n)):
        part = part.astype(F32)
        rest = part.shape[1] - d
        tail = jnp.concatenate(
            [part[:, d:], jnp.zeros((part.shape[0], d - rest), F32)], axis=1
        )
        ref[start + 16 * i : start + 16 * i + 16, :] = jnp.concatenate(
            [part[:, :d], tail], axis=0
        ).astype(BF)


def load_lines(block, rest, n):
    total = sum(block[16 * i : 16 * i + 16, :] for i in range(n))
    return jnp.concatenate([total[:8], total[8:, :rest]], axis=1)


def image_banks(banks, row, images):
    bank = jnp.full(row.shape, banks[0], I32)
    for i in range(1, images):
        bank = jnp.where(row >= SEQ * i, banks[i], bank)
    return bank


def bank_mask(banks, start, count, images, width):
    row = lax.broadcasted_iota(I32, (count, width), 0) + start
    col = lax.broadcasted_iota(I32, (count, width), 1)
    return (col // RANK == image_banks(banks, row, images)).astype(F32)


def norm_parts(x):
    mean = jnp.mean(x, axis=-1, keepdims=True)
    cen = x - mean
    rstd = lax.rsqrt(jnp.mean(cen * cen, axis=-1, keepdims=True) + EPS)
    return cen * rstd, rstd


def norm_back(xhat, rstd, gain, grad):
    gy = grad * gain
    return rstd * (
        gy
        - jnp.mean(gy, axis=-1, keepdims=True)
        - xhat * jnp.mean(gy * xhat, axis=-1, keepdims=True)
    )


def attn_fwd_kernel(
    need, flush, banks, tok, g1, wq, aq, bq, wk, ak, bk, wv, av, bv,
    n1_o, q_o, k_o, v_o, lq_o, lk_o, lv_o, att_o, lse_o, tokp,
    lset,
):
    rows = tok.shape[0]
    rp = n1_o.shape[0]
    images = rows // SEQ
    d = tok.shape[1]
    width = aq.shape[1]
    win = lse_o.shape[2]
    step_rows = 16 * (SEQ // 16)
    tokp[pl.ds(rp - 16, 16), :] = jnp.zeros((16, d), BF)
    tokp[0:rows, :] = tok[...]
    flush(tokp)
    need(g1)

    def ln1(i, _):
        r = pl.multiple_of(i * 160, 160)
        xhat, _r = norm_parts(tokp[pl.ds(r, 160), :].astype(F32))
        n1_o[pl.ds(r, 160), :] = (g1[...][None, :] * xhat).astype(BF)
        return 0

    lax.fori_loop(0, rp // 160, ln1, 0)
    flush(n1_o)
    half = rp // 2
    for w, a, b, out, low in (
        (wq, aq, bq, q_o, lq_o),
        (wk, ak, bk, k_o, lk_o),
        (wv, av, bv, v_o, lv_o),
    ):
        need(w, a, b)
        for r in (0, half):
            x = n1_o[r : r + half, :]
            mask = bank_mask(banks, r, half, images, width)
            u = (nn(x, a[...]) * mask).astype(BF)
            low[r : r + half, :] = u
            out[r : r + half, :] = (nn(x, w[...]) + nn(u, b[...])).astype(BF)
        flush(out, low)

    lane = lax.broadcasted_iota(I32, (win, 128), 1)
    first = lane < HEAD_DIM
    row_i = lax.broadcasted_iota(I32, (win, 128), 0)
    keys_i = lax.broadcasted_iota(I32, (win, win), 1)

    def image(i, _):
        off = pl.multiple_of(i * step_rows, 64)
        lo = i * (SEQ - step_rows)
        bias = jnp.where((keys_i >= lo) & (keys_i < lo + SEQ), 0.0, NEG)
        keep = row_i < lo
        lset[...] = jnp.zeros_like(lset)
        lse_tile = jnp.zeros((win, 128), F32)
        for p in range(d // 128):
            cols = slice(p * 128, p * 128 + 128)
            qp = q_o[pl.ds(off, win), cols]
            kp = k_o[pl.ds(off, win), cols]
            vp = v_o[pl.ds(off, win), cols]
            outs = []
            for h in range(2):
                mine = first if h == 0 else jnp.logical_not(first)
                qm = jnp.where(mine, qp, jnp.zeros_like(qp))
                s = nt(qm, kp) * SCALE2 + bias
                top = jnp.max(s, axis=-1, keepdims=True)
                e = jnp.exp2(s - top)
                den = jnp.sum(e, axis=-1, keepdims=True)
                w = (e * pl.reciprocal(den)).astype(BF)
                outs.append(nn(w, vp))
                lse = top + jnp.log2(den)
                lse_tile = jnp.where(lane == 2 * p + h, lse, lse_tile)
            new = jnp.where(first, outs[0], outs[1]).astype(BF)
            att_o[pl.ds(off, win), cols] = jnp.where(keep, att_o[pl.ds(off, win), cols], new)
        lset[0:win, :] = lse_tile
        lse_o[i] = jnp.transpose(lset[...])[0 : lse_o.shape[1], 0:win]
        return 0

    lax.fori_loop(0, images, image, 0)


def out_fwd_kernel(
    need, flush, banks, att, ao, bo, wo, tokp, g2, ra, rwt, rbt, *rest
):
    lo_o, mid_o, n2_o, lr_o, pt_o = rest[-5:]
    rp, d = tokp.shape
    images = banks.shape[0]
    width = ao.shape[1]
    half = rp // 2
    need(att, wo, ao, bo, tokp, g2)

    def out_proj(i, _):
        r = pl.multiple_of(i * half, 16)
        x = att[pl.ds(r, half), :]
        mask = bank_mask(banks, r, half, images, width)
        u = (nn(x, ao[...]) * mask).astype(BF)
        lo_o[pl.ds(r, half), :] = u
        mid_o[pl.ds(r, half), :] = (
            tokp[pl.ds(r, half), :].astype(F32) + nn(x, wo[...]) + nn(u, bo[...])
        )
        return 0

    lax.fori_loop(0, 2, out_proj, 0)
    flush(lo_o, mid_o)

    def ln2(i, _):
        r = pl.multiple_of(i * 160, 160)
        xhat, _r = norm_parts(mid_o[pl.ds(r, 160), :])
        n2_o[pl.ds(r, 160), :] = (g2[...][None, :] * xhat).astype(BF)
        return 0

    lax.fori_loop(0, rp // 160, ln2, 0)
    need(ra, rwt, rbt)
    x = n2_o[0:rp, :]
    u = (nn(x, ra[...]) * bank_mask(banks, 0, rp, images, width)).astype(BF)
    lr_o[...] = u
    logits = nt(rwt[...].astype(BF), x) + nt(rbt[...].astype(BF), u)
    e = jnp.exp(logits - jnp.max(logits, axis=0, keepdims=True))
    probs = e / jnp.sum(e, axis=0, keepdims=True)
    pt_o[...] = probs
    store_lines(n2_o, rp, probs, 3)


def attn_forward(banks, tok, g1, ws):
    rows, d = tok.shape
    rp = 32 * (-(-rows // 32))
    images = rows // SEQ
    step_rows = 16 * (SEQ // 16)
    win = rp - step_rows * (images - 1)
    width = ws[1].shape[1]
    heads_pad = 16 * (-(-d // (16 * HEAD_DIM)))
    bfd = jax.ShapeDtypeStruct((rp, d), BF)
    low = jax.ShapeDtypeStruct((rp, width), BF)
    out_shape = (bfd, bfd, bfd, bfd, low, low, low, bfd) + (
        jax.ShapeDtypeStruct((images, heads_pad, win), F32),
        bfd,
    )
    return staged(
        attn_fwd_kernel,
        (banks, tok, g1, *ws),
        "svm" + "m" * 9,
        out_shape,
        [pltpu.VMEM((256, 128), F32)],
        36, 20, "attn_fwd",
    )


def out_forward(banks, tokp, g2, att, ws, after):
    rp, d = tokp.shape
    low = jax.ShapeDtypeStruct((rp, ws[1].shape[1]), BF)
    out_shape = (
        low,
        jax.ShapeDtypeStruct((rp, d), F32),
        jax.ShapeDtypeStruct((rp + 48, d), BF),
        low,
        jax.ShapeDtypeStruct((ws[3].shape[0], rp), F32),
    )
    return staged(
        out_fwd_kernel,
        (banks, att, ws[1], ws[2], ws[0], tokp, g2, ws[4], ws[3], ws[5], *after),
        "s" + "m" * 9 + "h" * len(after),
        out_shape,
        [],
        24, 7, "out_fwd",
    )


def tables_kernel(need, flush, eidx, routes, posr_o, posc_o):
    groups, _, rp = routes.shape
    local = posr_o.shape[0] // groups
    need(routes)
    row = lax.broadcasted_iota(I32, (rp, rp), 0)
    col = lax.broadcasted_iota(I32, (rp, rp), 1)
    upper = (row < col).astype(BF)
    lower = (col < row).astype(BF)
    lower_inc = (col <= row).astype(BF)
    which = lax.broadcasted_iota(I32, (groups * local, rp), 0)
    hot = jnp.zeros((groups * local, rp), F32)
    for s in range(groups):
        r0 = routes[s, 0:1, :]
        r1 = routes[s, 1:2, :]
        for j in range(local):
            e = eidx[0] * local + j
            hit = ((r0 == e) | (r1 == e)).astype(F32)
            hot = jnp.where(which == s * local + j, hit, hot)
    hb = hot.astype(BF)
    posr_o[...] = jnp.where(hot > 0.0, nn(hb, upper), -1.0)
    before = nt(lower, hb)
    with_own = nt(lower_inc, hb)
    posc_o[...] = jnp.where(with_own > before, before, -1.0)


def routing_tables(eidx, routes, local):
    groups, _, rp = routes.shape
    n = groups * local
    return staged(
        tables_kernel,
        (eidx, routes),
        "sm",
        (jax.ShapeDtypeStruct((n, rp), F32), jax.ShapeDtypeStruct((rp, n), F32)),
        [],
        16, 2, "routing_tables",
    )


def gelu_parts(x):
    e = jnp.exp2((-0.5 * LOG2E) * (x * x))
    t = pl.reciprocal(1.0 + (0.3275911 / math.sqrt(2.0)) * jnp.abs(x))
    poly = 1.061405429 * 0.5
    for c in (-1.453152027, 1.421413741, -0.284496736, 0.254829592):
        poly = poly * t + 0.5 * c
    q = poly * t * e
    phi = jnp.where(x >= 0.0, 1.0 - q, q)
    return x * phi, phi + x * (e * (1.0 / math.sqrt(2.0 * math.pi)))


def slot_count(posr, row):
    n = jnp.sum((posr[row : row + 1, :] >= 0.0).astype(F32)).astype(I32)
    return ((n + 15) // 16) * 16


def expert_kernel(cfg, need, flush, *refs):
    j, sources, has_acc, merge, cap, local, experts = cfg
    last = has_acc
    streams = 2 if last and merge else 1
    n = len(sources)
    refs = list(refs)
    take = lambda k: [refs.pop(0) for _ in range(k)]
    (eidx,) = take(1)
    posr, meta = take(2)
    nrows = take(n)
    crows = take(n)
    upw, upa, upb, dnw, dna, dnb = take(6)
    if has_acc:
        (acc_in,) = take(1)
    if merge:
        posc, ret_in, grow_in, gg_in = take(4)
    if last:
        halves = take(2 * streams)
    else:
        (acc_b,) = take(1)
    if merge:
        grow_o = take(n)
        mix_o = take(n)
    else:
        ret_b, grow_b, gg_o = take(3)
    up, ua, dn, db, xbuf, cbuf, gate_b, mask_b, gg_b, hid, dgl, sems = take(12)
    (acc,) = take(1)
    if last:
        (acc_b,) = take(1)
    if merge:
        ret_b, grow_b, ret0, grow0 = take(4)
    rp = posr.shape[1]
    d = upw.shape[1]
    ff = upw.shape[2]
    width = upa.shape[2]
    loads = [
        pltpu.make_async_copy(upa.at[j], ua, sems.at[0]),
        pltpu.make_async_copy(upw.at[j], up.at[0:d], sems.at[1]),
        pltpu.make_async_copy(upb.at[j], up.at[d : d + width], sems.at[2]),
        pltpu.make_async_copy(dnw.at[j], dn.at[:, 0:d], sems.at[3]),
        pltpu.make_async_copy(dna.at[j], dn.at[:, d : d + width], sems.at[4]),
        pltpu.make_async_copy(dnb.at[j], db, sems.at[5]),
    ]
    late = []
    if has_acc:
        late.append(pltpu.make_async_copy(acc_in, acc_b, sems.at[6]))
    if merge:
        late.append(pltpu.make_async_copy(ret_in, ret0, sems.at[7]))
        late.append(pltpu.make_async_copy(grow_in, grow0, sems.at[8]))
    need(posr, meta, nrows[0], crows[0])
    for load in loads + late:
        load.start(priority=1)
    acc[...] = jnp.zeros_like(acc)
    slot_r = lax.broadcasted_iota(I32, (cap, rp), 0).astype(F32)
    mine = lax.broadcasted_iota(I32, (experts, rp), 0) == eidx[0] * local + j
    col_bank = (lax.broadcasted_iota(I32, (cap, width), 1) // RANK).astype(F32)
    offs = []
    off = jnp.int32(0)
    for i, s in enumerate(sources):
        off = pl.multiple_of(off, 16)
        offs.append(off)
        need(nrows[i], crows[i])
        hit = posr[s * local + j : s * local + j + 1, :] == slot_r
        probs = load_lines(nrows[i][rp : rp + 48, :].astype(F32), rp - d, 3)
        gate_line = jnp.sum(jnp.where(mine, probs, 0.0), axis=0, keepdims=True)
        bank = meta[s, 2:3, :].astype(F32)
        gate = jnp.sum(jnp.where(hit, gate_line, 0.0), axis=1, keepdims=True)
        slot_bank = jnp.sum(jnp.where(hit, bank, 0.0), axis=1, keepdims=True)
        pick = hit.astype(F32).astype(BF)
        xbuf[pl.ds(off, cap), :] = nn(pick, nrows[i][0:rp, :]).astype(BF)
        cbuf[pl.ds(off, cap), :] = nn(pick, crows[i][...]).astype(BF)
        gate_b[pl.ds(off, cap), :] = jnp.broadcast_to(gate, (cap, 128))
        mask_b[pl.ds(off, cap), :] = (col_bank == slot_bank).astype(F32)
        off = off + slot_count(posr, s * local + j)
    total = off
    rest = pl.ds(pl.multiple_of(offs[-1] + cap, 16), cap)
    xbuf[rest, :] = jnp.zeros((cap, d), BF)
    cbuf[rest, :] = jnp.zeros((cap, d), BF)
    gate_b[rest, :] = jnp.zeros((cap, 128), F32)
    mask_b[rest, :] = jnp.zeros((cap, width), F32)
    short = cap // 2
    rem = total % cap
    tiles = total // cap + (rem > short).astype(I32)
    tail = (rem > 0) & (rem <= short)
    chunks = [slice(c, min(c + CHUNK, ff)) for c in range(0, ff, CHUNK)]
    for load in loads:
        load.wait()

    def tile(start, size):
        rs = pl.ds(pl.multiple_of(start, 16), size)
        x = xbuf[rs, :]
        m = mask_b[rs, :]
        u = (nn(x, ua[...]) * m).astype(BF)
        xu = jnp.concatenate([x, u], axis=1)
        out = jnp.zeros((size, d + width), F32)
        for cs in chunks:
            h, dg = gelu_parts(nn(xu, up[:, cs]))
            hb = h.astype(BF)
            hid[0:size, cs] = hb
            dgl[0:size, cs] = dg
            out = out + nn(hb, dn[cs, :])
        ud = (out[:, d:] * m).astype(BF)
        ret = (out[:, :d] + nn(ud, db[...])).astype(BF).astype(F32)
        cot = cbuf[rs, :].astype(F32)
        gate = gate_b[rs, 0:1]
        gg_b[rs, :] = jnp.broadcast_to(jnp.sum(cot * ret, axis=1, keepdims=True), (size, 128))
        ret_b[rs, :] = (gate * ret).astype(BF)
        g = (gate * cot).astype(BF)
        gud = (nt(g, db[...]) * m).astype(BF)
        acc[:, d + 2 * ff :] += tn(ud, g)
        gg = jnp.concatenate([g, gud], axis=1)
        gr = jnp.zeros((size, d + width), F32)
        for cs in chunks:
            gp = (nt(gg, dn[cs, :]) * dgl[0:size, cs]).astype(BF)
            gr = gr + nt(gp, up[:, cs])
            acc[:, d + cs.start : d + cs.stop] += tn(u, gp)
            acc[:, d + ff + cs.start : d + ff + cs.stop] += tn(gud, hid[0:size, cs])
        guu = (gr[:, d:] * m).astype(BF)
        acc[:, 0:d] += tn(guu, x)
        grow_b[rs, :] = (gr[:, :d] + nt(guu, ua[...])).astype(BF)

    def whole(t, _):
        tile(t * cap, cap)
        return 0

    lax.fori_loop(0, tiles, whole, 0)

    @pl.when(tail)
    def _():
        tile(tiles * cap, short)

    done = pl.ds(pl.multiple_of(tiles * cap + tail.astype(I32) * short, 16), cap)
    ret_b[done, :] = jnp.zeros((cap, d), BF)
    grow_b[done, :] = jnp.zeros((cap, d), BF)
    gg_b[done, :] = jnp.zeros((cap, 128), F32)
    if last:
        late.pop(0).wait()
        half = width // 2
        part = half // 2
        wide = (2 * d + 2 * ff) // streams
        for n_s in range(streams):
            cols = slice(n_s * wide, (n_s + 1) * wide)
            for flip in range(2):
                out = halves[2 * n_s + flip]
                own = eidx[1 + n_s] if flip else 1 - eidx[1 + n_s]
                for b in range(2):
                    start = own * half + b * part if n_s == 0 else b * half + own * part
                    rs = pl.ds(pl.multiple_of(start, 16), part)
                    out[b * part : (b + 1) * part, :] = (
                        acc[rs, cols] + acc_b[rs, cols].astype(F32)
                    ).astype(BF)
        flush(*halves)
    else:
        acc_b[...] = acc[...].astype(BF)
        flush(acc_b)
    if not merge:
        flush(ret_b, grow_b)
    gg_lines = []
    for i, s in enumerate(sources):
        hit = posr[s * local + j : s * local + j + 1, :] == slot_r
        col = gg_b[pl.ds(offs[i], cap), 0:1]
        gg_lines.append(jnp.sum(jnp.where(hit, col, 0.0), axis=0, keepdims=True))
    if not merge:
        for i in range(n):
            gg_o[i : i + 1, :] = gg_lines[i]
    else:
        need(posc, gg_in)
        for load in late:
            load.wait()
        slot_c = lax.broadcasted_iota(I32, (rp, cap), 1).astype(F32)
        expert_row = lax.broadcasted_iota(I32, (experts, rp), 0)
        off0 = jnp.int32(0)
        for i, s in enumerate(sources):
            r0 = pl.ds(pl.multiple_of(off0, 16), cap)
            r1 = pl.ds(offs[i], cap)
            p0 = (posc[:, s * local : s * local + 1] == slot_c).astype(F32).astype(BF)
            p1 = (posc[:, s * local + 1 : s * local + 2] == slot_c).astype(F32).astype(BF)
            pick = jnp.concatenate([p0, p1], axis=1)
            for b0, b1, result in ((grow0, grow_b, grow_o[i]), (ret0, ret_b, mix_o[i])):
                both = jnp.concatenate([b0[r0, :], b1[r1, :]], axis=0)
                result[0:rp, :] = nn(pick, both).astype(BF)
            gg = jnp.where(
                expert_row == eidx[0] * local,
                gg_in[i : i + 1, :],
                jnp.where(expert_row == eidx[0] * local + 1, gg_lines[i], 0.0),
            )
            store_lines(grow_o[i], rp, gg, 2)
            flush(grow_o[i], mix_o[i])
            off0 = off0 + slot_count(posr, s * local)


def expert_call(j, sources, eidx, tables, nrows, crows, ws, cap, acc, first=None):
    posr, posc, meta = tables
    rp, d = crows[0].shape
    local, _, ff = ws[0].shape
    width = ws[1].shape[2]
    n = len(sources)
    experts = local * lax.axis_size("expert")
    merge = first is not None
    cfg = (j, tuple(sources), acc is not None, merge, cap, local, experts)
    buf = (n + 1) * cap
    kinds = "smm" + "m" * (2 * n) + "h" * 6
    args = [eidx, posr, meta]
    args += [nrows[s] for s in sources] + [crows[s] for s in sources] + list(ws)
    if acc is not None:
        args.append(acc)
        kinds += "h"
    if merge:
        args += [posc, *first]
        kinds += "mhhm"
    wide = (width, 2 * d + 2 * ff)
    if acc is not None:
        streams = 2 if merge else 1
        out_shape = (jax.ShapeDtypeStruct((width // 2, wide[1] // streams), BF),) * (2 * streams)
    else:
        out_shape = (jax.ShapeDtypeStruct(wide, BF),)
    if merge:
        out_shape += (jax.ShapeDtypeStruct((rp + 32, d), BF),) * n
        out_shape += (jax.ShapeDtypeStruct((rp, d), BF),) * n
    else:
        out_shape += (jax.ShapeDtypeStruct((buf, d), BF),) * 2
        out_shape += (jax.ShapeDtypeStruct((n, rp), F32),)
    scratch = [
        pltpu.VMEM((d + width, ff), BF),
        pltpu.VMEM((d, width), BF),
        pltpu.VMEM((ff, d + width), BF),
        pltpu.VMEM((width, d), BF),
        pltpu.VMEM((buf, d), BF),
        pltpu.VMEM((buf, d), BF),
        pltpu.VMEM((buf, 128), F32),
        pltpu.VMEM((buf, width), F32),
        pltpu.VMEM((buf, 128), F32),
        pltpu.VMEM((cap, ff), BF),
        pltpu.VMEM((cap, ff), F32),
        pltpu.SemaphoreType.DMA((9,)),
    ]
    scratch.append(pltpu.VMEM(wide, F32))
    if acc is not None:
        scratch.append(pltpu.VMEM(wide, BF))
    if merge:
        scratch += [pltpu.VMEM((buf, d), BF)] * 4
    return staged(
        functools.partial(expert_kernel, cfg),
        args,
        kinds,
        out_shape,
        scratch,
        60, 30, f"expert{j}_{'far' if sources[0] else 'near'}",
    )


def out_bwd_kernel(
    need, flush, banks, pt, p0, p1, p2, lr, rwt, rbt, n2, ra, mid, cot, g2, lo, bo, att, wo, ao,
    gmid, ga, gr_o,
    gml,
):
    rp, d = cot.shape
    experts = pt.shape[0]
    images = banks.shape[0]
    width = ao.shape[1]
    need(pt, p0, p1, p2)
    probs = pt[...]
    lines = sum(p[rp : rp + 32, :].astype(F32) for p in (p0, p1, p2))
    gp = load_lines(lines, rp - d, 2)
    glt = (probs * (gp - jnp.sum(gp * probs, axis=0, keepdims=True))).astype(BF)
    need(lr, rwt, rbt)
    rb = jnp.concatenate([nn(glt, lr[...]), jnp.zeros((experts, d - width), F32)], axis=1)
    rb = jnp.concatenate([rb, jnp.zeros((32 - experts, d), F32)], axis=0)
    gr_o[3 * width : 3 * width + 32, :] = rb.astype(BF)
    mask = bank_mask(banks, 0, rp, images, width)
    gu = (tn(glt, rbt[...].astype(BF)) * mask).astype(BF)
    need(n2, ra)
    gr_o[2 * width : 3 * width, :] = tn(gu, n2[0:rp, :]).astype(BF)
    gmid[...] = tn(glt, rwt[...].astype(BF)) + nt(gu, ra[...])

    need(mid, cot, g2)

    def ln2(i, _):
        rs = pl.ds(pl.multiple_of(i * 160, 160), 160)
        grad = gmid[rs, :] + (p0[rs, :].astype(F32) + p1[rs, :].astype(F32) + p2[rs, :].astype(F32))
        xhat, rstd = norm_parts(mid[rs, :])
        g = cot[rs, :].astype(F32) + norm_back(xhat, rstd, g2[...][None, :], grad)
        gmid[rs, :] = g
        gml[rs, :] = g.astype(BF)
        return 0

    lax.fori_loop(0, rp // 160, ln2, 0)
    flush(gmid)
    need(lo, bo, att, wo, ao)
    g = gml[...]
    gr_o[width : 2 * width, :] = tn(lo[...], g).astype(BF)
    gu = (nt(g, bo[...]) * mask).astype(BF)
    gr_o[0:width, :] = tn(gu, att[...]).astype(BF)
    ga[...] = (nt(g, wo[...]) + nt(gu, ao[...])).astype(BF)


def out_backward(banks, cot, g2, kept, ws, parts):
    rp, d = cot.shape
    width = ws[1].shape[1]
    wo, ao, bo, rwt, ra, rbt = ws
    att, lo, mid, n2, lr, pt = kept
    return staged(
        out_bwd_kernel,
        (banks, pt, *parts, lr, rwt, rbt, n2, ra, mid, cot, g2, lo, bo, att, wo, ao),
        "s" + "m" * 17,
        (
            jax.ShapeDtypeStruct((rp, d), F32),
            jax.ShapeDtypeStruct((rp, d), BF),
            jax.ShapeDtypeStruct((3 * width + 32, d), BF),
        ),
        [pltpu.VMEM((rp, d), BF)],
        36, 12, "out_bwd",
    )


def attn_bwd_kernel(
    need, flush, banks, core, q, k, lse, v, ga, lq, bq, n1, lk, bk, lv, bv, outr,
    gq, gk, gv, uq, uk, uv, send_o, keep_o,
    gr_o,
):
    rp, d = n1.shape
    images = banks.shape[0]
    width = bq.shape[0]
    win = lse.shape[2]
    step_rows = 16 * (SEQ // 16)
    lane = lax.broadcasted_iota(I32, (win, 128), 1)
    first = lane < HEAD_DIM
    row_i = lax.broadcasted_iota(I32, (win, 128), 0)
    key_i = lax.broadcasted_iota(I32, (win, win), 0)
    query_i = lax.broadcasted_iota(I32, (win, win), 1)

    need(q, k, v, ga, lse)

    def image(i, _):
        off = pl.multiple_of(i * step_rows, 64)
        start = i * (SEQ - step_rows)
        bias = jnp.where(
            (key_i >= start) & (key_i < start + SEQ) & (query_i >= start) & (query_i < start + SEQ),
            0.0,
            NEG,
        )
        keep = row_i < start
        ws = pl.ds(off, win)
        for p in range(d // 128):
            cols = slice(p * 128, p * 128 + 128)
            qp = q[ws, cols]
            kp = k[ws, cols]
            vp = v[ws, cols]
            gap = ga[ws, cols]
            rq, rk, rv = [], [], []
            for h in range(2):
                mine = first if h == 0 else jnp.logical_not(first)
                km = jnp.where(mine, kp, jnp.zeros_like(kp))
                vm = jnp.where(mine, vp, jnp.zeros_like(vp))
                prob = jnp.exp2(
                    nt(km, qp) * SCALE2 + bias - lse[i, 2 * p + h : 2 * p + h + 1, :]
                )
                gw = nt(vm, gap)
                delta = jnp.sum(gw * prob, axis=0, keepdims=True)
                gs = (prob * (gw - delta)).astype(BF)
                rv.append(nn(prob.astype(BF), gap))
                rk.append(nn(gs, qp))
                rq.append(tn(gs, kp))
            for parts, ref, scale in ((rq, gq, 0.125), (rk, gk, 0.125), (rv, gv, 1.0)):
                new = (jnp.where(first, parts[0], parts[1]) * scale).astype(BF)
                ref[ws, cols] = jnp.where(keep, ref[ws, cols], new)
        return 0

    lax.fori_loop(0, images, image, 0)
    flush(gq, gk, gv)
    need(n1, lq, lk, lv, bq, bk, bv)
    x = n1[...]
    mask = bank_mask(banks, 0, rp, images, width)
    for i, (grad, low, b, u) in enumerate(((gq, lq, bq, uq), (gk, lk, bk, uk), (gv, lv, bv, uv))):
        g = grad[...]
        gr_o[(2 * i + 1) * width : (2 * i + 2) * width, :] = tn(low[...], g).astype(BF)
        gu = (nt(g, b[...]) * mask).astype(BF)
        u[...] = gu
        gr_o[2 * i * width : (2 * i + 1) * width, :] = tn(gu, x).astype(BF)
    used = 6 * width + outr.shape[0]
    need(outr)
    gr_o[6 * width : used, :] = outr[...]
    if gr_o.shape[0] > used:
        gr_o[used:, :] = jnp.zeros((gr_o.shape[0] - used, d), BF)
    half = send_o.shape[0]
    keep_o[...] = gr_o[pl.ds(pl.multiple_of(core[0] * half, 16), half), :]
    send_o[...] = gr_o[pl.ds(pl.multiple_of((1 - core[0]) * half, 16), half), :]
    flush(send_o, keep_o)


def attn_backward(banks, core, kept, ga, bs, outr, shares):
    rp, d = ga.shape
    width = bs[0].shape[0]
    bfd = jax.ShapeDtypeStruct((rp, d), BF)
    low = jax.ShapeDtypeStruct((rp, width), BF)
    n1, q, k, v, lq, lk, lv, lse = kept
    bq, bk, bv = bs
    total = -(-(6 * width + outr.shape[0]) // (32 * shares)) * 32 * shares
    half = jax.ShapeDtypeStruct((total // 2, d), BF)
    return staged(
        attn_bwd_kernel,
        (banks, core, q, k, lse, v, ga, lq, bq, n1, lk, bk, lv, bv, outr),
        "ss" + "m" * 13,
        (bfd, bfd, bfd, low, low, low, half, half),
        [pltpu.VMEM((total, d), BF)],
        34, 20, "attn_bwd",
    )


def input_bwd_kernel(
    need, flush, gq, wq, uq, aq, gk, wk, uk, ak, gv, wv, uv, av, gmid, tok, g1, inp_o, total
):
    rows, d = inp_o.shape
    need(gq, wq, uq, aq)
    first = nt(gq[...], wq[...]) + nt(uq[...], aq[...])
    need(gk, wk, uk, ak)
    first = first + (nt(gk[...], wk[...]) + nt(uk[...], ak[...]))
    need(gv, wv, uv, av)
    total[...] = first + (nt(gv[...], wv[...]) + nt(uv[...], av[...]))
    need(gmid, tok, g1)
    whole = rows // 16 * 16
    for r, count in [(s, min(112, whole - s)) for s in range(0, whole, 112)] + (
        [(whole, rows - whole)] if rows > whole else []
    ):
        rs = slice(r, r + count)
        xhat, rstd = norm_parts(tok[rs, :].astype(F32))
        inp_o[rs, :] = gmid[rs, :] + norm_back(xhat, rstd, g1[...][None, :], total[rs, :])


def input_backward(tok, rows, g1, gmid, grads, ws):
    d = tok.shape[1]
    gq, gk, gv, uq, uk, uv = grads
    wq, wk, wv, aq, ak, av = ws
    return staged(
        input_bwd_kernel,
        (gq, wq, uq, aq, gk, wk, uk, ak, gv, wv, uv, av, gmid, tok, g1),
        "m" * 15,
        (jax.ShapeDtypeStruct((rows, d), F32),),
        [pltpu.VMEM(gmid.shape, F32)],
        34, 7, "input_bwd",
    )[0]


def join(bit, own, other, out, low, high):
    half = own.shape[0]
    out[0:half, low:high] = jnp.where(bit == 0, own[:, low:high], other[:, low:high])
    out[half : 2 * half, low:high] = jnp.where(bit == 0, other[:, low:high], own[:, low:high])


def finish_kernel(need, flush, bit, own, other, *rest):
    outs, flat = rest[:-1], rest[-1]
    width, d = outs[1].shape
    experts = outs[9].shape[0]
    need(own, other)
    join(bit[0], own, other, flat, 0, d)
    for i in range(5):
        base = 2 * i * width
        outs[2 * i][...] = jnp.transpose(flat[base : base + width, :].astype(F32))
        flush(outs[2 * i])
        if i < 4:
            outs[2 * i + 1][...] = flat[base + width : base + 2 * width, :].astype(F32)
            flush(outs[2 * i + 1])
    outs[9][...] = flat[9 * width : 9 * width + 16, 0:width].astype(F32)[0:experts]


def finish(bit, own, other, width, experts):
    d = own.shape[1]
    tall = jax.ShapeDtypeStruct((d, width), F32)
    wide = jax.ShapeDtypeStruct((width, d), F32)
    return staged(
        finish_kernel,
        (bit, own, other),
        "smm" if own.shape[0] % 16 == 0 else "svv",
        (tall, wide) * 4 + (tall, jax.ShapeDtypeStruct((experts, width), F32)),
        [pltpu.VMEM((2 * own.shape[0], d), BF)],
        16, 2, "finish",
    )


def finish_expert_kernel(cfg, need, flush, bit, own, other, *rest):
    j, aliased = cfg
    ua_o, ub_o, da_o, db_o, ua, ub, da, db, both, sems = rest[4:] if aliased else rest
    d, width = ua.shape
    ff = ub.shape[1]
    need(own, other)
    copies = []

    def put(n, src, out):
        copies.append(pltpu.make_async_copy(src, out.at[j], sems.at[n]))
        copies[-1].start()

    join(bit[0], own, other, both, d + ff, d + 2 * ff)
    da[...] = jnp.transpose(both[:, d + ff : d + 2 * ff].astype(F32))
    put(0, da, da_o)
    join(bit[0], own, other, both, d, d + ff)
    ub[...] = both[:, d : d + ff].astype(F32)
    put(1, ub, ub_o)
    join(bit[0], own, other, both, 0, d)
    ua[...] = jnp.transpose(both[:, 0:d].astype(F32))
    put(2, ua, ua_o)
    join(bit[0], own, other, both, d + 2 * ff, 2 * d + 2 * ff)
    db[...] = both[:, d + 2 * ff :].astype(F32)
    put(3, db, db_o)
    for copy in copies:
        copy.wait()


def finish_expert(j, n, bit, own, other, d, earlier=()):
    half, wide = own.shape
    width = 2 * half
    ff = wide // 2 - d
    shapes = ((d, width), (width, ff), (ff, width), (width, d))
    args = (bit, own, other, *earlier)
    return staged(
        functools.partial(finish_expert_kernel, (j, bool(earlier))),
        args,
        "smm" + "h" * len(earlier),
        tuple(jax.ShapeDtypeStruct((n,) + x, F32) for x in shapes),
        [pltpu.VMEM(x, F32) for x in shapes]
        + [pltpu.VMEM((width, wide), BF), pltpu.SemaphoreType.DMA((4,))],
        24, 3, f"finish_expert{j}",
        direct=True,
        aliases={3 + i: i for i in range(len(earlier))},
    )


def hop(x, axis, k):
    n = lax.axis_size(axis)
    return lax.ppermute(x, axis, [(i, i ^ k) for i in range(n)])


def bits(axis):
    n = lax.axis_size(axis)
    return [1 << i for i in range(n.bit_length() - 1)]


def add(a, b):
    return (a.astype(F32) + b.astype(F32)).astype(BF)


def part_of(terms, bit, flip):
    half = terms[0].shape[0] // 2
    start = (bit if not flip else 1 - bit) * half
    return sum(lax.dynamic_slice_in_dim(t, start, half, 0).astype(F32) for t in terms).astype(BF)


def reduce_step(terms, axis, k):
    bit = (lax.axis_index(axis) // k) % 2
    send = part_of(terms, bit, True)
    return send, part_of(terms, bit, False), hop(send, axis, k)


def gather_step(buf, axis, k, wait=None):
    bit = (lax.axis_index(axis) // k) % 2
    other = hop(buf, axis, k)
    if wait is not None:
        other = after(other, *(wait if isinstance(wait, tuple) else (wait,)))
    return jnp.where(
        bit == 0,
        jnp.concatenate([buf, other], axis=0),
        jnp.concatenate([other, buf], axis=0),
    )


def after(x, *deps):
    return lax.optimization_barrier((x,) + deps)[0]


def gather4(x):
    near = hop(x, "expert", 1)
    far = hop(x, "expert", 2)
    return [x, near, far, hop(far, "expert", 1)]


def body(
    tokens, cotangent, bank_ids, routes, attn_gain, expert_gain, query_w, key_w, value_w, out_w,
    query_a, query_b, key_a, key_b, value_a, value_b, out_a, out_b, router_w, router_a, router_b,
    up_w, up_a, up_b, down_w, down_a, down_b,
):
    rows, d = tokens.shape
    rp = 32 * (-(-rows // 32))
    width = query_a.shape[1]
    local = up_w.shape[0]
    groups = lax.axis_size("expert")
    experts = local * groups
    cap = 13 * rows // (4 * experts)
    place = lax.axis_index("dp")
    me = jnp.stack([lax.axis_index("expert"), place % 2, place // 2 % 2]).astype(I32)
    cot = jnp.pad(cotangent, ((0, rp - rows), (0, 0)))
    cot1 = hop(cot, "expert", 1)
    cot2 = hop(cot, "expert", 2)
    meta = jnp.concatenate([routes.T, jnp.repeat(bank_ids, SEQ)[None, :]], axis=0)
    meta = jnp.pad(meta, ((0, 0), (0, rp - rows)), constant_values=-1)
    meta = jnp.stack(gather4(meta))
    g1 = attn_gain
    g2 = expert_gain
    kept = attn_forward(
        bank_ids, tokens, g1,
        (query_w, query_a, query_b, key_w, key_a, key_b, value_w, value_a, value_b),
    )
    n1, q, k, v, lq, lk, lv, att, lse, tokp = kept
    out_ws = (out_w, out_a, out_b, router_w.T.astype(F32), router_a, router_b.T.astype(F32))
    lo, mid, n2, lr, pt = out_forward(
        bank_ids, tokp, g2, after(att, meta), out_ws, (cot1,)
    )
    near1 = hop(n2, "expert", 1)
    far2 = hop(after(n2, cot2), "expert", 2)
    cot3 = hop(after(cot2, n2), "expert", 1)
    tables = routing_tables(me, after(meta, n2), local) + (meta,)
    crows = [cot, cot1, cot2, cot3]
    ews = (up_w, up_a, up_b, down_w, down_a, down_b)
    common = (crows, ews, cap)
    nrows = [n2, near1, None, None]
    e0n = expert_call(0, (0, 1), after(me, cot3), tables, nrows, *common, None)
    far2 = after(far2, e0n[1])
    nrows = [n2, near1, far2, hop(far2, "expert", 1)]
    e0f = expert_call(0, (2, 3), me, tables, nrows, *common, e0n[0])
    dp_steps = [("dp", k) for k in bits("dp")]
    ex_steps = [("expert", k) for k in bits("expert")]
    got0 = hop(e0f[0], *dp_steps[0])
    keep0 = e0f[1]
    e1f = expert_call(
        1, (2, 3), after(me, keep0), tables, nrows, *common, None, e0f[2:]
    )
    grow = add(e1f[1], hop(e1f[2], "expert", 1))
    send0, keep0, got0 = reduce_step([keep0, after(got0, e1f[1])], *dp_steps[1])
    e1n = expert_call(
        1, (0, 1), after(me, grow, send0), tables, nrows, *common, e1f[0], e0n[1:]
    )
    send1, keep1, send2, keep2, *near = e1n
    grow_far = hop(grow, "expert", 2)
    grow_near = hop(after(near[1], grow_far), "expert", 1)
    mix_far = hop(after(e1f[3], near[0]), "expert", 2)
    mix_cross = hop(after(e1f[4], near[0]), "expert", 3)
    send0, keep0, got0 = reduce_step([keep0, after(got0, near[0])], *dp_steps[2])
    got1 = hop(after(send1, near[0]), *dp_steps[0])
    got2 = hop(after(send2, near[0]), *dp_steps[1])
    gmid, ga, outr = out_backward(
        bank_ids, cot, g2, (att, lo, mid, n2, lr, pt), out_ws,
        (near[0], after(grow_near, send0), grow_far),
    )
    got0 = after(got0, gmid)
    for step in dp_steps[3:]:
        _, keep0, got0 = reduce_step([keep0, got0], *step)
    buf0 = add(keep0, got0)
    send1, keep1, got1 = reduce_step([keep1, after(got1, gmid)], *dp_steps[1])
    send2, keep2, got2 = reduce_step([keep2, after(got2, gmid)], *dp_steps[0])
    core = lax.axis_index("expert").astype(I32).reshape(1) % 2
    shares = lax.axis_size("dp") * groups // 32
    *grads, qkv, keep = attn_backward(
        bank_ids, core, (n1, q, k, v, lq, lk, lv, lse), after(ga, buf0, send1, send2),
        (query_b, key_b, value_b), outr, shares,
    )
    up_steps = dp_steps[::-1]
    bit = me[1:2]
    buf0 = gather_step(buf0, *up_steps[0], wait=qkv)
    qkv = after(qkv, mix_far, mix_cross)
    mix_near = hop(after(near[3], qkv), "expert", 1)
    keep1 = jnp.concatenate([keep1, keep2], axis=1)
    got1 = jnp.concatenate([after(got1, qkv), after(got2, qkv)], axis=1)
    send1, keep1, got1 = reduce_step([keep1, got1], *dp_steps[2])
    got = hop(after(qkv, buf0, send1), *ex_steps[0])
    send, keep, got = reduce_step([keep, got], *ex_steps[1])
    input_grad = input_backward(
        tokp, rows, g1, after(gmid, send), grads,
        (query_w, key_w, value_w, query_a, key_a, value_a),
    )
    got = after(got, input_grad)
    for step in dp_steps[3:]:
        _, keep1, got1 = reduce_step([keep1, got1], *step)
    buf1 = add(keep1, after(got1, input_grad))
    for step in up_steps[1:-1]:
        buf0 = gather_step(buf0, *step, wait=input_grad)
    for step in ex_steps[2:]:
        _, keep, got = reduce_step([keep, got], *step)
    send, keep, got = reduce_step([keep, after(got, buf0, buf1)], *dp_steps[0])
    peer0 = hop(after(buf0, send), *up_steps[-1])
    buf1 = gather_step(buf1, *up_steps[0])
    for step in dp_steps[1:-1]:
        _, keep, got = reduce_step([keep, got], *step)
    _, keep, got = reduce_step([keep, after(got, buf1)], *dp_steps[-1])
    for step in up_steps[1:-1]:
        buf1 = gather_step(buf1, *step)
    flat = after(add(keep, got), peer0)
    flat = gather_step(flat, *up_steps[0])
    for step in up_steps[1:-1]:
        flat = gather_step(after(flat, buf1), *step)
    peer1 = hop(buf1, *up_steps[-1])
    flat = gather_step(flat, *up_steps[-1])
    for step in reversed(ex_steps[2:]):
        flat = gather_step(flat, *step)
    mixed = mid[:rows] + (
        (near[2][:rows].astype(F32) + mix_near[:rows].astype(F32))
        + (mix_far[:rows].astype(F32) + mix_cross[:rows].astype(F32))
    )
    mixed = mixed.astype(BF)
    large = finish_expert(0, local, bit, buf0, peer0, d)
    flat = gather_step(flat, *ex_steps[1], wait=(mixed, large[0]))
    peer = hop(after(flat, peer1), *ex_steps[0])
    large = finish_expert(1, local, bit, buf1, peer1, d, large)
    small = finish(
        core, flat, after(peer, large[0]), width, experts,
    )
    return (mixed, input_grad, *small[:9], small[9].T, *large)


def solution(mesh):
    split = P(("dp", "expert"), None)
    by_expert = P("expert", None, None)
    in_specs = (split, split, P(("dp", "expert")), split) + (P(),) * 17 + (by_expert,) * 6
    out_specs = (split, split) + (P(),) * 10 + (by_expert,) * 4
    return jax.shard_map(body, mesh=mesh, in_specs=in_specs, out_specs=out_specs, check_vma=False)
```
